32 devices in a mesh: dp: 8 (over y, x, core), blk: 4 (over z).
Axes of the slice: x: 2, y: 2, z: 4, core: 2. Of those that a mesh axis runs over, the one named last changes fastest.
Arguments:
- tokens: bfloat16 [16, 1024, 768], P('dp', 'blk'), may hold values from -6 to 6
- segment_ids: int32 [16, 1024], P('dp', 'blk'), may hold values from 0 to 32, as said below
- norm_attn: bfloat16 [768], replicated, may hold values from 0.099609375 to 1.8984375
- w_query: bfloat16 [768, 768], replicated, may hold values from -0.078125 to 0.078125
- w_key: bfloat16 [768, 768], replicated, may hold values from -0.078125 to 0.078125
- w_value: bfloat16 [768, 768], replicated, may hold values from -0.21875 to 0.21875
- w_out: bfloat16 [768, 768], replicated, may hold values from -0.875 to 0.875
- norm_ff: bfloat16 [768], replicated, may hold values from 0.099609375 to 1.8984375
- w_gate: bfloat16 [768, 2048], replicated, may hold values from -0.21875 to 0.21875
- w_up: bfloat16 [768, 2048], replicated, may hold values from -0.21875 to 0.21875
- w_down: bfloat16 [2048, 768], replicated, may hold values from -0.1875 to 0.1875
- bias_table: float32 [32, 12], replicated, may hold values from -5 to 5
- cotangent: bfloat16 [16, 1024, 768], P('dp', 'blk'), may hold values from -6 to 6
Outputs:
- output: bfloat16 [16, 1024, 768], P('dp', 'blk')
- input_grad: float32 [16, 1024, 768], P('dp', 'blk')
- grad_norm_attn: float32 [768], replicated
- grad_query: float32 [768, 768], P('dp', 'blk')
- grad_key: float32 [768, 768], P('dp', 'blk')
- grad_value: float32 [768, 768], P('dp', 'blk')
- grad_out: float32 [768, 768], P('dp', 'blk')
- grad_norm_ff: float32 [768], replicated
- grad_gate: float32 [768, 2048], P('dp', 'blk')
- grad_up: float32 [768, 2048], P('dp', 'blk')
- grad_down: float32 [2048, 768], P('dp', 'blk')
- grad_bias_table: float32 [32, 12], replicated
The draws below stay inside these ranges and needn't reach their ends.
Inputs may be any that keep to these rules, and one draw needn't show every extreme that they name: `segment_ids`: each row is packed with documents in order, each of 32 to 512 slots except a last one that the row's end cuts, then 0 to 24 padding slots of segment 0. The documents before the last are numbered 1, 2, 3 and so on; the last document of every row is numbered 1 + 1023 // 32. In each group of 2 rows that one index of dp holds, one row drawn from the seed holds instead document 1 of 1 to 128 slots, document 2 up to 1 to 128 slots before the row's end, and the last document after it.
All inputs are finite; a program needn't handle non-finite values.
Results may differ from the reference program's by a relative error of at most 0.02.
Values may be sent and summed in bfloat16 or wider, within the bound.
A program may use at most 192 MiB of HBM per device.

```python
import jax
import jax.numpy as jnp
from jax import lax

D = 768
H = 12
HD = 64
FF = 2048
BUCKETS = 32
SEQ = 1024
DOC_MIN = 32
DOC_MAX = 512
PAD_MAX = 24
ROWS_DP = 2
S_BLK = 256
ROWS = 16


def draw_segment_ids(key, part):
    key = jax.random.fold_in(key, 11)
    key_docs, key_pad, key_pick, key_lead, key_trail = jax.random.split(key, 5)
    top_id = 1 + (SEQ - 1) // DOC_MIN
    count_docs = SEQ // DOC_MIN + 1
    lengths = jax.random.randint(key_docs, (ROWS, count_docs), DOC_MIN, DOC_MAX + 1)
    boundary = jnp.cumsum(lengths, axis=1)
    slot_index = jnp.arange(SEQ, dtype=jnp.int32)
    packed = 1 + jnp.sum((slot_index[None, :, None] >= boundary[:, None, :]).astype(jnp.int32), axis=2)
    padding = jax.random.randint(key_pad, (ROWS, 1), 0, PAD_MAX + 1)
    packed = jnp.where(slot_index[None, :] >= SEQ - padding, 0, packed)
    last_doc = jnp.max(packed, axis=1, keepdims=True)
    packed = jnp.where((packed == last_doc) & (packed > 0), top_id, packed)
    leading = jax.random.randint(key_lead, (ROWS, 1), 1, S_BLK // 2 + 1)
    trailing = jax.random.randint(key_trail, (ROWS, 1), 1, S_BLK // 2 + 1)
    spanning = 1 + (slot_index[None, :] >= leading).astype(jnp.int32) + (slot_index[None, :] >= SEQ - trailing).astype(jnp.int32)
    spanning = jnp.where(spanning == 3, top_id, spanning)
    chosen = jax.random.randint(key_pick, (ROWS // ROWS_DP, 1), 0, ROWS_DP)
    row_index = jnp.arange(ROWS, dtype=jnp.int32).reshape(ROWS // ROWS_DP, ROWS_DP)
    picked = (row_index % ROWS_DP == chosen).reshape(ROWS, 1)
    return jnp.where(picked, spanning, packed).astype(jnp.int32)


def with_spikes(drawn, key, source, target, shards_of, factor):
    owner, partner = [(jnp.arange(drawn.shape[axis_at]) // (drawn.shape[axis_at] // shards_of)).reshape([-1 if axis == axis_at else 1 for axis in range(drawn.ndim)]) for axis_at in (source, target)]
    chosen = jax.random.permutation(key, shards_of)[partner]
    strong = (owner == chosen) | (owner == (partner + shards_of // 2) % shards_of)
    return jnp.where(strong, factor * drawn, drawn)


def level_of(key, extent, shards, low, largest):
    level = 1.0
    for axis_at, blocks in shards:
        steps = jax.random.uniform(jax.random.fold_in(jax.random.fold_in(key, 6), axis_at), (blocks,), jnp.float32, low / len(shards), largest / len(shards))
        level = level * jnp.repeat(jnp.exp(steps), extent[axis_at] // blocks).reshape((-1,) + (1,) * (len(extent) - 1 - axis_at))
    return level


def bell_draw(rng, extent, scale, reach, cuts=(), kind=jnp.bfloat16):
    factor_of = level_of(rng, extent, cuts, -0.22, 0.18) if cuts else 1.0
    result = jax.random.normal(rng, extent, jnp.float32) * scale * factor_of
    return jnp.minimum(jnp.maximum(result, -reach), reach).astype(kind)


def bell_draw_with(rng, extent, width, bound, cuts, heavy, kind=jnp.bfloat16):
    result = width * jax.random.normal(rng, extent, jnp.float32)
    if cuts:
        result = result * level_of(rng, extent, cuts, -0.22, 0.18)
    return jnp.clip(with_spikes(result, jax.random.fold_in(rng, 3), *heavy), -bound, bound).astype(kind)


def setup_inputs(seed: int = 0) -> dict:
    key_of = jax.random.split(jax.random.key(seed), 14)
    return {
        "tokens": bell_draw_with(key_of[0], (ROWS, SEQ, D), 1.0, 6.0, ((0, 8), (1, 4)), (0, 2, 8, 2.0)),
        "segment_ids": draw_segment_ids(jax.random.fold_in(key_of[13], 71), 0),
        "norm_attn": jnp.clip(1.0 + 0.18 * jax.random.normal(key_of[2], (D,), jnp.float32), 0.099609375, 1.8984375).astype(jnp.bfloat16),
        "w_query": bell_draw(key_of[3], (D, D), (8 * D) ** -0.5, 0.078125),
        "w_key": bell_draw(key_of[4], (D, D), (8 * D) ** -0.5, 0.078125),
        "w_value": bell_draw(key_of[5], (D, D), D ** -0.5, 0.21875),
        "w_out": bell_draw(key_of[6], (D, D), (D // 16) ** -0.5, 0.875),
        "norm_ff": jnp.clip(1.0 + 0.18 * jax.random.normal(key_of[7], (D,), jnp.float32), 0.099609375, 1.8984375).astype(jnp.bfloat16),
        "w_gate": bell_draw(key_of[8], (D, FF), D ** -0.5, 0.21875),
        "w_up": bell_draw(key_of[9], (D, FF), D ** -0.5, 0.21875),
        "w_down": bell_draw(key_of[10], (FF, D), (FF // 2) ** -0.5, 0.1875),
        "bias_table": bell_draw(key_of[11], (BUCKETS, H), 1.0, 5.0, (), jnp.float32),
        "cotangent": bell_draw(key_of[12], (ROWS, SEQ, D), 1.0, 6.0, ((0, 8), (1, 4))),
    }


EPSILON = 1e-06
MASKED = -1e+30
LIMITS = (12, 16, 23, 32, 46, 64, 91)
PRECISE = lax.Precision.HIGHEST

@jax.custom_vjp
def low(v):
    return lax.optimization_barrier(v.astype(jnp.bfloat16)).astype(jnp.float32)

@jax.custom_vjp
def low_back(v):
    return v

def low_keep(v):
    return (low(v), None)

def low_pass(kept, grad):
    return (grad,)

def back_keep(v):
    return (v, None)

def back_low(kept, grad):
    return (low(grad),)
low.defvjp(low_keep, low_pass)
low_back.defvjp(back_keep, back_low)

def bucket_of(distance):
    magnitude = jnp.abs(distance)
    beyond = jnp.full(distance.shape, 8, jnp.int32)
    for threshold in LIMITS:
        beyond = beyond + (magnitude >= threshold).astype(jnp.int32)
    inside = jnp.where(magnitude < 8, magnitude, beyond)
    return inside + 16 * (distance > 0).astype(jnp.int32)

def normalize(vector, scale_gain):
    return vector * lax.rsqrt(lax.optimization_barrier(jnp.mean(vector * vector, axis=-1, keepdims=True)) + EPSILON) * scale_gain

def project(operand, weight):
    return jnp.einsum('rsk,kn->rsn', operand, weight, precision=PRECISE)

def gated_unit(gate_proj, up_proj):
    return jax.nn.gelu(gate_proj, approximate=True) * up_proj

def attend_row(inputs, bias_full):
    query_row, key_row, value_row, segment_row = inputs
    query_heads = query_row.reshape(SEQ, H, HD)
    key_heads = key_row.reshape(SEQ, H, HD)
    value_heads = value_row.reshape(SEQ, H, HD)
    scores = low_back(jnp.einsum('qhd,khd->hqk', query_heads, key_heads, precision=PRECISE) + bias_full)
    same_doc = (segment_row[:, None] == segment_row[None, :])[None]
    scores = jnp.where(same_doc, scores, MASKED)
    weights = low(jax.nn.softmax(scores, axis=-1))
    mixed = jnp.einsum('hqk,khd->qhd', weights, value_heads, precision=PRECISE)
    return mixed.reshape(SEQ, H * HD)

def encoder_layer(tokens, norm_attn, w_query, w_key, w_value, w_out, norm_ff, w_gate, w_up, w_down, bias_table, segment_ids):
    normed = low(normalize(tokens, norm_attn))
    query_proj = low(low_back(project(normed, w_query)))
    key_proj = low(low_back(project(normed, w_key)))
    value_proj = low(low_back(project(normed, w_value)))
    slot_index = jnp.arange(SEQ, dtype=jnp.int32)
    distance = slot_index[None, :] - slot_index[:, None]
    bias_full = jnp.transpose(bias_table[bucket_of(distance)], (2, 0, 1))

    def one_row(inputs):
        return attend_row(inputs, bias_full)
    mixed = lax.map(jax.checkpoint(one_row), (query_proj, key_proj, value_proj, segment_ids))
    mixed = low(low_back(mixed))
    branch = low_back(project(mixed, w_out))
    middle = tokens + branch
    normed_ff = low(normalize(middle, norm_ff))
    gate_proj = low_back(project(normed_ff, w_gate))
    up_proj = low_back(project(normed_ff, w_up))
    hidden = low(gated_unit(gate_proj, up_proj))
    return middle + low_back(project(hidden, w_down))

def reference(tokens, segment_ids, norm_attn, w_query, w_key, w_value, w_out, norm_ff, w_gate, w_up, w_down, bias_table, cotangent):
    floats = [operand.astype(jnp.float32) for operand in (tokens, norm_attn, w_query, w_key, w_value, w_out, norm_ff, w_gate, w_up, w_down, bias_table)]

    def forward(*values):
        return encoder_layer(*values, segment_ids)
    output, pullback = jax.vjp(forward, *floats)
    grads = pullback(cotangent.astype(jnp.float32))
    return (output.astype(jnp.bfloat16), grads[0], grads[1], grads[2], grads[3], grads[4], grads[5], grads[6], grads[7], grads[8], grads[9], grads[10])
```

```python
import functools

import jax
import jax.numpy as jnp
from jax import lax
from jax.experimental import pallas as pl
from jax.experimental.pallas import tpu as pltpu
from jax.sharding import PartitionSpec as P

H = 12
HD = 64
EPSILON = 1e-06
MASKED = -1e30
LIMITS = (12, 16, 23, 32, 46, 64, 91)
FAR_BEFORE = 15
FAR_AFTER = 31

MESH = pl.DeviceIdType.MESH
BF = jnp.bfloat16
F32 = jnp.float32
ANY = pl.BlockSpec(memory_space=pl.ANY)
VM = pl.BlockSpec(memory_space=pltpu.VMEM)
SM = pl.BlockSpec(memory_space=pltpu.SMEM)

D = 768
HALF = 384
ZB = 192
SLOTS = 1024
STRIPE = 128
OWN = 512


def dot(a, b):
    return lax.dot_general(a, b, (((1,), (0,)), ((), ())), preferred_element_type=F32)


def dot_nt(a, b):
    return lax.dot_general(a, b, (((1,), (1,)), ((), ())), preferred_element_type=F32)


def dot_tn(a, b):
    return lax.dot_general(a, b, (((0,), (0,)), ((), ())), preferred_element_type=F32)


class Place:
    def __init__(self, low):
        self.low = low
        self.dp = lax.axis_index("dp")
        self.z = lax.axis_index("blk")
        high = self.dp // low
        self.c = high % 2
        self.x = (high // 2) % 2
        self.y = high // 4
        self.base = self.dp - self.c * low
        self.z0 = self.z % 2
        self.z1 = self.z // 2
        self.core = (self.dp + low * (1 - 2 * self.c), self.z)
        self.xp = (self.dp + 2 * low * (1 - 2 * self.x), self.z)
        self.yp = (self.dp + 4 * low * (1 - 2 * self.y), self.z)
        self.z0p = (self.dp, self.z + 1 - 2 * self.z0)
        self.z1p = (self.dp, self.z + 2 - 4 * self.z1)

    def group(self):
        found = []
        for dc in range(2):
            for dz in range(4):
                if dc or dz:
                    found.append((self.base + ((self.c + dc) % 2) * self.low, (self.z + dz) % 4))
        return found

    def near(self, k):
        fold = jnp.where(self.z < 2, self.z, 3 - self.z)
        step = (k + fold * (1 - 2 * k)) if k < 2 else k
        return jnp.where(self.z < 2, step, 3 - step)


def greet(others):
    barrier = pltpu.get_barrier_semaphore()
    for other in others:
        pl.semaphore_signal(barrier, inc=1, device_id=other, device_id_type=MESH)
    pl.semaphore_wait(barrier, len(others))


def remote(src, dst, send, recv, device):
    return pltpu.make_async_remote_copy(
        src_ref=src, dst_ref=dst, send_sem=send, recv_sem=recv, device_id=device, device_id_type=MESH
    )


def bucket_tile():
    key = lax.broadcasted_iota(jnp.int32, (128, 384), 0)
    query = lax.broadcasted_iota(jnp.int32, (128, 384), 1)
    rel = key - query + 128
    dist = jnp.abs(rel)
    beyond = jnp.full((128, 384), 8, jnp.int32)
    for threshold in LIMITS:
        beyond = beyond + (dist >= threshold).astype(jnp.int32)
    return jnp.where(dist < 8, dist, beyond) + jnp.where(rel > 0, 16, 0)


def head_of(place, local):
    return 3 * place.c + local % 3 + 6 * (local // 3)


def lane_mask(head_in_pair):
    lane = lax.broadcasted_iota(jnp.int32, (1, 128), 1)
    inside = (lane < HD) if head_in_pair == 0 else (lane >= HD)
    return inside.astype(F32).astype(BF)


def forward_kernel(
    low,
    tok, cot, seg, wq, wk, wv, gain, table,
    x_o, cot_o, n1_o, q_o, k_o, v_o, e_o, linv_o, o_o, ob_o, wown_o,
    xrow, segb, wfull, wown, n1, q, k, v, band, bkt, segcol, segrow, s_scr, e_scr, ot_scr, lt_scr, o, ob, linv,
    x_send, x_recv, f_send, f_recv, c_send, c_recv, g_send, g_recv, o_send, o_recv, l_sem, e_sem,
):
    me = Place(low)
    c, z = me.c, me.z

    loads = [pltpu.make_async_copy(w, wfull.at[i], l_sem.at[i]) for i, w in enumerate((wq, wk, wv))]
    for load in loads:
        load.start()
    greet(me.group())

    def targets():
        for r in range(2):
            for kk in range(2):
                yield r, kk, (me.base + kk * low, 2 * c + r), jnp.logical_and(2 * c + r == z, kk == c)

    for r, kk, device, here in targets():
        src = tok.at[r, pl.ds(STRIPE * kk, STRIPE)]
        dst = xrow.at[z, kk]
        far = remote(src, dst, x_send.at[r, kk], x_recv.at[z], device)
        near = pltpu.make_async_copy(src, dst, x_recv.at[z])
        sfar = remote(seg, segb.at[z], g_send.at[r, kk], g_recv.at[z], device)
        snear = pltpu.make_async_copy(seg, segb.at[z], g_recv.at[z])

        @pl.when(here)
        def _():
            near.start()
            snear.start()

        @pl.when(jnp.logical_not(here))
        def _():
            far.start()
            sfar.start()

    for i in range(3):
        loads[i].wait()
        lo = jnp.concatenate([wfull[i, :, 0:ZB], wfull[i, :, 2 * ZB : 3 * ZB]], axis=1)
        hi = jnp.concatenate([wfull[i, :, ZB : 2 * ZB], wfull[i, :, 3 * ZB : 4 * ZB]], axis=1)
        wown[:, HALF * i : HALF * (i + 1)] = jnp.where(c == 0, lo, hi)
    bkt[...] = bucket_tile()

    def make_band(hl, _):
        head = head_of(me, hl)
        for t in range(3):
            which = bkt[:, 128 * t : 128 * (t + 1)]
            total = jnp.zeros((128, 128), F32)
            for b in range(32):
                total = jnp.where(which == b, table[b, head], total)
            band[hl, :, 128 * t : 128 * (t + 1)] = total
        return 0

    lax.fori_loop(0, 6, make_band, 0)

    gain_f = gain[...].astype(F32)
    forwards = []
    for step in range(4):
        zz = me.near(step)
        own = xrow.at[zz, c]
        remote(own, own, x_send.at[0, 0], x_recv.at[zz], me.core).wait_recv()
        fwd = remote(own, own, f_send.at[step], f_recv.at[zz], me.core)
        fwd.start()
        forwards.append(fwd)
    for step in range(4):
        zz = me.near(step)
        other = xrow.at[zz, 1 - c]
        remote(other, other, f_send.at[step], f_recv.at[zz], me.core).wait_recv()
        xf = xrow[zz].reshape(256, D).astype(F32)
        r1 = lax.rsqrt(jnp.mean(xf * xf, axis=-1, keepdims=True) + EPSILON)
        nb = (xf * r1 * gain_f).astype(BF)
        rows = pl.ds(pl.multiple_of(zz * 256, 256), 256)
        n1[rows, :] = nb
        for i, dest in enumerate((q, k, v)):
            dest[rows, :] = dot(nb, wown[:, HALF * i : HALF * (i + 1)]).astype(BF)

    for r, kk, device, here in targets():
        src = cot.at[r, pl.ds(STRIPE * kk, STRIPE)]
        dst = cot_o.at[z]
        far = remote(src, dst, c_send.at[r, kk], c_recv.at[z], device)
        near = pltpu.make_async_copy(src, dst, c_recv.at[z])

        @pl.when(here)
        def _():
            near.start()

        @pl.when(jnp.logical_not(here))
        def _():
            far.start()

    saves = [
        pltpu.make_async_copy(src, dst, l_sem.at[i])
        for i, (src, dst) in enumerate(
            (
                (xrow.at[:, c], x_o),
                (n1, n1_o),
                (q, q_o),
                (k, k_o),
                (v, v_o),
                (wown, wown_o),
            )
        )
    ]
    for save in saves:
        save.start()

    for zz in range(4):
        blk_seg = segb.at[zz]
        remote(blk_seg, blk_seg, g_send.at[0, 0], g_recv.at[zz], me.core).wait_recv()
        segrow[:, 256 * zz : 256 * (zz + 1)] = segb[zz, pl.ds(z % 2, 1), :].astype(F32)
    segcol[...] = jnp.transpose(jnp.broadcast_to(segrow[...], (128, SLOTS)))
    linv[...] = jnp.zeros((8, SLOTS), F32)

    def pair_step(p, _):
        lanes = pl.ds(pl.multiple_of(p * 128, 128), 128)
        kp, vp = k[:, lanes], v[:, lanes]
        for hd in range(2):
            mask = lane_mask(hd)
            vm = vp * mask + (1 - mask)
            hl = 2 * p + hd
            head = head_of(me, hl)
            after, before = table[FAR_AFTER, head], table[FAR_BEFORE, head]

            @pl.when(p > 0)
            def _():
                pltpu.make_async_copy(e_scr.at[hd], e_o.at[hl], e_sem.at[hd]).wait()

            for ib in range(4):
                qm = q[256 * ib : 256 * (ib + 1), lanes] * mask
                scr = s_scr.at[ib % 2]
                scr[...] = dot_nt(kp, qm)
                for t in range(2):
                    here = 2 * ib + t
                    cols = slice(128 * t, 128 * (t + 1))
                    seg_q = segrow[:, 256 * ib + 128 * t : 256 * ib + 128 * (t + 1)]
                    top = jnp.full((8, 128), MASKED, F32)
                    for jb in range(8):
                        rows = slice(128 * jb, 128 * (jb + 1))
                        tile = scr[rows, cols]
                        if abs(jb - here) <= 1:
                            off = 128 * (here - jb + 1)
                            tile = tile + band[hl, :, off : off + 128]
                        else:
                            tile = tile + (after if jb > here else before)
                        tile = jnp.where(segcol[rows, :] == seg_q, tile, MASKED)
                        scr[rows, cols] = tile
                        top = jnp.maximum(top, jnp.max(tile.reshape(16, 8, 128), axis=0))
                    top = jnp.max(top, axis=0, keepdims=True)
                    for jb in range(8):
                        rows = slice(128 * jb, 128 * (jb + 1))
                        weight = jnp.exp(scr[rows, cols] - top)
                        e_scr[hd, rows, 256 * ib + 128 * t : 256 * ib + 128 * (t + 1)] = weight.astype(BF)
                both = dot_tn(vm, e_scr[hd, :, 256 * ib : 256 * (ib + 1)])
                span = slice(256 * ib, 256 * (ib + 1))
                data, sums = (both[0:HD], both[HD:128]) if hd == 0 else (both[HD:128], both[0:HD])
                inverse = 1.0 / sums
                ot_scr[HD * hd : HD * (hd + 1), span] = data * inverse
                linv[pl.ds(hl, 1), span] = inverse[0:1]
            pltpu.make_async_copy(e_scr.at[hd], e_o.at[hl], e_sem.at[hd]).start()
        mixed = jnp.transpose(ot_scr[...])
        o[:, lanes] = mixed
        ob[:, :, :, lanes] = mixed.astype(BF).reshape(4, 2, STRIPE, 128)
        mine = ob.at[:, 1 - c, :, lanes]
        remote(mine, ob_o.at[c, :, :, lanes], o_send.at[p], o_recv.at[p], me.core).start()
        return 0

    lax.fori_loop(0, 3, pair_step, 0)

    last = [
        pltpu.make_async_copy(ob.at[:, c], ob_o.at[c], l_sem.at[6]),
        pltpu.make_async_copy(o, o_o, l_sem.at[7]),
        pltpu.make_async_copy(linv, linv_o, l_sem.at[8]),
    ]
    for save in last:
        save.start()
    for hd in range(2):
        pltpu.make_async_copy(e_scr.at[hd], e_o.at[4 + hd], e_sem.at[hd]).wait()
    for p in range(3):
        lanes = slice(128 * p, 128 * (p + 1))
        mine = ob.at[:, 1 - c, :, lanes]
        there = remote(mine, ob_o.at[1 - c, :, :, lanes], o_send.at[p], o_recv.at[p], me.core)
        there.wait_send()
        there.wait_recv()
    for save in saves + last:
        save.wait()
    for fwd in forwards:
        fwd.wait_send()
    for zz in range(4):
        got = cot_o.at[zz]
        remote(got, got, c_send.at[0, 0], c_recv.at[zz], me.core).wait_recv()
    for r, kk, device, here in targets():

        @pl.when(jnp.logical_not(here))
        def _():
            src = tok.at[r, pl.ds(STRIPE * kk, STRIPE)]
            remote(src, xrow.at[z, kk], x_send.at[r, kk], x_recv.at[z], device).wait_send()
            remote(seg, segb.at[z], g_send.at[r, kk], g_recv.at[z], device).wait_send()
            srcc = cot.at[r, pl.ds(STRIPE * kk, STRIPE)]
            remote(srcc, cot_o.at[z], c_send.at[r, kk], c_recv.at[z], device).wait_send()


def run_forward(low, tokens, cotangent, segment_ids, w_query, w_key, w_value, norm_attn, bias_table):
    shapes = (
        ((4, STRIPE, D), BF),
        ((4, STRIPE, D), BF),
        ((SLOTS, D), BF),
        ((SLOTS, HALF), BF),
        ((SLOTS, HALF), BF),
        ((SLOTS, HALF), BF),
        ((6, SLOTS, SLOTS), BF),
        ((8, SLOTS), F32),
        ((SLOTS, HALF), F32),
        ((2, 4, STRIPE, HALF), BF),
        ((D, 3 * HALF), BF),
    )
    dma = pltpu.SemaphoreType.DMA
    return pl.pallas_call(
        functools.partial(forward_kernel, low),
        out_shape=[jax.ShapeDtypeStruct(s, t) for s, t in shapes],
        in_specs=[ANY, ANY, ANY, ANY, ANY, ANY, VM, SM],
        out_specs=[ANY] * len(shapes),
        scratch_shapes=[
            pltpu.VMEM((4, 2, STRIPE, D), BF),
            pltpu.VMEM((4, 2, 256), jnp.int32),
            pltpu.VMEM((3, D, D), BF),
            pltpu.VMEM((D, 3 * HALF), BF),
            pltpu.VMEM((SLOTS, D), BF),
            pltpu.VMEM((SLOTS, HALF), BF),
            pltpu.VMEM((SLOTS, HALF), BF),
            pltpu.VMEM((SLOTS, HALF), BF),
            pltpu.VMEM((6, 128, 384), F32),
            pltpu.VMEM((128, 384), jnp.int32),
            pltpu.VMEM((SLOTS, 128), F32),
            pltpu.VMEM((1, SLOTS), F32),
            pltpu.VMEM((2, SLOTS, 256), F32),
            pltpu.VMEM((2, SLOTS, SLOTS), BF),
            pltpu.VMEM((128, SLOTS), F32),
            pltpu.VMEM((128, SLOTS), F32),
            pltpu.VMEM((SLOTS, HALF), F32),
            pltpu.VMEM((4, 2, STRIPE, HALF), BF),
            pltpu.VMEM((8, SLOTS), F32),
            dma((2, 2)), dma((4,)), dma((4,)), dma((4,)), dma((2, 2)), dma((4,)),
            dma((2, 2)), dma((4,)), dma((3,)), dma((3,)), dma((9,)), dma((2,)),
        ],
        compiler_params=pltpu.CompilerParams(
            collective_id=0, has_side_effects=True, vmem_limit_bytes=56 * 2**20
        ),
        cost_estimate=pl.CostEstimate(flops=6 * 10**9, bytes_accessed=30 * 10**6, transcendentals=6 * 10**6),
        name="attention_forward",
    )(tokens, cotangent, segment_ids, w_query, w_key, w_value, norm_attn.reshape(1, D), bias_table)


GELU_SCALE = 0.7978845608028654
GELU_CUBE = 0.044715
GROUPS = ("gate0", "up0", "gate1", "up1", "down0", "down1", "out", "query", "key", "value")
WIDE = 6
SLOT = (0, 1, 2, 3, 4, 5, 6, 0, 1, 2)


class Reduction:
    def __init__(self, me, unit, wide, narrow, stage, send, recv, finish):
        self.me, self.unit, self.wide, self.narrow, self.stage = me, unit, wide, narrow, stage
        self.send, self.recv, self.finish = send, recv, finish
        self.step = [0] * len(GROUPS)

    def buffers(self, u):
        if u < WIDE:
            return [ref.at[u] for ref in self.wide]
        return [ref.at[u - WIDE] for ref in self.narrow]

    def copy(self, u, k):
        me = self.me
        r0, r1, r2, r3, r4 = self.buffers(u)
        cols = 512 if u < WIDE else HALF
        unit = self.unit.at[SLOT[u]]
        x_first = u % 2 == 0
        if k == 0 and u <= WIDE:
            src, dst, device = unit.at[:, :, :, 1 - me.c, :, pl.ds(0, cols)], r0, me.core
        elif k == 0:
            src, dst, device = unit.at[me.c, :, :, 1 - me.c, :, pl.ds(0, cols)], r0.at[me.c], me.core
        elif k == 1 and x_first:
            src, dst, device = r0.at[:, :, 1 - me.x], r1, me.xp
        elif k == 1:
            src, dst, device = r0.at[:, 1 - me.y], r1, me.yp
        elif k == 2 and x_first:
            src, dst, device = r1.at[:, 1 - me.y], r2, me.yp
        elif k == 2:
            src, dst, device = r1.at[:, 1 - me.x], r2, me.xp
        elif k == 3:
            src, dst, device = r2.at[1 - me.z0], r3, me.z0p
        elif u < WIDE:
            there = pl.ds(pl.multiple_of(256 * (1 - me.z1), 256), 256)
            src, dst, device = r3.at[:, there], r4, me.z1p
        else:
            src, dst, device = self.stage.at[u - WIDE], r4, me.z1p
        return remote(src, dst, self.send.at[u, k], self.recv.at[u, k], device)

    def advance(self, *names):
        for name in names:
            self.advance_one(GROUPS.index(name))

    def advance_one(self, u):
        me = self.me
        k = self.step[u]
        r0, r1, r2, r3, r4 = self.buffers(u)
        cols = 512 if u < WIDE else HALF
        unit = self.unit.at[SLOT[u]]
        x_first = u % 2 == 0
        if k > 0:
            self.copy(u, k - 1).wait()

        def add(into, other):
            into[...] = (into[...].astype(F32) + other[...].astype(F32)).astype(BF)

        if k == 1 and u <= WIDE:

            @pl.loop(0, 8)
            def _(i):
                a, y, x = i // 4, (i // 2) % 2, i % 2
                add(r0.at[a, y, x], unit.at[a, y, x, me.c, :, pl.ds(0, cols)])

        elif k == 1:

            @pl.loop(0, 4)
            def _(i):
                r0[me.c, i // 2, i % 2] = unit[me.c, i // 2, i % 2, me.c, :, pl.ds(0, cols)]

        elif k == 2:

            @pl.loop(0, 4)
            def _(i):
                a, b = i // 2, i % 2
                add(r1.at[a, b], r0.at[a, b, me.x] if x_first else r0.at[a, me.y, b])

        elif k == 3:

            @pl.loop(0, 2)
            def _(i):
                add(r2.at[i], r1.at[i, me.y if x_first else me.x])

        elif k == 4:
            add(r3, r2.at[me.z0])
            if u >= WIDE:
                self.stage[u - WIDE] = jnp.where(me.z1 == 0, r3[:, ZB:], r3[:, :ZB])
        elif k == 5:
            if u < WIDE:
                own = r3[:, pl.ds(pl.multiple_of(256 * me.z1, 256), 256)]
            else:
                own = jnp.where(me.z1 == 0, r3[:, :ZB], r3[:, ZB:])
            self.finish(GROUPS[u], own.astype(F32) + r4[...].astype(F32))
        if k < 5:
            self.copy(u, k).start()
        self.step[u] = k + 1


def backward_kernel(
    low,
    x_i, cot_i, n1_i, q_i, k_i, v_i, e_i, linv_i, o_i, ob_i, wown_i, w_out, w_gate, w_up, w_down, gain_a, gain_f,
    out_o, ig_o, gq_o, gk_o, gv_o, go_o, gg_o, gu_o, gd_o, stat_o,
    unit, a0, a1, a2, a3, a4, b0, b1, b2, b3, b4, bstage,
    xv, gv, obf, wout, dobv, dobrow, dqkv, pn_send, pn_recv, dh1, rows_out, dfin, bcount, stat, stat_in,
    red_send, red_recv, t_send, t_recv, i_send, i_recv, d_send, d_recv, p_send, p_recv, s_send, s_recv,
    l_sem, w_sem, a_sem, e_sem,
):
    me = Place(low)
    c, z = me.c, me.z

    def finish(name, total):
        if name[-1] in "01":
            kind, part = name[:-1], int(name[-1])
            if kind == "down":
                dfin[96 * part : 96 * (part + 1), :] = total
            else:
                {"gate": gg_o, "up": gu_o}[kind][:, 256 * part : 256 * (part + 1)] = total
        else:
            {"out": go_o, "query": gq_o, "key": gk_o, "value": gv_o}[name][...] = total

    red = Reduction(me, unit, (a0, a1, a2, a3, a4), (b0, b1, b2, b3, b4), bstage, red_send, red_recv, finish)

    first = [pltpu.make_async_copy(x_i, xv, l_sem.at[0]), pltpu.make_async_copy(ob_i, obf, l_sem.at[1]),
             pltpu.make_async_copy(cot_i, gv, l_sem.at[2])]
    for i in range(4):
        first.append(
            pltpu.make_async_copy(
                w_out.at[pl.ds(ZB * i, ZB)], wout.at[i % 2, pl.ds(ZB * (i // 2), ZB)], l_sem.at[3 + i]
            )
        )
    for copy in first:
        copy.start()

    def home(zz, send_sem, recv_sem, dest):
        dst = dest.at[me.z0, pl.ds(pl.multiple_of(STRIPE * c, STRIPE), STRIPE)]
        recv = recv_sem.at[me.z0, c]
        here = jnp.logical_and(zz == z, me.z1 == c)
        return here, rows_out.at[zz], dst, send_sem.at[zz], recv, (me.base + me.z1 * low, zz)

    def start_home(*where):
        for zz in range(4):
            here, src, dst, send, recv, device = home(zz, *where)

            @pl.when(here)
            def _():
                pltpu.make_async_copy(src, dst, send).start()

            @pl.when(jnp.logical_not(here))
            def _():
                remote(src, dst, send, recv, device).start()

    def sent_home(*where):
        for zz in range(4):
            here, src, dst, send, recv, device = home(zz, *where)

            @pl.when(here)
            def _():
                pltpu.make_async_copy(src, dst, send).wait()

            @pl.when(jnp.logical_not(here))
            def _():
                remote(src, dst, send, recv, device).wait_send()

    def got_home(send_sem, recv_sem, dest):
        for r in range(2):
            for kk in range(2):
                part = dest.at[r, pl.ds(STRIPE * kk, STRIPE)]

                @pl.when(jnp.logical_not(jnp.logical_and(2 * c + r == z, kk == c)))
                def _():
                    remote(part, part, send_sem.at[0], recv_sem.at[r, kk], me.core).wait_recv()

    to_partner = remote(dobv.at[1 - c], dobrow.at[:, c], d_send, d_recv, me.core)
    out_way = (t_send, t_recv, out_o)
    ig_way = (i_send, i_recv, ig_o)

    def feed_forward(wg, wu, wd, n2, h1, acc, hid, dga, dup):
        loads = {}
        for f in range(2):
            for which, (src, dst) in enumerate(((w_gate, wg), (w_up, wu), (w_down, wd))):
                for zz in range(4):
                    far = pl.ds(512 * zz + 256 * f, 256)
                    own = pl.ds(256 * zz, 256)
                    sem = w_sem.at[f, which, zz]
                    if which < 2:
                        copy = pltpu.make_async_copy(src.at[:, far], dst.at[f, :, own], sem)
                    else:
                        copy = pltpu.make_async_copy(src.at[far], dst.at[f, own], sem)
                    copy.start()
                    loads.setdefault((f, which), []).append(copy)
        greet(me.group() + [me.xp, me.yp])
        for copy in first:
            copy.wait()
        gain = gain_f[...].astype(F32)
        for i in range(2):
            rows = slice(256 * i, 256 * (i + 1))
            parts = slice(2 * i, 2 * (i + 1))
            h = xv[parts].reshape(256, D).astype(F32)
            h = h + dot(obf[0, parts].reshape(256, HALF), wout[0]) + dot(obf[1, parts].reshape(256, HALF), wout[1])
            h1[rows, :] = h
            r2 = lax.rsqrt(jnp.mean(h * h, axis=-1, keepdims=True) + EPSILON)
            n2[rows, :] = (h * r2 * gain).astype(BF)
        g = gv[...].reshape(OWN, D)
        for f in range(2):
            for which in range(3):
                for copy in loads[f, which]:
                    copy.wait()
            for i in range(2):
                rows = slice(256 * i, 256 * (i + 1))
                gate = dot(n2[rows, :], wg[f])
                up = dot(n2[rows, :], wu[f])
                dhid = dot_nt(gv[2 * i : 2 * (i + 1)].reshape(256, D), wd[f])
                square = gate * gate
                th = jnp.tanh(GELU_SCALE * gate * (1.0 + GELU_CUBE * square))
                half = 0.5 + 0.5 * th
                gelu = gate * half
                slope = half + 0.5 * GELU_SCALE * gate * (1.0 - th * th) * (1.0 + 3.0 * GELU_CUBE * square)
                hid[rows, :] = (gelu * up).astype(BF)
                dup[rows, :] = (dhid * gelu).astype(BF)
                dga[rows, :] = (dhid * up * slope).astype(BF)
            for which, grads in enumerate((dga, dup)):
                for zz in range(4):
                    piece = dot_tn(n2[...], grads[:, 256 * zz : 256 * (zz + 1)]).astype(BF)
                    unit[2 * f + which, zz % 2, :, :, :, :, 256 * (zz // 2) : 256 * (zz // 2 + 1)] = piece.reshape(
                        2, 2, 2, 96, 256
                    )
                red.advance(("gate0", "up0", "gate1", "up1")[2 * f + which])
            for zz in range(4):
                piece = dot_tn(g, hid[:, 256 * zz : 256 * (zz + 1)]).astype(BF)
                for to in range(4):
                    for part in range(2):
                        row = ZB * to + 96 * part
                        unit[4 + part, to % 2, zz // 2, zz % 2, f, :, 256 * (to // 2) : 256 * (to // 2 + 1)] = piece[
                            row : row + 96
                        ]
            if f == 0:
                red.advance("gate0", "up0")
                acc[...] = dot(hid[...], wd[f])
                dh1[...] = dot_nt(dga[...], wg[f]) + dot_nt(dup[...], wu[f])
            else:
                red.advance("down0", "down1", "gate1", "up1")
                acc[...] += dot(hid[...], wd[f])
                dh1[...] += dot_nt(dga[...], wg[f]) + dot_nt(dup[...], wu[f])
                red.advance("down0", "down1")
        total = jnp.zeros((1, D), F32)
        for i in range(4):
            rows = slice(128 * i, 128 * (i + 1))
            h = h1[rows, :]
            rows_out[i] = (h + acc[rows, :]).astype(BF)
            r2 = lax.rsqrt(jnp.mean(h * h, axis=-1, keepdims=True) + EPSILON)
            u2 = h * r2
            dn2 = dh1[rows, :]
            total = total + jnp.sum(dn2 * u2, axis=0, keepdims=True)
            wn = dn2 * gain
            dh = gv[i].astype(F32) + r2 * (wn - u2 * jnp.mean(wn * u2, axis=-1, keepdims=True))
            dh1[rows, :] = dh
            n2[rows, :] = dh.astype(BF)
        stat[...] = jnp.zeros((6, 8, 256), F32)
        for i in range(3):
            stat[0, i : i + 1, :] = total[:, 256 * i : 256 * (i + 1)]
        start_home(*out_way)
        dab = n2[...]
        for cp in range(2):
            dobv[cp] = dot_nt(dab, wout[cp]).astype(BF).reshape(4, STRIPE, HALF)
        to_partner.start()
        dobrow[:, c] = dobv[c]
        for a in range(2):
            dz = jnp.concatenate([dab[:, ZB * a : ZB * (a + 1)], dab[:, ZB * (a + 2) : ZB * (a + 3)]], axis=1)
            for cp in range(2):
                piece = dot_tn(obf[cp].reshape(OWN, HALF), dz).astype(BF)
                for yy in range(2):
                    for cc in range(2):
                        row = 96 * (2 * yy + cc)
                        unit[6, a, yy, cp, cc, :, 0:HALF] = piece[row : row + 96]
        red.advance("out")

    pl.run_scoped(
        feed_forward,
        pltpu.VMEM((2, D, 1024), BF),
        pltpu.VMEM((2, D, 1024), BF),
        pltpu.VMEM((2, 1024, D), BF),
        pltpu.VMEM((OWN, D), BF),
        pltpu.VMEM((OWN, D), F32),
        pltpu.VMEM((OWN, D), F32),
        pltpu.VMEM((OWN, 1024), BF),
        pltpu.VMEM((OWN, 1024), BF),
        pltpu.VMEM((OWN, 1024), BF),
    )

    plan = (
        ("out", "gate0", "up0"),
        ("gate1", "up1", "gate0", "up0"),
        ("down0", "down1", "gate0", "up0", "gate1", "up1"),
        ("out", "down0", "down1", "gate1", "up1"),
        ("down0", "down1", "out", "gate0", "up0"),
        ("out", "gate1", "up1"),
    )

    def attention(q, k, v, o, linv, e, ds, dp_scr, dob_scr, dv_scr, dk_scr, dqt_scr, band, bkt):
        loads = [
            pltpu.make_async_copy(src, dst, a_sem.at[i])
            for i, (src, dst) in enumerate(((q_i, q), (k_i, k), (v_i, v), (o_i, o), (linv_i, linv)))
        ]
        for load in loads:
            load.start()
        fetch = [pltpu.make_async_copy(e_i.at[h], e.at[h % 2], e_sem.at[h]) for h in range(6)]
        fetch[0].start()
        fetch[1].start()
        bkt[...] = bucket_tile()
        to_partner.wait()
        for load in loads:
            load.wait()
        first_half = lax.broadcasted_iota(jnp.int32, (1, 128), 1) < HD
        for p in range(3):
            lanes = slice(128 * p, 128 * (p + 1))
            kp, vp, qp = k[:, lanes], v[:, lanes], q[:, lanes]
            inverse = jnp.concatenate(
                [jnp.broadcast_to(linv[2 * p + hd : 2 * p + hd + 1, :], (HD, SLOTS)) for hd in range(2)], axis=0
            )
            scaled = dobrow[:, :, :, lanes].reshape(SLOTS, 128).astype(F32) * jnp.transpose(inverse)
            dob_scr[...] = scaled.astype(BF)
            product = jnp.transpose(scaled * o[:, lanes])
            for hd in range(2):
                h = 2 * p + hd
                delta = jnp.sum(product[HD * hd : HD * (hd + 1)], axis=0, keepdims=True)
                vm = vp * lane_mask(hd)
                fetch[h].wait()
                ev = e.at[hd]
                band[...] = jnp.zeros((128, 384), F32)
                after = jnp.zeros((8, 128), F32)
                before = jnp.zeros((8, 128), F32)
                for ib in range(4):
                    scr = dp_scr.at[ib % 2]
                    scr[...] = dot_nt(vm, dob_scr[256 * ib : 256 * (ib + 1), :])
                    for t in range(2):
                        here = 2 * ib + t
                        cols = slice(128 * here, 128 * (here + 1))
                        for jb in range(8):
                            rows = slice(128 * jb, 128 * (jb + 1))
                            dsv = ev[rows, cols].astype(F32) * (scr[rows, 128 * t : 128 * (t + 1)] - delta[:, cols])
                            ds[rows, cols] = dsv.astype(BF)
                            if abs(jb - here) <= 1:
                                off = 128 * (here - jb + 1)
                                band[:, off : off + 128] += dsv
                            elif jb > here:
                                after = after + jnp.sum(dsv.reshape(16, 8, 128), axis=0)
                            else:
                                before = before + jnp.sum(dsv.reshape(16, 8, 128), axis=0)
                dv = dot(ev[...], dob_scr[...])
                dk = dot(ds[...], qp)
                dqt_scr[HD * hd : HD * (hd + 1), :] = dot_tn(kp, ds[...])[HD * hd : HD * (hd + 1)]
                if hd == 0:
                    dv_scr[...] = dv
                    dk_scr[...] = dk
                else:
                    for i, val in enumerate(
                        (
                            jnp.transpose(dqt_scr[...]),
                            jnp.where(first_half, dk_scr[...], dk),
                            jnp.where(first_half, dv_scr[...], dv),
                        )
                    ):
                        dqkv[:, :, :, HALF * i + 128 * p : HALF * i + 128 * (p + 1)] = val.astype(BF).reshape(
                            4, 2, STRIPE, 128
                        )
                if h + 2 < 6:
                    fetch[h + 2].start()
                for b in range(32):
                    part = jnp.zeros((1, 128), F32)
                    for t in range(3):
                        own = slice(128 * t, 128 * (t + 1))
                        part = part + jnp.sum(jnp.where(bkt[:, own] == b, band[:, own], 0.0), axis=0, keepdims=True)
                    if b == FAR_AFTER:
                        part = part + jnp.sum(after, axis=0, keepdims=True)
                    if b == FAR_BEFORE:
                        part = part + jnp.sum(before, axis=0, keepdims=True)
                    bcount[32 * h + b : 32 * h + b + 1, :] = part
                red.advance(*plan[h])

    pl.run_scoped(
        attention,
        pltpu.VMEM((SLOTS, HALF), BF),
        pltpu.VMEM((SLOTS, HALF), BF),
        pltpu.VMEM((SLOTS, HALF), BF),
        pltpu.VMEM((SLOTS, HALF), F32),
        pltpu.VMEM((8, SLOTS), F32),
        pltpu.VMEM((2, SLOTS, SLOTS), BF),
        pltpu.VMEM((SLOTS, SLOTS), BF),
        pltpu.VMEM((2, SLOTS, 256), F32),
        pltpu.VMEM((SLOTS, 128), BF),
        pltpu.VMEM((SLOTS, 128), F32),
        pltpu.VMEM((SLOTS, 128), F32),
        pltpu.VMEM((128, SLOTS), F32),
        pltpu.VMEM((128, 384), F32),
        pltpu.VMEM((128, 384), jnp.int32),
    )

    def tail(n1, wown, dn1):
        loads = [pltpu.make_async_copy(n1_i, n1, a_sem.at[0]), pltpu.make_async_copy(wown_i, wown, a_sem.at[1])]
        for load in loads:
            load.start()
        sent_home(*out_way)
        loads[1].wait()
        pn_send[...] = dot_nt(dqkv[:, 1 - c].reshape(OWN, 3 * HALF), wown[...]).astype(BF).reshape(4, STRIPE, D)
        partial = remote(pn_send, pn_recv, p_send, p_recv, me.core)
        partial.start()
        loads[0].wait()
        for i, name in enumerate(("query", "key", "value")):
            grads = dqkv[:, :, :, HALF * i : HALF * (i + 1)].reshape(SLOTS, HALF)
            unit[i, c, :, :, :, :, 0:HALF] = dot_tn(n1[...], grads).astype(BF).reshape(2, 2, 2, 96, HALF)
            red.advance(name)
        dn1[...] = dot_nt(dqkv[:, c].reshape(OWN, 3 * HALF), wown[...])
        red.advance("query", "key", "value")
        partial.wait()
        gain = gain_a[...].astype(F32)
        total = jnp.zeros((1, D), F32)
        for i in range(4):
            rows = slice(128 * i, 128 * (i + 1))
            xf = xv[i].astype(F32)
            r1 = lax.rsqrt(jnp.mean(xf * xf, axis=-1, keepdims=True) + EPSILON)
            u1 = xf * r1
            dn = dn1[rows, :] + pn_recv[i].astype(F32)
            total = total + jnp.sum(dn * u1, axis=0, keepdims=True)
            wn = dn * gain
            ig = dh1[rows, :] + r1 * (wn - u1 * jnp.mean(wn * u1, axis=-1, keepdims=True))
            rows_out[i] = ig.astype(BF)
        start_home(*ig_way)
        for i in range(3):
            stat[0, 3 + i : 4 + i, :] = total[:, 256 * i : 256 * (i + 1)]
        counts = jnp.sum(jnp.transpose(bcount[...]), axis=0, keepdims=True)
        stat[0, pl.ds(6 + c, 1), :] = jnp.concatenate([counts, jnp.zeros((1, 64), F32)], axis=1)
        copies = []
        for i, other in enumerate((me.core, me.xp, me.yp, me.z0p, me.z1p)):
            copy = remote(stat.at[i], stat_in.at[i], s_send.at[i], s_recv.at[i], other)
            copy.start()
            if i == 0:
                red.advance("out", "query", "key", "value")
            if i == 1:
                red.advance("down0", "down1")
            if i == 2:
                red.advance("query", "key", "value")
            if i == 4:
                red.advance("query", "key", "value")
            copy.wait()
            stat[i + 1] = stat[i] + stat_in[i]
        stat_o[...] = stat[5]
        gd_o[...] = jnp.transpose(dfin[...])
        red.advance("query", "key", "value")
        sent_home(*ig_way)
        got_home(*out_way)
        got_home(*ig_way)

    pl.run_scoped(
        tail,
        pltpu.VMEM((SLOTS, D), BF),
        pltpu.VMEM((D, 3 * HALF), BF),
        pltpu.VMEM((OWN, D), F32),
    )


def run_backward(low, saved, w_out, w_gate, w_up, w_down, norm_attn, norm_ff):
    shapes = (
        ((2, 256, D), BF),
        ((2, 256, D), BF),
        ((96, ZB), F32),
        ((96, ZB), F32),
        ((96, ZB), F32),
        ((96, ZB), F32),
        ((96, 512), F32),
        ((96, 512), F32),
        ((256, ZB), F32),
        ((8, 256), F32),
    )
    dma = pltpu.SemaphoreType.DMA
    wide = [(2, 2, 2, 96, 512), (2, 2, 96, 512), (2, 96, 512), (96, 512), (96, 256)]
    narrow = [(2, 2, 2, 96, HALF), (2, 2, 96, HALF), (2, 96, HALF), (96, HALF), (96, ZB)]
    return pl.pallas_call(
        functools.partial(backward_kernel, low),
        out_shape=[jax.ShapeDtypeStruct(s, t) for s, t in shapes],
        in_specs=[ANY] * 15 + [VM, VM],
        out_specs=[ANY, ANY] + [VM] * 8,
        scratch_shapes=[
            pltpu.VMEM((7, 2, 2, 2, 2, 96, 512), BF),
            *[pltpu.VMEM((6, *s), BF) for s in wide],
            *[pltpu.VMEM((4, *s), BF) for s in narrow],
            pltpu.VMEM((4, 96, ZB), BF),
            pltpu.VMEM((4, STRIPE, D), BF),
            pltpu.VMEM((4, STRIPE, D), BF),
            pltpu.VMEM((2, 4, STRIPE, HALF), BF),
            pltpu.VMEM((2, HALF, D), BF),
            pltpu.VMEM((2, 4, STRIPE, HALF), BF),
            pltpu.VMEM((4, 2, STRIPE, HALF), BF),
            pltpu.VMEM((4, 2, STRIPE, 3 * HALF), BF),
            pltpu.VMEM((4, STRIPE, D), BF),
            pltpu.VMEM((4, STRIPE, D), BF),
            pltpu.VMEM((OWN, D), F32),
            pltpu.VMEM((4, STRIPE, D), BF),
            pltpu.VMEM((ZB, 256), F32),
            pltpu.VMEM((192, 128), F32),
            pltpu.VMEM((6, 8, 256), F32),
            pltpu.VMEM((5, 8, 256), F32),
            dma((10, 5)), dma((10, 5)),
            dma((4,)), dma((2, 2)), dma((4,)), dma((2, 2)),
            dma, dma, dma, dma, dma((5,)), dma((5,)),
            dma((7,)), dma((2, 3, 4)), dma((5,)), dma((6,)),
        ],
        compiler_params=pltpu.CompilerParams(
            collective_id=1, has_side_effects=True, vmem_limit_bytes=63 * 2**20
        ),
        cost_estimate=pl.CostEstimate(flops=30 * 10**9, bytes_accessed=40 * 10**6, transcendentals=10**6),
        name="layer_backward",
    )(*saved, w_out, w_gate, w_up, w_down, norm_attn.reshape(1, D), norm_ff.reshape(1, D))


def on_device(
    low,
    tokens,
    segment_ids,
    norm_attn,
    w_query,
    w_key,
    w_value,
    w_out,
    norm_ff,
    w_gate,
    w_up,
    w_down,
    bias_table,
    cotangent,
):
    saved = run_forward(low, tokens, cotangent, segment_ids, w_query, w_key, w_value, norm_attn, bias_table)
    output, input_grad, gq, gk, gv, go, gg, gu, gd, stat = run_backward(
        low, saved, w_out, w_gate, w_up, w_down, norm_attn, norm_ff
    )
    grads = (gq, gk, gv, go, gg, gu, gd)
    if low > 1:
        groups = [[low * high + i for i in range(low)] for high in range(8)]
        grads = tuple(
            lax.psum_scatter(g, "dp", scatter_dimension=0, axis_index_groups=groups, tiled=True) for g in grads
        )
        stat = lax.psum(stat, "dp", axis_index_groups=groups)
    gq, gk, gv, go, gg, gu, gd = grads
    table = jnp.transpose(stat[6:8, :192].reshape(2, 2, 3, 32), (1, 0, 2, 3)).reshape(H, 32).T
    return (
        output,
        input_grad.astype(F32),
        stat[3:6].reshape(D),
        gq,
        gk,
        gv,
        go,
        stat[0:3].reshape(D),
        gg,
        gu,
        gd,
        table,
    )


def solution(mesh):
    rows = P("dp", "blk", None)
    split = P("dp", "blk")
    return jax.shard_map(
        functools.partial(on_device, mesh.shape["dp"] // 8),
        mesh=mesh,
        in_specs=(rows, split, P(), P(), P(), P(), P(), P(), P(), P(), P(), P(), rows),
        out_specs=(rows, rows, P(), split, split, split, split, P(), split, split, split, P()),
        check_vma=False,
    )
```

```python
import functools

import jax
import jax.numpy as jnp
from jax import lax
from jax.experimental import pallas as pl
from jax.experimental.pallas import tpu as pltpu
from jax.sharding import PartitionSpec as P

H = 12
HD = 64
EPSILON = 1e-06
MASKED = -1e30
LIMITS = (12, 16, 23, 32, 46, 64, 91)
FAR_BEFORE = 15
FAR_AFTER = 31

MESH = pl.DeviceIdType.MESH
BF = jnp.bfloat16
F32 = jnp.float32
ANY = pl.BlockSpec(memory_space=pl.ANY)
VM = pl.BlockSpec(memory_space=pltpu.VMEM)

D = 768
HALF = 384
ZB = 192
SLOTS = 1024
STRIPE = 128
OWN = 512


def dot(a, b):
    return lax.dot_general(a, b, (((1,), (0,)), ((), ())), preferred_element_type=F32)


def dot_nt(a, b):
    return lax.dot_general(a, b, (((1,), (1,)), ((), ())), preferred_element_type=F32)


def dot_tn(a, b):
    return lax.dot_general(a, b, (((0,), (0,)), ((), ())), preferred_element_type=F32)


class Place:
    def __init__(self, low):
        self.low = low
        self.dp = lax.axis_index("dp")
        self.z = lax.axis_index("blk")
        high = self.dp // low
        self.c = high % 2
        self.x = (high // 2) % 2
        self.y = high // 4
        self.base = self.dp - self.c * low
        self.z0 = self.z % 2
        self.z1 = self.z // 2
        self.core = (self.dp + low * (1 - 2 * self.c), self.z)
        self.xp = (self.dp + 2 * low * (1 - 2 * self.x), self.z)
        self.yp = (self.dp + 4 * low * (1 - 2 * self.y), self.z)
        self.z0p = (self.dp, self.z + 1 - 2 * self.z0)
        self.z1p = (self.dp, self.z + 2 - 4 * self.z1)

    def group(self):
        found = []
        for dc in range(2):
            for dz in range(4):
                if dc or dz:
                    found.append((self.base + ((self.c + dc) % 2) * self.low, (self.z + dz) % 4))
        return found

    def near(self, k):
        fold = jnp.where(self.z < 2, self.z, 3 - self.z)
        step = (k + fold * (1 - 2 * k)) if k < 2 else k
        return jnp.where(self.z < 2, step, 3 - step)


def greet(others):
    barrier = pltpu.get_barrier_semaphore()
    for other in others:
        pl.semaphore_signal(barrier, inc=1, device_id=other, device_id_type=MESH)
    pl.semaphore_wait(barrier, len(others))


def remote(src, dst, send, recv, device):
    return pltpu.make_async_remote_copy(
        src_ref=src, dst_ref=dst, send_sem=send, recv_sem=recv, device_id=device, device_id_type=MESH
    )


def bucket_tile():
    key = lax.broadcasted_iota(jnp.int32, (128, 384), 0)
    query = lax.broadcasted_iota(jnp.int32, (128, 384), 1)
    rel = key - query + 128
    dist = jnp.abs(rel)
    beyond = jnp.full((128, 384), 8, jnp.int32)
    for threshold in LIMITS:
        beyond = beyond + (dist >= threshold).astype(jnp.int32)
    return jnp.where(dist < 8, dist, beyond) + jnp.where(rel > 0, 16, 0)


def head_of(place, local):
    return 3 * place.c + local % 3 + 6 * (local // 3)


def lane_mask(head_in_pair):
    lane = lax.broadcasted_iota(jnp.int32, (1, 128), 1)
    inside = (lane < HD) if head_in_pair == 0 else (lane >= HD)
    return inside.astype(F32).astype(BF)


def forward_kernel(
    low,
    tok, cot, seg, wq, wk, wv, gain, table_i,
    x_o, cot_o, n1_o, q_o, k_o, v_o, e_o, linv_o, o_o, ob_o, wown_o,
    table, xrow, segb, wfull, wown, n1, q, k, v, band, bkt, segcol, segrow, s_scr, e_scr, ot_scr, o, ob, linv,
    x_send, x_recv, f_send, f_recv, c_send, c_recv, g_send, g_recv, o_send, o_recv, l_sem, e_sem,
):
    me = Place(low)
    c, z = me.c, me.z

    loads = [pltpu.make_async_copy(w, wfull.at[i], l_sem.at[i]) for i, w in enumerate((wq, wk, wv))]
    for load in loads:
        load.start()
    table_load = pltpu.make_async_copy(table_i, table, l_sem.at[3])
    table_load.start()
    greet(me.group())

    def targets():
        for r in range(2):
            for kk in range(2):
                yield r, kk, (me.base + kk * low, 2 * c + r), jnp.logical_and(2 * c + r == z, kk == c)

    for r, kk, device, here in targets():
        src = tok.at[r, pl.ds(STRIPE * kk, STRIPE)]
        dst = xrow.at[z, kk]
        far = remote(src, dst, x_send.at[r, kk], x_recv.at[z], device)
        near = pltpu.make_async_copy(src, dst, x_recv.at[z])
        sfar = remote(seg, segb.at[z], g_send.at[r, kk], g_recv.at[z], device)
        snear = pltpu.make_async_copy(seg, segb.at[z], g_recv.at[z])

        @pl.when(here)
        def _():
            near.start()
            snear.start()

        @pl.when(jnp.logical_not(here))
        def _():
            far.start()
            sfar.start()

    for i in range(3):
        loads[i].wait()
        lo = jnp.concatenate([wfull[i, :, 0:ZB], wfull[i, :, 2 * ZB : 3 * ZB]], axis=1)
        hi = jnp.concatenate([wfull[i, :, ZB : 2 * ZB], wfull[i, :, 3 * ZB : 4 * ZB]], axis=1)
        wown[:, HALF * i : HALF * (i + 1)] = jnp.where(c == 0, lo, hi)
    bkt[...] = bucket_tile()
    table_load.wait()

    def make_band(hl, _):
        head = head_of(me, hl)
        for t in range(3):
            which = bkt[:, 128 * t : 128 * (t + 1)]
            total = jnp.zeros((128, 128), F32)
            for b in range(32):
                total = jnp.where(which == b, table[b, head], total)
            band[hl, :, 128 * t : 128 * (t + 1)] = total
        return 0

    lax.fori_loop(0, 6, make_band, 0)

    gain_f = gain[...].astype(F32).reshape(1, D)
    forwards = []
    for step in range(4):
        zz = me.near(step)
        own = xrow.at[zz, c]
        remote(own, own, x_send.at[0, 0], x_recv.at[zz], me.core).wait_recv()
        fwd = remote(own, own, f_send.at[step], f_recv.at[zz], me.core)
        fwd.start()
        forwards.append(fwd)
    for step in range(4):
        zz = me.near(step)
        other = xrow.at[zz, 1 - c]
        remote(other, other, f_send.at[step], f_recv.at[zz], me.core).wait_recv()
        xf = xrow[zz].reshape(256, D).astype(F32)
        r1 = lax.rsqrt(jnp.mean(xf * xf, axis=-1, keepdims=True) + EPSILON)
        nb = (xf * r1 * gain_f).astype(BF)
        rows = pl.ds(pl.multiple_of(zz * 256, 256), 256)
        n1[rows, :] = nb
        for i, dest in enumerate((q, k, v)):
            dest[rows, :] = dot(nb, wown[:, HALF * i : HALF * (i + 1)]).astype(BF)

    for r, kk, device, here in targets():
        src = cot.at[r, pl.ds(STRIPE * kk, STRIPE)]
        dst = cot_o.at[z]
        far = remote(src, dst, c_send.at[r, kk], c_recv.at[z], device)
        near = pltpu.make_async_copy(src, dst, c_recv.at[z])

        @pl.when(here)
        def _():
            near.start()

        @pl.when(jnp.logical_not(here))
        def _():
            far.start()

    saves = [
        pltpu.make_async_copy(src, dst, l_sem.at[i])
        for i, (src, dst) in enumerate(
            (
                (xrow.at[:, c], x_o),
                (n1, n1_o),
                (q, q_o),
                (k, k_o),
                (v, v_o),
                (wown, wown_o),
            )
        )
    ]
    for save in saves:
        save.start()

    for zz in range(4):
        blk_seg = segb.at[zz]
        remote(blk_seg, blk_seg, g_send.at[0, 0], g_recv.at[zz], me.core).wait_recv()
        segrow[:, 256 * zz : 256 * (zz + 1)] = segb[zz, pl.ds(z % 2, 1), :].astype(F32)
    segcol[...] = jnp.transpose(jnp.broadcast_to(segrow[...], (128, SLOTS)))
    linv[...] = jnp.zeros((8, SLOTS), F32)

    def pair_step(p, _):
        lanes = pl.ds(pl.multiple_of(p * 128, 128), 128)
        kp, vp = k[:, lanes], v[:, lanes]
        for hd in range(2):
            mask = lane_mask(hd)
            vm = vp * mask + (1 - mask)
            hl = 2 * p + hd
            head = head_of(me, hl)
            after, before = table[FAR_AFTER, head], table[FAR_BEFORE, head]

            @pl.when(p > 0)
            def _():
                pltpu.make_async_copy(e_scr.at[hd], e_o.at[hl], e_sem.at[hd]).wait()

            for ib in range(4):
                qm = q[256 * ib : 256 * (ib + 1), lanes] * mask
                scr = s_scr.at[ib % 2]
                scr[...] = dot_nt(kp, qm)
                for t in range(2):
                    here = 2 * ib + t
                    cols = slice(128 * t, 128 * (t + 1))
                    seg_q = segrow[:, 256 * ib + 128 * t : 256 * ib + 128 * (t + 1)]
                    top = jnp.full((8, 128), MASKED, F32)
                    for jb in range(8):
                        rows = slice(128 * jb, 128 * (jb + 1))
                        tile = scr[rows, cols]
                        if abs(jb - here) <= 1:
                            off = 128 * (here - jb + 1)
                            tile = tile + band[hl, :, off : off + 128]
                        else:
                            tile = tile + (after if jb > here else before)
                        tile = jnp.where(segcol[rows, :] == seg_q, tile, MASKED)
                        scr[rows, cols] = tile
                        top = jnp.maximum(top, jnp.max(tile.reshape(16, 8, 128), axis=0))
                    top = jnp.max(top, axis=0, keepdims=True)
                    for jb in range(8):
                        rows = slice(128 * jb, 128 * (jb + 1))
                        weight = jnp.exp(scr[rows, cols] - top)
                        e_scr[hd, rows, 256 * ib + 128 * t : 256 * ib + 128 * (t + 1)] = weight.astype(BF)
            both = dot_tn(vm, e_scr[hd])
            data, sums = (both[0:HD], both[HD:128]) if hd == 0 else (both[HD:128], both[0:HD])
            inverse = 1.0 / sums
            ot_scr[HD * hd : HD * (hd + 1), :] = data * inverse
            linv[pl.ds(hl, 1), :] = inverse[0:1]
            pltpu.make_async_copy(e_scr.at[hd], e_o.at[hl], e_sem.at[hd]).start()
        mixed = jnp.transpose(ot_scr[...])
        o[:, lanes] = mixed
        ob[:, :, :, lanes] = mixed.astype(BF).reshape(4, 2, STRIPE, 128)
        mine = ob.at[:, 1 - c, :, lanes]
        remote(mine, ob_o.at[c, :, :, lanes], o_send.at[p], o_recv.at[p], me.core).start()
        return 0

    lax.fori_loop(0, 3, pair_step, 0)

    last = [
        pltpu.make_async_copy(ob.at[:, c], ob_o.at[c], l_sem.at[6]),
        pltpu.make_async_copy(o, o_o, l_sem.at[7]),
        pltpu.make_async_copy(linv, linv_o, l_sem.at[8]),
    ]
    for save in last:
        save.start()
    for hd in range(2):
        pltpu.make_async_copy(e_scr.at[hd], e_o.at[4 + hd], e_sem.at[hd]).wait()
    for p in range(3):
        lanes = slice(128 * p, 128 * (p + 1))
        mine = ob.at[:, 1 - c, :, lanes]
        there = remote(mine, ob_o.at[1 - c, :, :, lanes], o_send.at[p], o_recv.at[p], me.core)
        there.wait_send()
        there.wait_recv()
    for save in saves + last:
        save.wait()
    for fwd in forwards:
        fwd.wait_send()
    for zz in range(4):
        got = cot_o.at[zz]
        remote(got, got, c_send.at[0, 0], c_recv.at[zz], me.core).wait_recv()
    for r, kk, device, here in targets():

        @pl.when(jnp.logical_not(here))
        def _():
            src = tok.at[r, pl.ds(STRIPE * kk, STRIPE)]
            remote(src, xrow.at[z, kk], x_send.at[r, kk], x_recv.at[z], device).wait_send()
            remote(seg, segb.at[z], g_send.at[r, kk], g_recv.at[z], device).wait_send()
            srcc = cot.at[r, pl.ds(STRIPE * kk, STRIPE)]
            remote(srcc, cot_o.at[z], c_send.at[r, kk], c_recv.at[z], device).wait_send()


def run_forward(low, tokens, cotangent, segment_ids, w_query, w_key, w_value, norm_attn, bias_table):
    shapes = (
        ((4, STRIPE, D), BF),
        ((4, STRIPE, D), BF),
        ((SLOTS, D), BF),
        ((SLOTS, HALF), BF),
        ((SLOTS, HALF), BF),
        ((SLOTS, HALF), BF),
        ((6, SLOTS, SLOTS), BF),
        ((8, SLOTS), F32),
        ((SLOTS, HALF), F32),
        ((2, 4, STRIPE, HALF), BF),
        ((D, 3 * HALF), BF),
    )
    dma = pltpu.SemaphoreType.DMA
    return pl.pallas_call(
        functools.partial(forward_kernel, low),
        out_shape=[jax.ShapeDtypeStruct(s, t) for s, t in shapes],
        in_specs=[ANY, ANY, ANY, ANY, ANY, ANY, VM, ANY],
        out_specs=[ANY] * len(shapes),
        scratch_shapes=[
            pltpu.SMEM((32, H), F32),
            pltpu.VMEM((4, 2, STRIPE, D), BF),
            pltpu.VMEM((4, 2, 256), jnp.int32),
            pltpu.VMEM((3, D, D), BF),
            pltpu.VMEM((D, 3 * HALF), BF),
            pltpu.VMEM((SLOTS, D), BF),
            pltpu.VMEM((SLOTS, HALF), BF),
            pltpu.VMEM((SLOTS, HALF), BF),
            pltpu.VMEM((SLOTS, HALF), BF),
            pltpu.VMEM((6, 128, 384), F32),
            pltpu.VMEM((128, 384), jnp.int32),
            pltpu.VMEM((SLOTS, 128), F32),
            pltpu.VMEM((1, SLOTS), F32),
            pltpu.VMEM((2, SLOTS, 256), F32),
            pltpu.VMEM((2, SLOTS, SLOTS), BF),
            pltpu.VMEM((128, SLOTS), F32),
            pltpu.VMEM((SLOTS, HALF), F32),
            pltpu.VMEM((4, 2, STRIPE, HALF), BF),
            pltpu.VMEM((8, SLOTS), F32),
            dma((2, 2)), dma((4,)), dma((4,)), dma((4,)), dma((2, 2)), dma((4,)),
            dma((2, 2)), dma((4,)), dma((3,)), dma((3,)), dma((9,)), dma((2,)),
        ],
        compiler_params=pltpu.CompilerParams(
            collective_id=0, has_side_effects=True, vmem_limit_bytes=56 * 2**20
        ),
        cost_estimate=pl.CostEstimate(flops=6 * 10**9, bytes_accessed=30 * 10**6, transcendentals=6 * 10**6),
        name="attention_forward",
    )(tokens, cotangent, segment_ids, w_query, w_key, w_value, norm_attn, bias_table)


GELU_SCALE = 0.7978845608028654
GELU_CUBE = 0.044715
GROUPS = ("gate0", "up0", "gate1", "up1", "down0", "down1", "out", "query", "key", "value")
WIDE = 6
SLOT = (0, 1, 2, 3, 4, 5, 6, 0, 1, 2)
PLAN = (
    (0,), (1,), (), (), (), (0,), (1,), (), (), (), (2,), (3,), (), (4, 5), (), (2,), (0, 3, 1, 4), (5,), (6,), (),
    (), (), (6,), (0,), (), (), (), (), (2,), (), (), (), (), (), (), (1,), (0,), (3,), (), (), (), (), (), (),
    (1, 7), (0, 8), (4, 9), (5, 7, 8), (1, 9), (2, 6), (4, 3), (2,), (5, 7), (),
    (4, 8, 3, 9, 2, 7, 5, 6, 9, 4, 8, 3, 7, 5, 6, 8, 9, 7, 6, 8, 9),
)


class Reduction:
    def __init__(self, me, unit, wide, narrow, stage, send, recv, finish):
        self.me, self.unit, self.wide, self.narrow, self.stage = me, unit, wide, narrow, stage
        self.send, self.recv, self.finish = send, recv, finish
        self.step = [0] * len(GROUPS)
        self.polls = 0

    def buffers(self, u):
        if u < WIDE:
            return [ref.at[u] for ref in self.wide]
        return [ref.at[u - WIDE] for ref in self.narrow]

    def copy(self, u, k):
        me = self.me
        r0, r1, r2, r3, r4 = self.buffers(u)
        cols = 512 if u < WIDE else HALF
        unit = self.unit.at[SLOT[u]]
        x_first = u % 2 == 0
        if k == 0 and u <= WIDE:
            src, dst, device = unit.at[:, :, :, 1 - me.c, :, pl.ds(0, cols)], r0, me.core
        elif k == 0:
            src, dst, device = unit.at[me.c, :, :, 1 - me.c, :, pl.ds(0, cols)], r0.at[me.c], me.core
        elif k == 1 and x_first:
            src, dst, device = r0.at[:, :, 1 - me.x], r1, me.xp
        elif k == 1:
            src, dst, device = r0.at[:, 1 - me.y], r1, me.yp
        elif k == 2 and x_first:
            src, dst, device = r1.at[:, 1 - me.y], r2, me.yp
        elif k == 2:
            src, dst, device = r1.at[:, 1 - me.x], r2, me.xp
        elif k == 3:
            src, dst, device = r2.at[1 - me.z0], r3, me.z0p
        elif u < WIDE:
            there = pl.ds(pl.multiple_of(256 * (1 - me.z1), 256), 256)
            src, dst, device = r3.at[:, there], r4, me.z1p
        else:
            src, dst, device = self.stage.at[u - WIDE], r4, me.z1p
        return remote(src, dst, self.send.at[u, k], self.recv.at[u, k], device)

    def poll(self):
        for u in PLAN[self.polls]:
            self.advance_one(u)
        self.polls += 1

    def advance_one(self, u):
        me = self.me
        k = self.step[u]
        r0, r1, r2, r3, r4 = self.buffers(u)
        cols = 512 if u < WIDE else HALF
        unit = self.unit.at[SLOT[u]]
        x_first = u % 2 == 0
        if k > 0:
            self.copy(u, k - 1).wait()

        def add(into, other):
            into[...] = (into[...].astype(F32) + other[...].astype(F32)).astype(BF)

        if k == 1 and u <= WIDE:

            @pl.loop(0, 8)
            def _(i):
                a, y, x = i // 4, (i // 2) % 2, i % 2
                add(r0.at[a, y, x], unit.at[a, y, x, me.c, :, pl.ds(0, cols)])

        elif k == 1:

            @pl.loop(0, 4)
            def _(i):
                r0[me.c, i // 2, i % 2] = unit[me.c, i // 2, i % 2, me.c, :, pl.ds(0, cols)]

        elif k == 2:

            @pl.loop(0, 4)
            def _(i):
                a, b = i // 2, i % 2
                add(r1.at[a, b], r0.at[a, b, me.x] if x_first else r0.at[a, me.y, b])

        elif k == 3:

            @pl.loop(0, 2)
            def _(i):
                add(r2.at[i], r1.at[i, me.y if x_first else me.x])

        elif k == 4:
            add(r3, r2.at[me.z0])
            if u >= WIDE:
                self.stage[u - WIDE] = jnp.where(me.z1 == 0, r3[:, ZB:], r3[:, :ZB])
        elif k == 5:
            if u < WIDE:
                own = r3[:, pl.ds(pl.multiple_of(256 * me.z1, 256), 256)]
            else:
                own = jnp.where(me.z1 == 0, r3[:, :ZB], r3[:, ZB:])
            self.finish(GROUPS[u], own.astype(F32) + r4[...].astype(F32))
        if k < 5:
            self.copy(u, k).start()
        self.step[u] = k + 1


def backward_kernel(
    low,
    x_i, cot_i, n1_i, q_i, k_i, v_i, e_i, linv_i, o_i, ob_i, wown_i, w_out, w_gate, w_up, w_down, gain_a, gain_f,
    out_o, ig_o, gq_o, gk_o, gv_o, go_o, gg_o, gu_o, gd_o, stat_o,
    unit, a0, a1, a2, a3, a4, b0, b1, b2, b3, b4, bstage,
    xv, gv, obf, wout, dobv, dobrow, dqkv, pn_send, pn_recv, dh1, rows_out, dfin, bcount, stat, stat_in,
    red_send, red_recv, t_send, t_recv, i_send, i_recv, d_send, d_recv, p_send, p_recv, s_send, s_recv,
    l_sem, w_sem, a_sem, e_sem,
):
    me = Place(low)
    c, z = me.c, me.z

    def finish(name, total):
        if name[-1] in "01":
            kind, part = name[:-1], int(name[-1])
            if kind == "down":
                dfin[96 * part : 96 * (part + 1), :] = total
            else:
                {"gate": gg_o, "up": gu_o}[kind][:, 256 * part : 256 * (part + 1)] = total
        else:
            {"out": go_o, "query": gq_o, "key": gk_o, "value": gv_o}[name][...] = total

    red = Reduction(me, unit, (a0, a1, a2, a3, a4), (b0, b1, b2, b3, b4), bstage, red_send, red_recv, finish)

    first = [pltpu.make_async_copy(x_i, xv, l_sem.at[0]), pltpu.make_async_copy(ob_i, obf, l_sem.at[1]),
             pltpu.make_async_copy(cot_i, gv, l_sem.at[2])]
    for i in range(4):
        first.append(
            pltpu.make_async_copy(
                w_out.at[pl.ds(ZB * i, ZB)], wout.at[i % 2, pl.ds(ZB * (i // 2), ZB)], l_sem.at[3 + i]
            )
        )
    for copy in first:
        copy.start()

    def home(zz, send_sem, recv_sem, dest):
        dst = dest.at[me.z0, pl.ds(pl.multiple_of(STRIPE * c, STRIPE), STRIPE)]
        recv = recv_sem.at[me.z0, c]
        here = jnp.logical_and(zz == z, me.z1 == c)
        return here, rows_out.at[zz], dst, send_sem.at[zz], recv, (me.base + me.z1 * low, zz)

    def start_home(*where):
        for zz in range(4):
            here, src, dst, send, recv, device = home(zz, *where)

            @pl.when(here)
            def _():
                pltpu.make_async_copy(src, dst, send).start()

            @pl.when(jnp.logical_not(here))
            def _():
                remote(src, dst, send, recv, device).start()

    def sent_home(*where):
        for zz in range(4):
            here, src, dst, send, recv, device = home(zz, *where)

            @pl.when(here)
            def _():
                pltpu.make_async_copy(src, dst, send).wait()

            @pl.when(jnp.logical_not(here))
            def _():
                remote(src, dst, send, recv, device).wait_send()

    def got_home(send_sem, recv_sem, dest):
        for r in range(2):
            for kk in range(2):
                part = dest.at[r, pl.ds(STRIPE * kk, STRIPE)]

                @pl.when(jnp.logical_not(jnp.logical_and(2 * c + r == z, kk == c)))
                def _():
                    remote(part, part, send_sem.at[0], recv_sem.at[r, kk], me.core).wait_recv()

    to_partner = remote(dobv.at[1 - c], dobrow.at[:, c], d_send, d_recv, me.core)
    out_way = (t_send, t_recv, out_o)
    ig_way = (i_send, i_recv, ig_o)

    def feed_forward(wg, wu, wd, n2, h1, acc, hid, dga, dup):
        loads = {}
        for f in range(2):
            for which, (src, dst) in enumerate(((w_gate, wg), (w_up, wu), (w_down, wd))):
                for zz in range(4):
                    far = pl.ds(512 * zz + 256 * f, 256)
                    own = pl.ds(256 * zz, 256)
                    sem = w_sem.at[f, which, zz]
                    if which < 2:
                        copy = pltpu.make_async_copy(src.at[:, far], dst.at[f, :, own], sem)
                    else:
                        copy = pltpu.make_async_copy(src.at[far], dst.at[f, own], sem)
                    copy.start()
                    loads.setdefault((f, which), []).append(copy)
        greet(me.group() + [me.xp, me.yp])
        for copy in first:
            copy.wait()
        gain = gain_f[...].astype(F32).reshape(1, D)
        for i in range(2):
            rows = slice(256 * i, 256 * (i + 1))
            parts = slice(2 * i, 2 * (i + 1))
            h = xv[parts].reshape(256, D).astype(F32)
            h = h + dot(obf[0, parts].reshape(256, HALF), wout[0]) + dot(obf[1, parts].reshape(256, HALF), wout[1])
            h1[rows, :] = h
            r2 = lax.rsqrt(jnp.mean(h * h, axis=-1, keepdims=True) + EPSILON)
            n2[rows, :] = (h * r2 * gain).astype(BF)
        g = gv[...].reshape(OWN, D)
        for f in range(2):
            for which in range(3):
                for copy in loads[f, which]:
                    copy.wait()
            for i in range(2):
                rows = slice(256 * i, 256 * (i + 1))
                gate = dot(n2[rows, :], wg[f])
                up = dot(n2[rows, :], wu[f])
                dhid = dot_nt(gv[2 * i : 2 * (i + 1)].reshape(256, D), wd[f])
                square = gate * gate
                th = jnp.tanh(GELU_SCALE * gate * (1.0 + GELU_CUBE * square))
                half = 0.5 + 0.5 * th
                gelu = gate * half
                slope = half + 0.5 * GELU_SCALE * gate * (1.0 - th * th) * (1.0 + 3.0 * GELU_CUBE * square)
                hid[rows, :] = (gelu * up).astype(BF)
                dup[rows, :] = (dhid * gelu).astype(BF)
                dga[rows, :] = (dhid * up * slope).astype(BF)
                if f == 1:
                    red.poll()
            if f == 1:
                for i in range(4):
                    rows = slice(128 * i, 128 * (i + 1))
                    rows_out[i] = (h1[rows, :] + acc[rows, :] + dot(hid[rows, :], wd[f])).astype(BF)
                start_home(*out_way)
                red.poll()
            for which, grads in enumerate((dga, dup)):
                for zz in range(4):
                    piece = dot_tn(n2[...], grads[:, 256 * zz : 256 * (zz + 1)]).astype(BF)
                    unit[2 * f + which, zz % 2, :, :, :, :, 256 * (zz // 2) : 256 * (zz // 2 + 1)] = piece.reshape(
                        2, 2, 2, 96, 256
                    )
                red.poll()
            for zz in range(4):
                piece = dot_tn(g, hid[:, 256 * zz : 256 * (zz + 1)]).astype(BF)
                for to in range(4):
                    for part in range(2):
                        row = ZB * to + 96 * part
                        unit[4 + part, to % 2, zz // 2, zz % 2, f, :, 256 * (to // 2) : 256 * (to // 2 + 1)] = piece[
                            row : row + 96
                        ]
                if zz % 2:
                    red.poll()
            if f == 0:
                acc[...] = dot(hid[...], wd[f])
                red.poll()
                dh1[...] = dot_nt(dga[...], wg[f])
            else:
                dh1[...] += dot_nt(dga[...], wg[f])
            red.poll()
            dh1[...] += dot_nt(dup[...], wu[f])
            red.poll()
        total = jnp.zeros((1, D), F32)
        for i in range(4):
            rows = slice(128 * i, 128 * (i + 1))
            h = h1[rows, :]
            r2 = lax.rsqrt(jnp.mean(h * h, axis=-1, keepdims=True) + EPSILON)
            u2 = h * r2
            dn2 = dh1[rows, :]
            total = total + jnp.sum(dn2 * u2, axis=0, keepdims=True)
            wn = dn2 * gain
            dh = gv[i].astype(F32) + r2 * (wn - u2 * jnp.mean(wn * u2, axis=-1, keepdims=True))
            dh1[rows, :] = dh
            n2[rows, :] = dh.astype(BF)
        stat[...] = jnp.zeros((6, 8, 256), F32)
        for i in range(3):
            stat[0, i : i + 1, :] = total[:, 256 * i : 256 * (i + 1)]
        red.poll()
        dab = n2[...]
        for cp in range(2):
            dobv[cp] = dot_nt(dab, wout[cp]).astype(BF).reshape(4, STRIPE, HALF)
        to_partner.start()
        dobrow[:, c] = dobv[c]
        red.poll()
        for a in range(2):
            dz = jnp.concatenate([dab[:, ZB * a : ZB * (a + 1)], dab[:, ZB * (a + 2) : ZB * (a + 3)]], axis=1)
            for cp in range(2):
                piece = dot_tn(obf[cp].reshape(OWN, HALF), dz).astype(BF)
                for yy in range(2):
                    for cc in range(2):
                        row = 96 * (2 * yy + cc)
                        unit[6, a, yy, cp, cc, :, 0:HALF] = piece[row : row + 96]
        red.poll()

    pl.run_scoped(
        feed_forward,
        pltpu.VMEM((2, D, 1024), BF),
        pltpu.VMEM((2, D, 1024), BF),
        pltpu.VMEM((2, 1024, D), BF),
        pltpu.VMEM((OWN, D), BF),
        pltpu.VMEM((OWN, D), F32),
        pltpu.VMEM((OWN, D), F32),
        pltpu.VMEM((OWN, 1024), BF),
        pltpu.VMEM((OWN, 1024), BF),
        pltpu.VMEM((OWN, 1024), BF),
    )

    def attention(q, k, v, o, linv, e, ds, dp_scr, dob_scr, dv_scr, dk_scr, dqt_scr, band, bkt):
        loads = [
            pltpu.make_async_copy(src, dst, a_sem.at[i])
            for i, (src, dst) in enumerate(((q_i, q), (k_i, k), (v_i, v), (o_i, o), (linv_i, linv)))
        ]
        for load in loads:
            load.start()
        fetch = [pltpu.make_async_copy(e_i.at[h], e.at[h % 2], e_sem.at[h]) for h in range(6)]
        fetch[0].start()
        fetch[1].start()
        bkt[...] = bucket_tile()
        to_partner.wait()
        for load in loads:
            load.wait()
        first_half = lax.broadcasted_iota(jnp.int32, (1, 128), 1) < HD
        for p in range(3):
            lanes = slice(128 * p, 128 * (p + 1))
            kp, vp, qp = k[:, lanes], v[:, lanes], q[:, lanes]
            inverse = jnp.concatenate(
                [jnp.broadcast_to(linv[2 * p + hd : 2 * p + hd + 1, :], (HD, SLOTS)) for hd in range(2)], axis=0
            )
            scaled = dobrow[:, :, :, lanes].reshape(SLOTS, 128).astype(F32) * jnp.transpose(inverse)
            dob_scr[...] = scaled.astype(BF)
            product = jnp.transpose(scaled * o[:, lanes])
            for hd in range(2):
                h = 2 * p + hd
                delta = jnp.sum(product[HD * hd : HD * (hd + 1)], axis=0, keepdims=True)
                vm = vp * lane_mask(hd)
                fetch[h].wait()
                ev = e.at[hd]
                band[...] = jnp.zeros((128, 384), F32)
                after = jnp.zeros((8, 128), F32)
                before = jnp.zeros((8, 128), F32)
                for ib in range(4):
                    scr = dp_scr.at[ib % 2]
                    scr[...] = dot_nt(vm, dob_scr[256 * ib : 256 * (ib + 1), :])
                    for t in range(2):
                        here = 2 * ib + t
                        cols = slice(128 * here, 128 * (here + 1))
                        for jb in range(8):
                            rows = slice(128 * jb, 128 * (jb + 1))
                            dsv = ev[rows, cols].astype(F32) * (scr[rows, 128 * t : 128 * (t + 1)] - delta[:, cols])
                            ds[rows, cols] = dsv.astype(BF)
                            if abs(jb - here) <= 1:
                                off = 128 * (here - jb + 1)
                                band[:, off : off + 128] += dsv
                            elif jb > here:
                                after = after + jnp.sum(dsv.reshape(16, 8, 128), axis=0)
                            else:
                                before = before + jnp.sum(dsv.reshape(16, 8, 128), axis=0)
                    red.poll()
                dv = dot(ev[...], dob_scr[...])
                dk = dot(ds[...], qp)
                dqt_scr[HD * hd : HD * (hd + 1), :] = dot_tn(kp, ds[...])[HD * hd : HD * (hd + 1)]
                if hd == 0:
                    dv_scr[...] = dv
                    dk_scr[...] = dk
                else:
                    for i, val in enumerate(
                        (
                            jnp.transpose(dqt_scr[...]),
                            jnp.where(first_half, dk_scr[...], dk),
                            jnp.where(first_half, dv_scr[...], dv),
                        )
                    ):
                        dqkv[:, :, :, HALF * i + 128 * p : HALF * i + 128 * (p + 1)] = val.astype(BF).reshape(
                            4, 2, STRIPE, 128
                        )
                if h + 2 < 6:
                    fetch[h + 2].start()
                for b in range(32):
                    part = jnp.zeros((1, 128), F32)
                    for t in range(3):
                        own = slice(128 * t, 128 * (t + 1))
                        part = part + jnp.sum(jnp.where(bkt[:, own] == b, band[:, own], 0.0), axis=0, keepdims=True)
                    if b == FAR_AFTER:
                        part = part + jnp.sum(after, axis=0, keepdims=True)
                    if b == FAR_BEFORE:
                        part = part + jnp.sum(before, axis=0, keepdims=True)
                    bcount[32 * h + b : 32 * h + b + 1, :] = part

    pl.run_scoped(
        attention,
        pltpu.VMEM((SLOTS, HALF), BF),
        pltpu.VMEM((SLOTS, HALF), BF),
        pltpu.VMEM((SLOTS, HALF), BF),
        pltpu.VMEM((SLOTS, HALF), F32),
        pltpu.VMEM((8, SLOTS), F32),
        pltpu.VMEM((2, SLOTS, SLOTS), BF),
        pltpu.VMEM((SLOTS, SLOTS), BF),
        pltpu.VMEM((2, SLOTS, 256), F32),
        pltpu.VMEM((SLOTS, 128), BF),
        pltpu.VMEM((SLOTS, 128), F32),
        pltpu.VMEM((SLOTS, 128), F32),
        pltpu.VMEM((128, SLOTS), F32),
        pltpu.VMEM((128, 384), F32),
        pltpu.VMEM((128, 384), jnp.int32),
    )

    def tail(n1, wown, dn1):
        loads = [pltpu.make_async_copy(n1_i, n1, a_sem.at[0]), pltpu.make_async_copy(wown_i, wown, a_sem.at[1])]
        for load in loads:
            load.start()
        sent_home(*out_way)
        loads[1].wait()
        pn_send[...] = dot_nt(dqkv[:, 1 - c].reshape(OWN, 3 * HALF), wown[...]).astype(BF).reshape(4, STRIPE, D)
        partial = remote(pn_send, pn_recv, p_send, p_recv, me.core)
        partial.start()
        red.poll()
        loads[0].wait()
        for i in range(3):
            grads = dqkv[:, :, :, HALF * i : HALF * (i + 1)].reshape(SLOTS, HALF)
            unit[i, c, :, :, :, :, 0:HALF] = dot_tn(n1[...], grads).astype(BF).reshape(2, 2, 2, 96, HALF)
            red.poll()
        dn1[...] = dot_nt(dqkv[:, c].reshape(OWN, 3 * HALF), wown[...])
        red.poll()
        partial.wait()
        gain = gain_a[...].astype(F32).reshape(1, D)
        total = jnp.zeros((1, D), F32)
        for i in range(4):
            rows = slice(128 * i, 128 * (i + 1))
            xf = xv[i].astype(F32)
            r1 = lax.rsqrt(jnp.mean(xf * xf, axis=-1, keepdims=True) + EPSILON)
            u1 = xf * r1
            dn = dn1[rows, :] + pn_recv[i].astype(F32)
            total = total + jnp.sum(dn * u1, axis=0, keepdims=True)
            wn = dn * gain
            ig = dh1[rows, :] + r1 * (wn - u1 * jnp.mean(wn * u1, axis=-1, keepdims=True))
            rows_out[i] = ig.astype(BF)
        start_home(*ig_way)
        red.poll()
        for i in range(3):
            stat[0, 3 + i : 4 + i, :] = total[:, 256 * i : 256 * (i + 1)]
        counts = jnp.sum(jnp.transpose(bcount[...]), axis=0, keepdims=True)
        stat[0, pl.ds(6 + c, 1), :] = jnp.concatenate([counts, jnp.zeros((1, 64), F32)], axis=1)
        copies = []
        for i, other in enumerate((me.core, me.xp, me.yp, me.z0p, me.z1p)):
            copy = remote(stat.at[i], stat_in.at[i], s_send.at[i], s_recv.at[i], other)
            copy.start()
            red.poll()
            copy.wait()
            stat[i + 1] = stat[i] + stat_in[i]
        stat_o[...] = stat[5]
        red.poll()
        gd_o[...] = jnp.transpose(dfin[...])
        sent_home(*ig_way)
        got_home(*out_way)
        got_home(*ig_way)

    pl.run_scoped(
        tail,
        pltpu.VMEM((SLOTS, D), BF),
        pltpu.VMEM((D, 3 * HALF), BF),
        pltpu.VMEM((OWN, D), F32),
    )


def run_backward(low, saved, w_out, w_gate, w_up, w_down, norm_attn, norm_ff):
    shapes = (
        ((2, 256, D), BF),
        ((2, 256, D), BF),
        ((96, ZB), F32),
        ((96, ZB), F32),
        ((96, ZB), F32),
        ((96, ZB), F32),
        ((96, 512), F32),
        ((96, 512), F32),
        ((256, ZB), F32),
        ((8, 256), F32),
    )
    dma = pltpu.SemaphoreType.DMA
    wide = [(2, 2, 2, 96, 512), (2, 2, 96, 512), (2, 96, 512), (96, 512), (96, 256)]
    narrow = [(2, 2, 2, 96, HALF), (2, 2, 96, HALF), (2, 96, HALF), (96, HALF), (96, ZB)]
    return pl.pallas_call(
        functools.partial(backward_kernel, low),
        out_shape=[jax.ShapeDtypeStruct(s, t) for s, t in shapes],
        in_specs=[ANY] * 15 + [VM, VM],
        out_specs=[ANY, ANY] + [VM] * 8,
        scratch_shapes=[
            pltpu.VMEM((7, 2, 2, 2, 2, 96, 512), BF),
            *[pltpu.VMEM((6, *s), BF) for s in wide],
            *[pltpu.VMEM((4, *s), BF) for s in narrow],
            pltpu.VMEM((4, 96, ZB), BF),
            pltpu.VMEM((4, STRIPE, D), BF),
            pltpu.VMEM((4, STRIPE, D), BF),
            pltpu.VMEM((2, 4, STRIPE, HALF), BF),
            pltpu.VMEM((2, HALF, D), BF),
            pltpu.VMEM((2, 4, STRIPE, HALF), BF),
            pltpu.VMEM((4, 2, STRIPE, HALF), BF),
            pltpu.VMEM((4, 2, STRIPE, 3 * HALF), BF),
            pltpu.VMEM((4, STRIPE, D), BF),
            pltpu.VMEM((4, STRIPE, D), BF),
            pltpu.VMEM((OWN, D), F32),
            pltpu.VMEM((4, STRIPE, D), BF),
            pltpu.VMEM((ZB, 256), F32),
            pltpu.VMEM((192, 128), F32),
            pltpu.VMEM((6, 8, 256), F32),
            pltpu.VMEM((5, 8, 256), F32),
            dma((10, 5)), dma((10, 5)),
            dma((4,)), dma((2, 2)), dma((4,)), dma((2, 2)),
            dma, dma, dma, dma, dma((5,)), dma((5,)),
            dma((7,)), dma((2, 3, 4)), dma((5,)), dma((6,)),
        ],
        compiler_params=pltpu.CompilerParams(
            collective_id=1, has_side_effects=True, vmem_limit_bytes=63 * 2**20
        ),
        cost_estimate=pl.CostEstimate(flops=30 * 10**9, bytes_accessed=40 * 10**6, transcendentals=10**6),
        name="layer_backward",
    )(*saved, w_out, w_gate, w_up, w_down, norm_attn, norm_ff)


def finish_kernel(
    out_i, ig_i, gq_i, gk_i, gv_i, go_i, gg_i, gu_i, gd_i, stat,
    out_o, ig_o, na_o, gq_o, gk_o, gv_o, go_o, nf_o, gg_o, gu_o, gd_o, table_o,
):
    out_o[...] = out_i[...]
    ig_o[...] = ig_i[...].astype(F32)
    for src, dst in (
        (gq_i, gq_o), (gk_i, gk_o), (gv_i, gv_o), (go_i, go_o), (gg_i, gg_o), (gu_i, gu_o), (gd_i, gd_o)
    ):
        dst[...] = src[...]
    nf_o[...] = jnp.concatenate([stat[i : i + 1, :] for i in range(3)], axis=1).reshape(D)
    na_o[...] = jnp.concatenate([stat[i : i + 1, :] for i in range(3, 6)], axis=1).reshape(D)
    rows = []
    for head in range(H):
        core, local = (head // 3) % 2, head % 3 + 3 * (head // 6)
        rows.append(stat[6 + core : 7 + core, 32 * local : 32 * (local + 1)])
    table_o[...] = jnp.transpose(jnp.concatenate(rows, axis=0))


def run_finish(results):
    output, input_grad, gq, gk, gv, go, gg, gu, gd, stat = results
    outs = [
        (output.shape, BF), (input_grad.shape, F32), ((D,), F32), (gq.shape, F32), (gk.shape, F32), (gv.shape, F32),
        (go.shape, F32), ((D,), F32), (gg.shape, F32), (gu.shape, F32), (gd.shape, F32), ((32, H), F32),
    ]
    return pl.pallas_call(
        finish_kernel,
        out_shape=[jax.ShapeDtypeStruct(s, t) for s, t in outs],
        in_specs=[VM] * 10,
        out_specs=[VM] * 12,
        compiler_params=pltpu.CompilerParams(vmem_limit_bytes=32 * 2**20),
        name="finish",
    )(*results)


def on_device(
    low,
    tokens,
    segment_ids,
    norm_attn,
    w_query,
    w_key,
    w_value,
    w_out,
    norm_ff,
    w_gate,
    w_up,
    w_down,
    bias_table,
    cotangent,
):
    saved = run_forward(low, tokens, cotangent, segment_ids, w_query, w_key, w_value, norm_attn, bias_table)
    output, input_grad, *grads, stat = run_backward(low, saved, w_out, w_gate, w_up, w_down, norm_attn, norm_ff)
    if low > 1:
        groups = [[low * high + i for i in range(low)] for high in range(8)]
        grads = [
            lax.psum_scatter(g, "dp", scatter_dimension=0, axis_index_groups=groups, tiled=True) for g in grads
        ]
        stat = lax.psum(stat, "dp", axis_index_groups=groups)
    return tuple(run_finish([output, input_grad, *grads, stat]))


def solution(mesh):
    rows = P("dp", "blk", None)
    split = P("dp", "blk")
    return jax.shard_map(
        functools.partial(on_device, mesh.shape["dp"] // 8),
        mesh=mesh,
        in_specs=(rows, split, P(), P(), P(), P(), P(), P(), P(), P(), P(), P(), rows),
        out_specs=(rows, rows, P(), split, split, split, split, P(), split, split, split, P()),
        check_vma=False,
    )
```

```python
import functools

import jax
import jax.numpy as jnp
from jax import lax
from jax.experimental import pallas as pl
from jax.experimental.pallas import tpu as pltpu
from jax.sharding import PartitionSpec as P

H = 12
HD = 64
EPSILON = 1e-06
MASKED = -1e30
LIMITS = (12, 16, 23, 32, 46, 64, 91)
FAR_BEFORE = 15
FAR_AFTER = 31

MESH = pl.DeviceIdType.MESH
BF = jnp.bfloat16
F32 = jnp.float32
ANY = pl.BlockSpec(memory_space=pl.ANY)
VM = pl.BlockSpec(memory_space=pltpu.VMEM)

D = 768
HALF = 384
ZB = 192
SLOTS = 1024
STRIPE = 128
OWN = 512


def dot(a, b):
    return lax.dot_general(a, b, (((1,), (0,)), ((), ())), preferred_element_type=F32)


def dot_nt(a, b):
    return lax.dot_general(a, b, (((1,), (1,)), ((), ())), preferred_element_type=F32)


def dot_tn(a, b):
    return lax.dot_general(a, b, (((0,), (0,)), ((), ())), preferred_element_type=F32)


class Place:
    def __init__(self, low):
        self.low = low
        self.dp = lax.axis_index("dp")
        self.z = lax.axis_index("blk")
        high = self.dp // low
        self.c = high % 2
        self.x = (high // 2) % 2
        self.y = high // 4
        self.base = self.dp - self.c * low
        self.z0 = self.z % 2
        self.z1 = self.z // 2
        self.core = (self.dp + low * (1 - 2 * self.c), self.z)
        self.xp = (self.dp + 2 * low * (1 - 2 * self.x), self.z)
        self.yp = (self.dp + 4 * low * (1 - 2 * self.y), self.z)
        self.z0p = (self.dp, self.z + 1 - 2 * self.z0)
        self.z1p = (self.dp, self.z + 2 - 4 * self.z1)

    def group(self):
        found = []
        for dc in range(2):
            for dz in range(4):
                if dc or dz:
                    found.append((self.base + ((self.c + dc) % 2) * self.low, (self.z + dz) % 4))
        return found

    def near(self, k):
        fold = jnp.where(self.z < 2, self.z, 3 - self.z)
        step = (k + fold * (1 - 2 * k)) if k < 2 else k
        return jnp.where(self.z < 2, step, 3 - step)


def greet(others):
    barrier = pltpu.get_barrier_semaphore()
    for other in others:
        pl.semaphore_signal(barrier, inc=1, device_id=other, device_id_type=MESH)
    pl.semaphore_wait(barrier, len(others))


def remote(src, dst, send, recv, device):
    return pltpu.make_async_remote_copy(
        src_ref=src, dst_ref=dst, send_sem=send, recv_sem=recv, device_id=device, device_id_type=MESH
    )


def bucket_tile():
    key = lax.broadcasted_iota(jnp.int32, (128, 384), 0)
    query = lax.broadcasted_iota(jnp.int32, (128, 384), 1)
    rel = key - query + 128
    dist = jnp.abs(rel)
    beyond = jnp.full((128, 384), 8, jnp.int32)
    for threshold in LIMITS:
        beyond = beyond + (dist >= threshold).astype(jnp.int32)
    return jnp.where(dist < 8, dist, beyond) + jnp.where(rel > 0, 16, 0)


def head_of(place, local):
    return 3 * place.c + local % 3 + 6 * (local // 3)


def lane_mask(head_in_pair):
    lane = lax.broadcasted_iota(jnp.int32, (1, 128), 1)
    inside = (lane < HD) if head_in_pair == 0 else (lane >= HD)
    return inside.astype(F32).astype(BF)


GELU_SCALE = 0.7978845608028654
GELU_CUBE = 0.044715
GROUPS = ("gate0", "up0", "gate1", "up1", "down0", "down1", "out", "query", "key", "value")
WIDE = 6
SLOT = (0, 1, 2, 3, 4, 5, 6, 0, 1, 2)
PLAN = (
    (0,), (1,), (), (), (), (0,), (1,), (), (), (), (2,), (3,), (), (4, 5), (), (2,), (0, 3, 1, 4), (5,), (6,), (),
    (), (), (6,), (0,), (), (), (), (), (2,), (), (), (), (), (), (), (1,), (0,), (3,), (), (), (), (), (), (),
    (1, 7), (0, 8), (4, 9), (5, 7, 8), (1, 9), (2, 6), (4, 3), (2,), (5, 7), (),
    (4, 8, 3, 9, 2, 7, 5, 6, 9, 4, 8, 3, 7, 5, 6, 8, 9, 7, 6, 8, 9),
)


class Reduction:
    def __init__(self, me, unit, wide, narrow, stage, send, recv, finish):
        self.me, self.unit, self.wide, self.narrow, self.stage = me, unit, wide, narrow, stage
        self.send, self.recv, self.finish = send, recv, finish
        self.step = [0] * len(GROUPS)
        self.polls = 0

    def buffers(self, u):
        if u < WIDE:
            return [ref.at[u] for ref in self.wide]
        return [ref.at[u - WIDE] for ref in self.narrow]

    def copy(self, u, k):
        me = self.me
        r0, r1, r2, r3, r4 = self.buffers(u)
        cols = 512 if u < WIDE else HALF
        unit = self.unit.at[SLOT[u]]
        x_first = u % 2 == 0
        if k == 0 and u <= WIDE:
            src, dst, device = unit.at[:, :, :, 1 - me.c, :, pl.ds(0, cols)], r0, me.core
        elif k == 0:
            src, dst, device = unit.at[me.c, :, :, 1 - me.c, :, pl.ds(0, cols)], r0.at[me.c], me.core
        elif k == 1 and x_first:
            src, dst, device = r0.at[:, :, 1 - me.x], r1, me.xp
        elif k == 1:
            src, dst, device = r0.at[:, 1 - me.y], r1, me.yp
        elif k == 2 and x_first:
            src, dst, device = r1.at[:, 1 - me.y], r2, me.yp
        elif k == 2:
            src, dst, device = r1.at[:, 1 - me.x], r2, me.xp
        elif k == 3:
            src, dst, device = r2.at[1 - me.z0], r3, me.z0p
        elif u < WIDE:
            there = pl.ds(pl.multiple_of(256 * (1 - me.z1), 256), 256)
            src, dst, device = r3.at[:, there], r4, me.z1p
        else:
            src, dst, device = self.stage.at[u - WIDE], r4, me.z1p
        return remote(src, dst, self.send.at[u, k], self.recv.at[u, k], device)

    def poll(self):
        for u in PLAN[self.polls]:
            self.advance_one(u)
        self.polls += 1

    def advance_one(self, u):
        me = self.me
        k = self.step[u]
        r0, r1, r2, r3, r4 = self.buffers(u)
        cols = 512 if u < WIDE else HALF
        unit = self.unit.at[SLOT[u]]
        x_first = u % 2 == 0
        if k > 0:
            self.copy(u, k - 1).wait()

        def add(into, other):
            into[...] = (into[...].astype(F32) + other[...].astype(F32)).astype(BF)

        if k == 1 and u <= WIDE:

            @pl.loop(0, 8)
            def _(i):
                a, y, x = i // 4, (i // 2) % 2, i % 2
                add(r0.at[a, y, x], unit.at[a, y, x, me.c, :, pl.ds(0, cols)])

        elif k == 1:

            @pl.loop(0, 4)
            def _(i):
                r0[me.c, i // 2, i % 2] = unit[me.c, i // 2, i % 2, me.c, :, pl.ds(0, cols)]

        elif k == 2:

            @pl.loop(0, 4)
            def _(i):
                a, b = i // 2, i % 2
                add(r1.at[a, b], r0.at[a, b, me.x] if x_first else r0.at[a, me.y, b])

        elif k == 3:

            @pl.loop(0, 2)
            def _(i):
                add(r2.at[i], r1.at[i, me.y if x_first else me.x])

        elif k == 4:
            add(r3, r2.at[me.z0])
            if u >= WIDE:
                self.stage[u - WIDE] = jnp.where(me.z1 == 0, r3[:, ZB:], r3[:, :ZB])
        elif k == 5:
            if u < WIDE:
                own = r3[:, pl.ds(pl.multiple_of(256 * me.z1, 256), 256)]
            else:
                own = jnp.where(me.z1 == 0, r3[:, :ZB], r3[:, ZB:])
            self.finish(GROUPS[u], own.astype(F32) + r4[...].astype(F32))
        if k < 5:
            self.copy(u, k).start()
        self.step[u] = k + 1


def layer_kernel(
    low,
    tok, seg, gain_a, wq, wk, wv, w_out, gain_f, w_gate, w_up, w_down, table_i, cot,
    out_o, ig_o, gq_o, gk_o, gv_o, go_o, gg_o, gu_o, gd_o, stat_o, e_o, wown_o,
    table, unit, a0, a1, a2, a3, a4, b0, b1, b2, b3, b4, bstage,
    xrow, segb, n1, q, k, v, o, linv, bkt,
    gv, obf, wout, dobv, dobrow, pn_recv, dh1, rows_out, bcount, stat, stat_in,
    x_send, x_recv, f_send, f_recv, c_send, c_recv, g_send, g_recv, o_send, o_recv,
    red_send, red_recv, t_send, t_recv, i_send, i_recv, d_send, d_recv, p_send, p_recv, s_send, s_recv,
    l_sem, w_sem, e_sem,
):
    me = Place(low)
    c, z = me.c, me.z

    def finish(name, total):
        if name[-1] in "01":
            kind, part = name[:-1], int(name[-1])
            if kind == "down":
                gd_o[96 * part : 96 * (part + 1), :] = total
            else:
                {"gate": gg_o, "up": gu_o}[kind][:, 256 * part : 256 * (part + 1)] = total
        else:
            {"out": go_o, "query": gq_o, "key": gk_o, "value": gv_o}[name][...] = total

    red = Reduction(me, unit, (a0, a1, a2, a3, a4), (b0, b1, b2, b3, b4), bstage, red_send, red_recv, finish)

    def targets():
        for r in range(2):
            for kk in range(2):
                yield r, kk, (me.base + kk * low, 2 * c + r), jnp.logical_and(2 * c + r == z, kk == c)

    def home(zz, send_sem, recv_sem, dest):
        dst = dest.at[me.z0, pl.ds(pl.multiple_of(STRIPE * c, STRIPE), STRIPE)]
        recv = recv_sem.at[me.z0, c]
        here = jnp.logical_and(zz == z, me.z1 == c)
        return here, rows_out.at[zz], dst, send_sem.at[zz], recv, (me.base + me.z1 * low, zz)

    def start_home(*where):
        for zz in range(4):
            here, src, dst, send, recv, device = home(zz, *where)

            @pl.when(here)
            def _():
                pltpu.make_async_copy(src, dst, send).start()

            @pl.when(jnp.logical_not(here))
            def _():
                remote(src, dst, send, recv, device).start()

    def sent_home(*where):
        for zz in range(4):
            here, src, dst, send, recv, device = home(zz, *where)

            @pl.when(here)
            def _():
                pltpu.make_async_copy(src, dst, send).wait()

            @pl.when(jnp.logical_not(here))
            def _():
                remote(src, dst, send, recv, device).wait_send()

    def got_home(send_sem, recv_sem, dest):
        for r in range(2):
            for kk in range(2):
                part = dest.at[r, pl.ds(STRIPE * kk, STRIPE)]

                @pl.when(jnp.logical_not(jnp.logical_and(2 * c + r == z, kk == c)))
                def _():
                    remote(part, part, send_sem.at[0], recv_sem.at[r, kk], me.core).wait_recv()

    to_partner = remote(dobv.at[1 - c], dobrow.at[:, c], d_send, d_recv, me.core)
    out_way = (t_send, t_recv, out_o)
    ig_way = (i_send, i_recv, ig_o)

    def attend(wg, wu, wd, wown, band, segcol, segrow, s_scr, e_scr, ot_scr, ob):
        raw = (wd.at[0, pl.ds(0, D)], wd.at[1, pl.ds(0, D)], wu.at[0, :, pl.ds(0, D)])
        loads = [pltpu.make_async_copy(w, dst, l_sem.at[i]) for i, (w, dst) in enumerate(zip((wq, wk, wv), raw))]
        table_load = pltpu.make_async_copy(table_i, table, l_sem.at[3])
        for load in loads + [table_load]:
            load.start()
        greet(me.group() + [me.xp, me.yp])

        for r, kk, device, here in targets():
            src = tok.at[r, pl.ds(STRIPE * kk, STRIPE)]
            dst = xrow.at[z, kk]
            far = remote(src, dst, x_send.at[r, kk], x_recv.at[z], device)
            near = pltpu.make_async_copy(src, dst, x_recv.at[z])
            sfar = remote(seg, segb.at[z], g_send.at[r, kk], g_recv.at[z], device)
            snear = pltpu.make_async_copy(seg, segb.at[z], g_recv.at[z])

            @pl.when(here)
            def _():
                near.start()
                snear.start()

            @pl.when(jnp.logical_not(here))
            def _():
                far.start()
                sfar.start()

        for i in range(3):
            loads[i].wait()
            w = raw[i]
            lo = jnp.concatenate([w[:, 0:ZB], w[:, 2 * ZB : 3 * ZB]], axis=1)
            hi = jnp.concatenate([w[:, ZB : 2 * ZB], w[:, 3 * ZB : 4 * ZB]], axis=1)
            wown[:, HALF * i : HALF * (i + 1)] = jnp.where(c == 0, lo, hi)
        bkt[...] = bucket_tile()
        table_load.wait()

        def make_band(hl, _):
            head = head_of(me, hl)
            for t in range(3):
                which = bkt[:, 128 * t : 128 * (t + 1)]
                total = jnp.zeros((128, 128), F32)
                for b in range(32):
                    total = jnp.where(which == b, table[head, b], total)
                band[hl, :, 128 * t : 128 * (t + 1)] = total
            return 0

        lax.fori_loop(0, 6, make_band, 0)

        for load in weight_loads(wg, wu, wd):
            load.start()
        keep = pltpu.make_async_copy(wown, wown_o, l_sem.at[0])
        keep.start()

        gain_f = gain_a[...].astype(F32).reshape(1, D)
        forwards = []
        for step in range(4):
            zz = me.near(step)
            own = xrow.at[zz, c]
            remote(own, own, x_send.at[0, 0], x_recv.at[zz], me.core).wait_recv()
            fwd = remote(own, own, f_send.at[step], f_recv.at[zz], me.core)
            fwd.start()
            forwards.append(fwd)
        for step in range(4):
            zz = me.near(step)
            other = xrow.at[zz, 1 - c]
            remote(other, other, f_send.at[step], f_recv.at[zz], me.core).wait_recv()
            xf = xrow[zz].reshape(256, D).astype(F32)
            r1 = lax.rsqrt(jnp.mean(xf * xf, axis=-1, keepdims=True) + EPSILON)
            nb = (xf * r1 * gain_f).astype(BF)
            rows = pl.ds(pl.multiple_of(zz * 256, 256), 256)
            n1[rows, :] = nb
            for i, dest in enumerate((q, k, v)):
                dest[rows, :] = dot(nb, wown[:, HALF * i : HALF * (i + 1)]).astype(BF)

        for r, kk, device, here in targets():
            src = cot.at[r, pl.ds(STRIPE * kk, STRIPE)]
            dst = gv.at[z]
            far = remote(src, dst, c_send.at[r, kk], c_recv.at[z], device)
            near = pltpu.make_async_copy(src, dst, c_recv.at[z])

            @pl.when(here)
            def _():
                near.start()

            @pl.when(jnp.logical_not(here))
            def _():
                far.start()

        for zz in range(4):
            blk_seg = segb.at[zz]
            remote(blk_seg, blk_seg, g_send.at[0, 0], g_recv.at[zz], me.core).wait_recv()
            segrow[:, 256 * zz : 256 * (zz + 1)] = segb[zz, pl.ds(z % 2, 1), :].astype(F32)
        segcol[...] = jnp.transpose(jnp.broadcast_to(segrow[...], (128, SLOTS)))
        linv[...] = jnp.zeros((8, SLOTS), F32)

        def pair_step(p, _):
            lanes = pl.ds(pl.multiple_of(p * 128, 128), 128)
            kp, vp = k[:, lanes], v[:, lanes]
            for hd in range(2):
                mask = lane_mask(hd)
                vm = vp * mask + (1 - mask)
                hl = 2 * p + hd
                head = head_of(me, hl)
                after, before = table[head, FAR_AFTER], table[head, FAR_BEFORE]

                @pl.when(p > 0)
                def _():
                    pltpu.make_async_copy(e_scr.at[hd], e_o.at[hl], e_sem.at[hd]).wait()

                for ib in range(4):
                    qm = q[256 * ib : 256 * (ib + 1), lanes] * mask
                    scr = s_scr.at[ib % 2]
                    scr[...] = dot_nt(kp, qm)
                    for t in range(2):
                        here = 2 * ib + t
                        cols = slice(128 * t, 128 * (t + 1))
                        seg_q = segrow[:, 256 * ib + 128 * t : 256 * ib + 128 * (t + 1)]
                        top = jnp.full((8, 128), MASKED, F32)
                        for jb in range(8):
                            rows = slice(128 * jb, 128 * (jb + 1))
                            tile = scr[rows, cols]
                            if abs(jb - here) <= 1:
                                off = 128 * (here - jb + 1)
                                tile = tile + band[hl, :, off : off + 128]
                            else:
                                tile = tile + (after if jb > here else before)
                            tile = jnp.where(segcol[rows, :] == seg_q, tile, MASKED)
                            scr[rows, cols] = tile
                            top = jnp.maximum(top, jnp.max(tile.reshape(16, 8, 128), axis=0))
                        top = jnp.max(top, axis=0, keepdims=True)
                        for jb in range(8):
                            rows = slice(128 * jb, 128 * (jb + 1))
                            weight = jnp.exp(scr[rows, cols] - top)
                            e_scr[hd, rows, 256 * ib + 128 * t : 256 * ib + 128 * (t + 1)] = weight.astype(BF)
                both = dot_tn(vm, e_scr[hd])
                data, sums = (both[0:HD], both[HD:128]) if hd == 0 else (both[HD:128], both[0:HD])
                inverse = 1.0 / sums
                ot_scr[HD * hd : HD * (hd + 1), :] = data * inverse
                linv[pl.ds(hl, 1), :] = inverse[0:1]
                pltpu.make_async_copy(e_scr.at[hd], e_o.at[hl], e_sem.at[hd]).start()
            mixed = jnp.transpose(ot_scr[...])
            o[:, lanes] = mixed
            ob[:, :, :, lanes] = mixed.astype(BF).reshape(4, 2, STRIPE, 128)
            mine = ob.at[:, 1 - c, :, lanes]
            remote(mine, obf.at[c, :, :, lanes], o_send.at[p], o_recv.at[p], me.core).start()
            return 0

        lax.fori_loop(0, 3, pair_step, 0)

        for hd in range(2):
            pltpu.make_async_copy(e_scr.at[hd], e_o.at[4 + hd], e_sem.at[hd]).wait()
        obf[c] = ob[:, c]
        for p in range(3):
            lanes = slice(128 * p, 128 * (p + 1))
            mine = ob.at[:, 1 - c, :, lanes]
            there = remote(mine, obf.at[1 - c, :, :, lanes], o_send.at[p], o_recv.at[p], me.core)
            there.wait_send()
            there.wait_recv()
        keep.wait()
        for fwd in forwards:
            fwd.wait_send()

    def weight_loads(wg, wu, wd):
        loads = []
        for i in range(4):
            loads.append(
                pltpu.make_async_copy(
                    w_out.at[pl.ds(ZB * i, ZB)], wout.at[i % 2, pl.ds(ZB * (i // 2), ZB)], l_sem.at[4 + i]
                )
            )
        for f in range(2):
            for which, (src, dst) in enumerate(((w_gate, wg), (w_up, wu), (w_down, wd))):
                for zz in range(4):
                    far = pl.ds(512 * zz + 256 * f, 256)
                    own = pl.ds(256 * zz, 256)
                    sem = w_sem.at[f, which, zz]
                    if which < 2:
                        loads.append(pltpu.make_async_copy(src.at[:, far], dst.at[f, :, own], sem))
                    else:
                        loads.append(pltpu.make_async_copy(src.at[far], dst.at[f, own], sem))
        return loads

    def feed_forward(wg, wu, wd, n2, h1, acc, hid, dga, dup):
        loads = weight_loads(wg, wu, wd)
        for load in loads[:4]:
            load.wait()
        gain = gain_f[...].astype(F32).reshape(1, D)
        for i in range(2):
            rows = slice(256 * i, 256 * (i + 1))
            parts = slice(2 * i, 2 * (i + 1))
            h = xrow[parts, c].reshape(256, D).astype(F32)
            h = h + dot(obf[0, parts].reshape(256, HALF), wout[0]) + dot(obf[1, parts].reshape(256, HALF), wout[1])
            h1[rows, :] = h
            r2 = lax.rsqrt(jnp.mean(h * h, axis=-1, keepdims=True) + EPSILON)
            n2[rows, :] = (h * r2 * gain).astype(BF)
        for zz in range(4):
            got = gv.at[zz]
            remote(got, got, c_send.at[0, 0], c_recv.at[zz], me.core).wait_recv()
        g = gv[...].reshape(OWN, D)
        for f in range(2):
            for load in loads[4 + 12 * f : 16 + 12 * f]:
                load.wait()
            for i in range(2):
                rows = slice(256 * i, 256 * (i + 1))
                gate = dot(n2[rows, :], wg[f])
                up = dot(n2[rows, :], wu[f])
                dhid = dot_nt(gv[2 * i : 2 * (i + 1)].reshape(256, D), wd[f])
                square = gate * gate
                th = jnp.tanh(GELU_SCALE * gate * (1.0 + GELU_CUBE * square))
                half = 0.5 + 0.5 * th
                gelu = gate * half
                slope = half + 0.5 * GELU_SCALE * gate * (1.0 - th * th) * (1.0 + 3.0 * GELU_CUBE * square)
                hid[rows, :] = (gelu * up).astype(BF)
                dup[rows, :] = (dhid * gelu).astype(BF)
                dga[rows, :] = (dhid * up * slope).astype(BF)
                if f == 1:
                    red.poll()
            if f == 1:
                for i in range(4):
                    rows = slice(128 * i, 128 * (i + 1))
                    rows_out[i] = (h1[rows, :] + acc[rows, :] + dot(hid[rows, :], wd[f])).astype(BF)
                start_home(*out_way)
                red.poll()
            for which, grads in enumerate((dga, dup)):
                for zz in range(4):
                    piece = dot_tn(n2[...], grads[:, 256 * zz : 256 * (zz + 1)]).astype(BF)
                    unit[2 * f + which, zz % 2, :, :, :, :, 256 * (zz // 2) : 256 * (zz // 2 + 1)] = piece.reshape(
                        2, 2, 2, 96, 256
                    )
                red.poll()
            for zz in range(4):
                piece = dot_tn(g, hid[:, 256 * zz : 256 * (zz + 1)]).astype(BF)
                for to in range(4):
                    for part in range(2):
                        row = ZB * to + 96 * part
                        unit[4 + part, to % 2, zz // 2, zz % 2, f, :, 256 * (to // 2) : 256 * (to // 2 + 1)] = piece[
                            row : row + 96
                        ]
                if zz % 2:
                    red.poll()
            if f == 0:
                acc[...] = dot(hid[...], wd[f])
                red.poll()
                dh1[...] = dot_nt(dga[...], wg[f])
            else:
                dh1[...] += dot_nt(dga[...], wg[f])
            red.poll()
            dh1[...] += dot_nt(dup[...], wu[f])
            red.poll()
        total = jnp.zeros((1, D), F32)
        for i in range(4):
            rows = slice(128 * i, 128 * (i + 1))
            h = h1[rows, :]
            r2 = lax.rsqrt(jnp.mean(h * h, axis=-1, keepdims=True) + EPSILON)
            u2 = h * r2
            dn2 = dh1[rows, :]
            total = total + jnp.sum(dn2 * u2, axis=0, keepdims=True)
            wn = dn2 * gain
            dh = gv[i].astype(F32) + r2 * (wn - u2 * jnp.mean(wn * u2, axis=-1, keepdims=True))
            dh1[rows, :] = dh
            n2[rows, :] = dh.astype(BF)
        stat[...] = jnp.zeros((6, 8, 256), F32)
        for i in range(3):
            stat[0, i : i + 1, :] = total[:, 256 * i : 256 * (i + 1)]
        red.poll()
        dab = n2[...]
        for cp in range(2):
            dobv[cp] = dot_nt(dab, wout[cp]).astype(BF).reshape(4, STRIPE, HALF)
        to_partner.start()
        dobrow[:, c] = dobv[c]
        red.poll()
        for a in range(2):
            dz = jnp.concatenate([dab[:, ZB * a : ZB * (a + 1)], dab[:, ZB * (a + 2) : ZB * (a + 3)]], axis=1)
            for cp in range(2):
                piece = dot_tn(obf[cp].reshape(OWN, HALF), dz).astype(BF)
                for yy in range(2):
                    for cc in range(2):
                        row = 96 * (2 * yy + cc)
                        unit[6, a, yy, cp, cc, :, 0:HALF] = piece[row : row + 96]
        red.poll()

    def attention(dqkv, e, ds, dp_scr, dob_scr, dv_scr, dk_scr, dqt_scr, band):
        fetch = [pltpu.make_async_copy(e_o.at[h], e.at[h % 2], e_sem.at[2 + h]) for h in range(6)]
        fetch[0].start()
        fetch[1].start()
        to_partner.wait()
        first_half = lax.broadcasted_iota(jnp.int32, (1, 128), 1) < HD
        for p in range(3):
            lanes = slice(128 * p, 128 * (p + 1))
            kp, vp, qp = k[:, lanes], v[:, lanes], q[:, lanes]
            inverse = jnp.concatenate(
                [jnp.broadcast_to(linv[2 * p + hd : 2 * p + hd + 1, :], (HD, SLOTS)) for hd in range(2)], axis=0
            )
            scaled = dobrow[:, :, :, lanes].reshape(SLOTS, 128).astype(F32) * jnp.transpose(inverse)
            dob_scr[...] = scaled.astype(BF)
            product = jnp.transpose(scaled * o[:, lanes])
            for hd in range(2):
                h = 2 * p + hd
                delta = jnp.sum(product[HD * hd : HD * (hd + 1)], axis=0, keepdims=True)
                vm = vp * lane_mask(hd)
                fetch[h].wait()
                ev = e.at[hd]
                band[...] = jnp.zeros((128, 384), F32)
                after = jnp.zeros((8, 128), F32)
                before = jnp.zeros((8, 128), F32)
                for ib in range(4):
                    scr = dp_scr.at[ib % 2]
                    scr[...] = dot_nt(vm, dob_scr[256 * ib : 256 * (ib + 1), :])
                    for t in range(2):
                        here = 2 * ib + t
                        cols = slice(128 * here, 128 * (here + 1))
                        for jb in range(8):
                            rows = slice(128 * jb, 128 * (jb + 1))
                            dsv = ev[rows, cols].astype(F32) * (scr[rows, 128 * t : 128 * (t + 1)] - delta[:, cols])
                            ds[rows, cols] = dsv.astype(BF)
                            if abs(jb - here) <= 1:
                                off = 128 * (here - jb + 1)
                                band[:, off : off + 128] += dsv
                            elif jb > here:
                                after = after + jnp.sum(dsv.reshape(16, 8, 128), axis=0)
                            else:
                                before = before + jnp.sum(dsv.reshape(16, 8, 128), axis=0)
                    red.poll()
                dv = dot(ev[...], dob_scr[...])
                dk = dot(ds[...], qp)
                dqt_scr[HD * hd : HD * (hd + 1), :] = dot_tn(kp, ds[...])[HD * hd : HD * (hd + 1)]
                if hd == 0:
                    dv_scr[...] = dv
                    dk_scr[...] = dk
                else:
                    for i, val in enumerate(
                        (
                            jnp.transpose(dqt_scr[...]),
                            jnp.where(first_half, dk_scr[...], dk),
                            jnp.where(first_half, dv_scr[...], dv),
                        )
                    ):
                        dqkv[:, :, :, HALF * i + 128 * p : HALF * i + 128 * (p + 1)] = val.astype(BF).reshape(
                            4, 2, STRIPE, 128
                        )
                if h + 2 < 6:
                    fetch[h + 2].start()
                for b in range(32):
                    part = jnp.zeros((1, 128), F32)
                    for t in range(3):
                        own = slice(128 * t, 128 * (t + 1))
                        part = part + jnp.sum(jnp.where(bkt[:, own] == b, band[:, own], 0.0), axis=0, keepdims=True)
                    if b == FAR_AFTER:
                        part = part + jnp.sum(after, axis=0, keepdims=True)
                    if b == FAR_BEFORE:
                        part = part + jnp.sum(before, axis=0, keepdims=True)
                    bcount[32 * h + b : 32 * h + b + 1, :] = part

    def tail(dqkv, wown, dn1, pn_send):
        load = pltpu.make_async_copy(wown_o, wown, l_sem.at[0])
        load.start()
        sent_home(*out_way)
        load.wait()
        pn_send[...] = dot_nt(dqkv[:, 1 - c].reshape(OWN, 3 * HALF), wown[...]).astype(BF).reshape(4, STRIPE, D)
        partial = remote(pn_send, pn_recv, p_send, p_recv, me.core)
        partial.start()
        red.poll()
        for i in range(3):
            grads = dqkv[:, :, :, HALF * i : HALF * (i + 1)].reshape(SLOTS, HALF)
            unit[i, c, :, :, :, :, 0:HALF] = dot_tn(n1[...], grads).astype(BF).reshape(2, 2, 2, 96, HALF)
            red.poll()
        dn1[...] = dot_nt(dqkv[:, c].reshape(OWN, 3 * HALF), wown[...])
        red.poll()
        partial.wait()
        gain = gain_a[...].astype(F32).reshape(1, D)
        total = jnp.zeros((1, D), F32)
        for i in range(4):
            rows = slice(128 * i, 128 * (i + 1))
            xf = xrow[i, c].astype(F32)
            r1 = lax.rsqrt(jnp.mean(xf * xf, axis=-1, keepdims=True) + EPSILON)
            u1 = xf * r1
            dn = dn1[rows, :] + pn_recv[i].astype(F32)
            total = total + jnp.sum(dn * u1, axis=0, keepdims=True)
            wn = dn * gain
            ig = dh1[rows, :] + r1 * (wn - u1 * jnp.mean(wn * u1, axis=-1, keepdims=True))
            rows_out[i] = ig.astype(BF)
        start_home(*ig_way)
        red.poll()
        for i in range(3):
            stat[0, 3 + i : 4 + i, :] = total[:, 256 * i : 256 * (i + 1)]
        counts = jnp.sum(jnp.transpose(bcount[...]), axis=0, keepdims=True)
        stat[0, pl.ds(6 + c, 1), :] = jnp.concatenate([counts, jnp.zeros((1, 64), F32)], axis=1)
        copies = []
        for i, other in enumerate((me.core, me.xp, me.yp, me.z0p, me.z1p)):
            copy = remote(stat.at[i], stat_in.at[i], s_send.at[i], s_recv.at[i], other)
            copy.start()
            red.poll()
            copy.wait()
            stat[i + 1] = stat[i] + stat_in[i]
        stat_o[...] = stat[5]
        red.poll()
        sent_home(*ig_way)
        got_home(*out_way)
        got_home(*ig_way)
        for r, kk, device, here in targets():

            @pl.when(jnp.logical_not(here))
            def _():
                src = tok.at[r, pl.ds(STRIPE * kk, STRIPE)]
                remote(src, xrow.at[z, kk], x_send.at[r, kk], x_recv.at[z], device).wait_send()
                remote(seg, segb.at[z], g_send.at[r, kk], g_recv.at[z], device).wait_send()
                srcc = cot.at[r, pl.ds(STRIPE * kk, STRIPE)]
                remote(srcc, gv.at[z], c_send.at[r, kk], c_recv.at[z], device).wait_send()

    def first_half(wg, wu, wd):
        pl.run_scoped(
            functools.partial(attend, wg, wu, wd),
            pltpu.VMEM((D, 3 * HALF), BF),
            pltpu.VMEM((6, 128, 384), F32),
            pltpu.VMEM((SLOTS, 128), F32),
            pltpu.VMEM((1, SLOTS), F32),
            pltpu.VMEM((2, SLOTS, 256), F32),
            pltpu.VMEM((2, SLOTS, SLOTS), BF),
            pltpu.VMEM((128, SLOTS), F32),
            pltpu.VMEM((4, 2, STRIPE, HALF), BF),
        )
        pl.run_scoped(
            functools.partial(feed_forward, wg, wu, wd),
            pltpu.VMEM((OWN, D), BF),
            pltpu.VMEM((OWN, D), F32),
            pltpu.VMEM((OWN, D), F32),
            pltpu.VMEM((OWN, 1024), BF),
            pltpu.VMEM((OWN, 1024), BF),
            pltpu.VMEM((OWN, 1024), BF),
        )

    def second_half(dqkv):
        pl.run_scoped(
            functools.partial(attention, dqkv),
            pltpu.VMEM((2, SLOTS, SLOTS), BF),
            pltpu.VMEM((SLOTS, SLOTS), BF),
            pltpu.VMEM((2, SLOTS, 256), F32),
            pltpu.VMEM((SLOTS, 128), BF),
            pltpu.VMEM((SLOTS, 128), F32),
            pltpu.VMEM((SLOTS, 128), F32),
            pltpu.VMEM((128, SLOTS), F32),
            pltpu.VMEM((128, 384), F32),
        )
        pl.run_scoped(
            functools.partial(tail, dqkv),
            pltpu.VMEM((D, 3 * HALF), BF),
            pltpu.VMEM((OWN, D), F32),
            pltpu.VMEM((4, STRIPE, D), BF),
        )

    pl.run_scoped(first_half, pltpu.VMEM((2, D, 1024), BF), pltpu.VMEM((2, D, 1024), BF), pltpu.VMEM((2, 1024, D), BF))
    pl.run_scoped(second_half, pltpu.VMEM((4, 2, STRIPE, 3 * HALF), BF))


def run_layer(low, *arrays):
    shapes = (
        ((2, 256, D), BF),
        ((2, 256, D), BF),
        ((96, ZB), F32),
        ((96, ZB), F32),
        ((96, ZB), F32),
        ((96, ZB), F32),
        ((96, 512), F32),
        ((96, 512), F32),
        ((ZB, 256), F32),
        ((8, 256), F32),
        ((6, SLOTS, SLOTS), BF),
        ((D, 3 * HALF), BF),
    )
    dma = pltpu.SemaphoreType.DMA
    wide = [(2, 2, 2, 96, 512), (2, 2, 96, 512), (2, 96, 512), (96, 512), (96, 256)]
    narrow = [(2, 2, 2, 96, HALF), (2, 2, 96, HALF), (2, 96, HALF), (96, HALF), (96, ZB)]
    specs = [ANY] * 13
    specs[2] = specs[7] = VM
    return pl.pallas_call(
        functools.partial(layer_kernel, low),
        out_shape=[jax.ShapeDtypeStruct(s, t) for s, t in shapes],
        in_specs=specs,
        out_specs=[ANY, ANY] + [VM] * 8 + [ANY, ANY],
        scratch_shapes=[
            pltpu.SMEM((H, 32), F32),
            pltpu.VMEM((7, 2, 2, 2, 2, 96, 512), BF),
            *[pltpu.VMEM((6, *s), BF) for s in wide],
            *[pltpu.VMEM((4, *s), BF) for s in narrow],
            pltpu.VMEM((4, 96, ZB), BF),
            pltpu.VMEM((4, 2, STRIPE, D), BF),
            pltpu.VMEM((4, 2, 256), jnp.int32),
            pltpu.VMEM((SLOTS, D), BF),
            pltpu.VMEM((SLOTS, HALF), BF),
            pltpu.VMEM((SLOTS, HALF), BF),
            pltpu.VMEM((SLOTS, HALF), BF),
            pltpu.VMEM((SLOTS, HALF), F32),
            pltpu.VMEM((8, SLOTS), F32),
            pltpu.VMEM((128, 384), jnp.int32),
            pltpu.VMEM((4, STRIPE, D), BF),
            pltpu.VMEM((2, 4, STRIPE, HALF), BF),
            pltpu.VMEM((2, HALF, D), BF),
            pltpu.VMEM((2, 4, STRIPE, HALF), BF),
            pltpu.VMEM((4, 2, STRIPE, HALF), BF),
            pltpu.VMEM((4, STRIPE, D), BF),
            pltpu.VMEM((OWN, D), F32),
            pltpu.VMEM((4, STRIPE, D), BF),
            pltpu.VMEM((192, 128), F32),
            pltpu.VMEM((6, 8, 256), F32),
            pltpu.VMEM((5, 8, 256), F32),
            dma((2, 2)), dma((4,)), dma((4,)), dma((4,)), dma((2, 2)), dma((4,)),
            dma((2, 2)), dma((4,)), dma((3,)), dma((3,)),
            dma((10, 5)), dma((10, 5)),
            dma((4,)), dma((2, 2)), dma((4,)), dma((2, 2)),
            dma, dma, dma, dma, dma((5,)), dma((5,)),
            dma((8,)), dma((2, 3, 4)), dma((8,)),
        ],
        compiler_params=pltpu.CompilerParams(
            collective_id=0, has_side_effects=True, vmem_limit_bytes=63 * 2**20
        ),
        cost_estimate=pl.CostEstimate(flops=36 * 10**9, bytes_accessed=60 * 10**6, transcendentals=8 * 10**6),
        name="layer",
    )(*arrays)


def finish_kernel(*refs):
    ins, outs, held, (igf, na, nf, table), sems = refs[:10], refs[10:22], refs[22:32], refs[32:36], refs[36]
    out_o, ig_o, na_o, gq_o, gk_o, gv_o, go_o, nf_o, gg_o, gu_o, gd_o, table_o = outs
    loads = [pltpu.make_async_copy(src, dst, sems.at[i]) for i, (src, dst) in enumerate(zip(ins, held))]
    saves = []

    def save(src, dst):
        saves.append(pltpu.make_async_copy(src, dst, sems.at[10 + len(saves)]))
        saves[-1].start()

    for load in loads:
        load.start()
    ig, stat = held[1], held[9]
    loads[9].wait()
    nf[...] = jnp.concatenate([stat[i : i + 1, :] for i in range(3)], axis=1).reshape(D)
    na[...] = jnp.concatenate([stat[i : i + 1, :] for i in range(3, 6)], axis=1).reshape(D)
    rows = []
    for head in range(H):
        core, local = (head // 3) % 2, head % 3 + 3 * (head // 6)
        rows.append(stat[6 + core : 7 + core, 32 * local : 32 * (local + 1)])
    table[...] = jnp.concatenate(rows, axis=0)
    save(nf, nf_o)
    save(na, na_o)
    save(table, table_o)
    for i, dst in ((2, gq_o), (3, gk_o), (4, gv_o), (5, go_o), (6, gg_o), (7, gu_o), (8, gd_o), (0, out_o)):
        loads[i].wait()
        save(held[i], dst)
    loads[1].wait()
    for r in range(2):
        igf[r] = ig[r].astype(F32)
        save(igf.at[r], ig_o.at[r])
    for copy in saves:
        copy.wait()


def run_finish(results):
    output, input_grad, gq, gk, gv, go, gg, gu, gd, stat = results
    outs = [
        (output.shape, BF), (input_grad.shape, F32), ((D,), F32), (gq.shape, F32), (gk.shape, F32), (gv.shape, F32),
        (go.shape, F32), ((D,), F32), (gg.shape, F32), (gu.shape, F32), (gd.shape, F32), ((H, 32), F32),
    ]
    return pl.pallas_call(
        finish_kernel,
        out_shape=[jax.ShapeDtypeStruct(s, t) for s, t in outs],
        in_specs=[ANY] * 10,
        out_specs=[ANY] * 12,
        scratch_shapes=[
            *[pltpu.VMEM(r.shape, r.dtype) for r in results],
            pltpu.VMEM(input_grad.shape, F32),
            pltpu.VMEM((D,), F32),
            pltpu.VMEM((D,), F32),
            pltpu.VMEM((H, 32), F32),
            pltpu.SemaphoreType.DMA((24,)),
        ],
        compiler_params=pltpu.CompilerParams(vmem_limit_bytes=60 * 2**20),
        name="finish",
    )(*results)


def on_device(low, *arrays):
    arrays = list(arrays)
    arrays[11] = arrays[11].T
    output, input_grad, *grads, stat, _, _ = run_layer(low, *arrays)
    if low > 1:
        groups = [[low * high + i for i in range(low)] for high in range(8)]
        *grads, down = grads
        grads = [
            lax.psum_scatter(g, "dp", scatter_dimension=0, axis_index_groups=groups, tiled=True) for g in grads
        ]
        grads.append(lax.psum_scatter(down, "dp", scatter_dimension=1, axis_index_groups=groups, tiled=True))
        stat = lax.psum(stat, "dp", axis_index_groups=groups)
    results = list(run_finish([output, input_grad, *grads, stat]))
    results[10] = results[10].T
    results[11] = results[11].T
    return tuple(results)


def solution(mesh):
    rows = P("dp", "blk", None)
    split = P("dp", "blk")
    return jax.shard_map(
        functools.partial(on_device, mesh.shape["dp"] // 8),
        mesh=mesh,
        in_specs=(rows, split, P(), P(), P(), P(), P(), P(), P(), P(), P(), P(), rows),
        out_specs=(rows, rows, P(), split, split, split, split, P(), split, split, split, P()),
        check_vma=False,
    )
```

```python
import functools

import jax
import jax.numpy as jnp
from jax import lax
from jax.experimental import pallas as pl
from jax.experimental.pallas import tpu as pltpu
from jax.sharding import PartitionSpec as P

H = 12
HD = 64
EPSILON = 1e-06
MASKED = -1e30
LIMITS = (12, 16, 23, 32, 46, 64, 91)
FAR_BEFORE = 15
FAR_AFTER = 31

MESH = pl.DeviceIdType.MESH
BF = jnp.bfloat16
F32 = jnp.float32
ANY = pl.BlockSpec(memory_space=pl.ANY)
VM = pl.BlockSpec(memory_space=pltpu.VMEM)

D = 768
HALF = 384
ZB = 192
SLOTS = 1024
STRIPE = 128
OWN = 512


def dot(a, b):
    return lax.dot_general(a, b, (((1,), (0,)), ((), ())), preferred_element_type=F32)


def dot_nt(a, b):
    return lax.dot_general(a, b, (((1,), (1,)), ((), ())), preferred_element_type=F32)


def dot_tn(a, b):
    return lax.dot_general(a, b, (((0,), (0,)), ((), ())), preferred_element_type=F32)


class Place:
    def __init__(self, low):
        self.low = low
        self.dp = lax.axis_index("dp")
        self.z = lax.axis_index("blk")
        high = self.dp // low
        self.c = high % 2
        self.x = (high // 2) % 2
        self.y = high // 4
        self.base = self.dp - self.c * low
        self.z0 = self.z % 2
        self.z1 = self.z // 2
        self.core = (self.dp + low * (1 - 2 * self.c), self.z)
        self.xp = (self.dp + 2 * low * (1 - 2 * self.x), self.z)
        self.yp = (self.dp + 4 * low * (1 - 2 * self.y), self.z)
        self.z0p = (self.dp, self.z + 1 - 2 * self.z0)
        self.z1p = (self.dp, self.z + 2 - 4 * self.z1)

    def group(self):
        found = []
        for dc in range(2):
            for dz in range(4):
                if dc or dz:
                    found.append((self.base + ((self.c + dc) % 2) * self.low, (self.z + dz) % 4))
        return found

    def near(self, k):
        fold = jnp.where(self.z < 2, self.z, 3 - self.z)
        step = (k + fold * (1 - 2 * k)) if k < 2 else k
        return jnp.where(self.z < 2, step, 3 - step)


def greet(others):
    barrier = pltpu.get_barrier_semaphore()
    for other in others:
        pl.semaphore_signal(barrier, inc=1, device_id=other, device_id_type=MESH)
    pl.semaphore_wait(barrier, len(others))


def remote(src, dst, send, recv, device):
    return pltpu.make_async_remote_copy(
        src_ref=src, dst_ref=dst, send_sem=send, recv_sem=recv, device_id=device, device_id_type=MESH
    )


def bucket_tile():
    key = lax.broadcasted_iota(jnp.int32, (128, 384), 0)
    query = lax.broadcasted_iota(jnp.int32, (128, 384), 1)
    rel = key - query + 128
    dist = jnp.abs(rel)
    beyond = jnp.full((128, 384), 8, jnp.int32)
    for threshold in LIMITS:
        beyond = beyond + (dist >= threshold).astype(jnp.int32)
    return jnp.where(dist < 8, dist, beyond) + jnp.where(rel > 0, 16, 0)


def head_of(place, local):
    return 3 * place.c + local % 3 + 6 * (local // 3)


def lane_mask(head_in_pair):
    lane = lax.broadcasted_iota(jnp.int32, (1, 128), 1)
    inside = (lane < HD) if head_in_pair == 0 else (lane >= HD)
    return inside.astype(F32).astype(BF)


GELU_SCALE = 0.7978845608028654
GELU_CUBE = 0.044715
GROUPS = ("gate0", "up0", "gate1", "up1", "down0", "down1", "out", "query", "key", "value")
WIDE = 6
DOWN_AFTER = 2
SLOT = (0, 1, 2, 3, 0, 1, 4, 2, 3, 4)
PLAN = (
    (0,), (1,), (), (), (0,), (1,), (), (), (), (), (), (), (2,), (3,), (0, 6), (), (), (1, 2), (), (3,), (6,), (),
    (), (), (), (), (0,), (), (1, 4, 5), (), (), (), (), (), (4,), (), (5,), (), (), (0,), (3,), (1, 2), (), (0,),
    (7,), (1, 8), (9,), (6, 7, 8, 5), (9,), (2,), (4, 6), (3, 2),
    (7, 6, 8, 9, 2, 3, 6, 5, 4, 7, 3, 5, 8, 9, 4, 7, 5, 8, 9, 7, 4, 8, 9),
)


class Reduction:
    def __init__(self, me, unit, wide, narrow, stage, send, recv, finish):
        self.me, self.unit, self.wide, self.narrow, self.stage = me, unit, wide, narrow, stage
        self.send, self.recv, self.finish = send, recv, finish
        self.step = [0] * len(GROUPS)
        self.polls = 0

    def buffers(self, u):
        if u < WIDE:
            return [ref.at[u] for ref in self.wide]
        return [ref.at[u - WIDE] for ref in self.narrow]

    def copy(self, u, k):
        me = self.me
        r0, r1, r2, r3, r4 = self.buffers(u)
        cols = 512 if u < WIDE else HALF
        unit = self.unit.at[SLOT[u]]
        x_first = u % 2 == 0
        if k == 0 and u <= WIDE:
            src, dst, device = unit.at[:, :, :, 1 - me.c, :, pl.ds(0, cols)], r0, me.core
        elif k == 0:
            src, dst, device = unit.at[me.c, :, :, 1 - me.c, :, pl.ds(0, cols)], r0.at[me.c], me.core
        elif k == 1 and x_first:
            src, dst, device = r0.at[:, :, 1 - me.x], r1, me.xp
        elif k == 1:
            src, dst, device = r0.at[:, 1 - me.y], r1, me.yp
        elif k == 2 and x_first:
            src, dst, device = r1.at[:, 1 - me.y], r2, me.yp
        elif k == 2:
            src, dst, device = r1.at[:, 1 - me.x], r2, me.xp
        elif k == 3:
            src, dst, device = r2.at[1 - me.z0], r3, me.z0p
        elif u < WIDE:
            there = pl.ds(pl.multiple_of(256 * (1 - me.z1), 256), 256)
            src, dst, device = r3.at[:, there], r4, me.z1p
        else:
            src, dst, device = self.stage.at[u - WIDE], r4, me.z1p
        return remote(src, dst, self.send.at[u, k], self.recv.at[u, k], device)

    def poll(self):
        for u in PLAN[self.polls]:
            self.advance_one(u)
        self.polls += 1

    def advance_one(self, u):
        me = self.me
        k = self.step[u]
        r0, r1, r2, r3, r4 = self.buffers(u)
        cols = 512 if u < WIDE else HALF
        unit = self.unit.at[SLOT[u]]
        x_first = u % 2 == 0
        if k > 0:
            self.copy(u, k - 1).wait()

        if k == 1 and u <= WIDE:
            r0[...] += unit[:, :, :, me.c, :, 0:cols]
        elif k == 1:
            r0[me.c] = unit[me.c, :, :, me.c, :, 0:cols]
        elif k == 2:
            r1[...] += r0[:, :, me.x] if x_first else r0[:, me.y]
        elif k == 3:
            r2[...] += r1[:, me.y if x_first else me.x]
        elif k == 4:
            r3[...] += r2[me.z0]
            if u >= WIDE:
                self.stage[u - WIDE] = jnp.where(me.z1 == 0, r3[:, ZB:], r3[:, :ZB])
        elif k == 5:
            if u < WIDE:
                own = r3[:, pl.ds(pl.multiple_of(256 * me.z1, 256), 256)]
            else:
                own = jnp.where(me.z1 == 0, r3[:, :ZB], r3[:, ZB:])
            self.finish(GROUPS[u], own.astype(F32) + r4[...].astype(F32))
        if k < 5:
            self.copy(u, k).start()
        self.step[u] = k + 1


def layer_kernel(
    low,
    tok, seg, gain_a, wq, wk, wv, w_out, gain_f, w_gate, w_up, w_down, table_i, cot,
    out_o, ig_o, gq_o, gk_o, gv_o, go_o, gg_o, gu_o, gd_o, stat_o, e_o, wown_o,
    table, unit, a0, a1, a2, a3, a4, b0, b1, b2, b3, b4, bstage,
    xrow, segb, n1, q, k, v, o, linv, bkt,
    gv, obf, wout, dobv, dobrow, pn_recv, dh1, rows_out, bcount, stat, stat_in,
    x_send, x_recv, f_send, f_recv, c_send, c_recv, g_send, g_recv, o_send, o_recv,
    red_send, red_recv, t_send, t_recv, i_send, i_recv, d_send, d_recv, p_send, p_recv, s_send, s_recv,
    l_sem, w_sem, e_sem,
):
    me = Place(low)
    c, z = me.c, me.z

    def finish(name, total):
        if name[-1] in "01":
            kind, part = name[:-1], int(name[-1])
            if kind == "down":
                gd_o[96 * part : 96 * (part + 1), :] = total
            else:
                {"gate": gg_o, "up": gu_o}[kind][:, 256 * part : 256 * (part + 1)] = total
        else:
            {"out": go_o, "query": gq_o, "key": gk_o, "value": gv_o}[name][...] = total

    red = Reduction(me, unit, (a0, a1, a2, a3, a4), (b0, b1, b2, b3, b4), bstage, red_send, red_recv, finish)

    def targets():
        for r in range(2):
            for kk in range(2):
                yield r, kk, (me.base + kk * low, 2 * c + r), jnp.logical_and(2 * c + r == z, kk == c)

    def home(zz, send_sem, recv_sem, dest):
        dst = dest.at[me.z0, pl.ds(pl.multiple_of(STRIPE * c, STRIPE), STRIPE)]
        recv = recv_sem.at[me.z0, c]
        here = jnp.logical_and(zz == z, me.z1 == c)
        return here, rows_out.at[zz], dst, send_sem.at[zz], recv, (me.base + me.z1 * low, zz)

    def start_home(*where):
        for zz in range(4):
            here, src, dst, send, recv, device = home(zz, *where)

            @pl.when(here)
            def _():
                pltpu.make_async_copy(src, dst, send).start()

            @pl.when(jnp.logical_not(here))
            def _():
                remote(src, dst, send, recv, device).start()

    def sent_home(*where):
        for zz in range(4):
            here, src, dst, send, recv, device = home(zz, *where)

            @pl.when(here)
            def _():
                pltpu.make_async_copy(src, dst, send).wait()

            @pl.when(jnp.logical_not(here))
            def _():
                remote(src, dst, send, recv, device).wait_send()

    def got_home(send_sem, recv_sem, dest):
        for r in range(2):
            for kk in range(2):
                part = dest.at[r, pl.ds(STRIPE * kk, STRIPE)]

                @pl.when(jnp.logical_not(jnp.logical_and(2 * c + r == z, kk == c)))
                def _():
                    remote(part, part, send_sem.at[0], recv_sem.at[r, kk], me.core).wait_recv()

    to_partner = remote(dobv.at[1 - c], dobrow.at[:, c], d_send, d_recv, me.core)
    out_way = (t_send, t_recv, out_o)
    ig_way = (i_send, i_recv, ig_o)

    def attend(wg, wu, wd, wown, band, segcol, segrow, s_scr, e_scr, ot_scr, ob):
        raw = (wd.at[0, pl.ds(0, D)], wd.at[1, pl.ds(0, D)], wu.at[0, :, pl.ds(0, D)])
        loads = [pltpu.make_async_copy(w, dst, l_sem.at[i]) for i, (w, dst) in enumerate(zip((wq, wk, wv), raw))]
        table_load = pltpu.make_async_copy(table_i, table, l_sem.at[3])
        for load in loads + [table_load]:
            load.start()
        greet(me.group() + [me.xp, me.yp])

        for r, kk, device, here in targets():
            src = tok.at[r, pl.ds(STRIPE * kk, STRIPE)]
            dst = xrow.at[z, kk]
            far = remote(src, dst, x_send.at[r, kk], x_recv.at[z], device)
            near = pltpu.make_async_copy(src, dst, x_recv.at[z])
            sfar = remote(seg, segb.at[z], g_send.at[r, kk], g_recv.at[z], device)
            snear = pltpu.make_async_copy(seg, segb.at[z], g_recv.at[z])

            @pl.when(here)
            def _():
                near.start()
                snear.start()

            @pl.when(jnp.logical_not(here))
            def _():
                far.start()
                sfar.start()

        for i in range(3):
            loads[i].wait()
            w = raw[i]
            lo = jnp.concatenate([w[:, 0:ZB], w[:, 2 * ZB : 3 * ZB]], axis=1)
            hi = jnp.concatenate([w[:, ZB : 2 * ZB], w[:, 3 * ZB : 4 * ZB]], axis=1)
            wown[:, HALF * i : HALF * (i + 1)] = jnp.where(c == 0, lo, hi)
        bkt[...] = bucket_tile()
        table_load.wait()

        def make_band(hl, _):
            head = head_of(me, hl)
            for t in range(3):
                which = bkt[:, 128 * t : 128 * (t + 1)]
                total = jnp.zeros((128, 128), F32)
                for b in range(32):
                    total = jnp.where(which == b, table[head, b], total)
                band[hl, :, 128 * t : 128 * (t + 1)] = total
            return 0

        lax.fori_loop(0, 6, make_band, 0)

        for load in weight_loads(wg, wu, wd):
            load.start()
        keep = pltpu.make_async_copy(wown, wown_o, l_sem.at[0])
        keep.start()

        gain_f = gain_a[...].astype(F32).reshape(1, D)
        forwards = []
        for step in range(4):
            zz = me.near(step)
            own = xrow.at[zz, c]
            remote(own, own, x_send.at[0, 0], x_recv.at[zz], me.core).wait_recv()
            fwd = remote(own, own, f_send.at[step], f_recv.at[zz], me.core)
            fwd.start()
            forwards.append(fwd)
        for r, kk, device, here in targets():
            src = cot.at[r, pl.ds(STRIPE * kk, STRIPE)]
            dst = gv.at[z]
            far = remote(src, dst, c_send.at[r, kk], c_recv.at[z], device)
            near = pltpu.make_async_copy(src, dst, c_recv.at[z])

            @pl.when(here)
            def _():
                near.start()

            @pl.when(jnp.logical_not(here))
            def _():
                far.start()

        for step in range(4):
            zz = me.near(step)
            other = xrow.at[zz, 1 - c]
            remote(other, other, f_send.at[step], f_recv.at[zz], me.core).wait_recv()
            xf = xrow[zz].reshape(256, D).astype(F32)
            r1 = lax.rsqrt(jnp.mean(xf * xf, axis=-1, keepdims=True) + EPSILON)
            nb = (xf * r1 * gain_f).astype(BF)
            rows = pl.ds(pl.multiple_of(zz * 256, 256), 256)
            n1[rows, :] = nb
            for i, dest in enumerate((q, k, v)):
                dest[rows, :] = dot(nb, wown[:, HALF * i : HALF * (i + 1)]).astype(BF)

        for zz in range(4):
            blk_seg = segb.at[zz]
            remote(blk_seg, blk_seg, g_send.at[0, 0], g_recv.at[zz], me.core).wait_recv()
            segrow[:, 256 * zz : 256 * (zz + 1)] = segb[zz, pl.ds(z % 2, 1), :].astype(F32)
        segcol[...] = jnp.transpose(jnp.broadcast_to(segrow[...], (128, SLOTS)))
        linv[...] = jnp.zeros((8, SLOTS), F32)

        def pair_step(p, _):
            lanes = pl.ds(pl.multiple_of(p * 128, 128), 128)
            kp, vp = k[:, lanes], v[:, lanes]
            for hd in range(2):
                mask = lane_mask(hd)
                vm = vp * mask + (1 - mask)
                hl = 2 * p + hd
                head = head_of(me, hl)
                after, before = table[head, FAR_AFTER], table[head, FAR_BEFORE]

                @pl.when(p > 0)
                def _():
                    pltpu.make_async_copy(e_scr.at[hd], e_o.at[hl], e_sem.at[hd]).wait()

                for ib in range(4):
                    qm = q[256 * ib : 256 * (ib + 1), lanes] * mask
                    scr = s_scr.at[ib % 2]
                    scr[...] = dot_nt(kp, qm)
                    for t in range(2):
                        here = 2 * ib + t
                        cols = slice(128 * t, 128 * (t + 1))
                        seg_q = segrow[:, 256 * ib + 128 * t : 256 * ib + 128 * (t + 1)]
                        top = jnp.full((8, 128), MASKED, F32)
                        for jb in range(8):
                            rows = slice(128 * jb, 128 * (jb + 1))
                            tile = scr[rows, cols]
                            if abs(jb - here) <= 1:
                                off = 128 * (here - jb + 1)
                                tile = tile + band[hl, :, off : off + 128]
                            else:
                                tile = tile + (after if jb > here else before)
                            tile = jnp.where(segcol[rows, :] == seg_q, tile, MASKED)
                            scr[rows, cols] = tile
                            top = jnp.maximum(top, jnp.max(tile.reshape(16, 8, 128), axis=0))
                        top = jnp.max(top, axis=0, keepdims=True)
                        for jb in range(8):
                            rows = slice(128 * jb, 128 * (jb + 1))
                            weight = jnp.exp(scr[rows, cols] - top)
                            e_scr[hd, rows, 256 * ib + 128 * t : 256 * ib + 128 * (t + 1)] = weight.astype(BF)
                both = dot_tn(vm, e_scr[hd])
                data, sums = (both[0:HD], both[HD:128]) if hd == 0 else (both[HD:128], both[0:HD])
                inverse = 1.0 / sums
                ot_scr[HD * hd : HD * (hd + 1), :] = data * inverse
                linv[pl.ds(hl, 1), :] = inverse[0:1]
                pltpu.make_async_copy(e_scr.at[hd], e_o.at[hl], e_sem.at[hd]).start()
            mixed = jnp.transpose(ot_scr[...])
            o[:, lanes] = mixed
            ob[:, :, :, lanes] = mixed.astype(BF).reshape(4, 2, STRIPE, 128)
            mine = ob.at[:, 1 - c, :, lanes]
            remote(mine, obf.at[c, :, :, lanes], o_send.at[p], o_recv.at[p], me.core).start()
            return 0

        lax.fori_loop(0, 3, pair_step, 0)

        for hd in range(2):
            pltpu.make_async_copy(e_scr.at[hd], e_o.at[4 + hd], e_sem.at[hd]).wait()
        obf[c] = ob[:, c]
        for p in range(3):
            lanes = slice(128 * p, 128 * (p + 1))
            mine = ob.at[:, 1 - c, :, lanes]
            there = remote(mine, obf.at[1 - c, :, :, lanes], o_send.at[p], o_recv.at[p], me.core)
            there.wait_send()
            there.wait_recv()
        keep.wait()
        for fwd in forwards:
            fwd.wait_send()

    def weight_loads(wg, wu, wd):
        loads = []
        for i in range(4):
            loads.append(
                pltpu.make_async_copy(
                    w_out.at[pl.ds(ZB * i, ZB)], wout.at[i % 2, pl.ds(ZB * (i // 2), ZB)], l_sem.at[4 + i]
                )
            )
        for f in range(2):
            for which, (src, dst) in enumerate(((w_gate, wg), (w_up, wu), (w_down, wd))):
                for zz in range(4):
                    far = pl.ds(512 * zz + 256 * f, 256)
                    own = pl.ds(256 * zz, 256)
                    sem = w_sem.at[f, which, zz]
                    if which < 2:
                        loads.append(pltpu.make_async_copy(src.at[:, far], dst.at[f, :, own], sem))
                    else:
                        loads.append(pltpu.make_async_copy(src.at[far], dst.at[f, own], sem))
        return loads

    def feed_forward(hid, wg, wu, wd, n2, h1, acc, dga, dup, dab_v):
        loads = weight_loads(wg, wu, wd)
        for load in loads[:4]:
            load.wait()
        gain = gain_f[...].astype(F32).reshape(1, D)
        for i in range(2):
            rows = slice(256 * i, 256 * (i + 1))
            parts = slice(2 * i, 2 * (i + 1))
            h = xrow[parts, c].reshape(256, D).astype(F32)
            h = h + dot(obf[0, parts].reshape(256, HALF), wout[0]) + dot(obf[1, parts].reshape(256, HALF), wout[1])
            h1[rows, :] = h
            r2 = lax.rsqrt(jnp.mean(h * h, axis=-1, keepdims=True) + EPSILON)
            n2[rows, :] = (h * r2 * gain).astype(BF)
        for zz in range(4):
            got = gv.at[zz]
            remote(got, got, c_send.at[0, 0], c_recv.at[zz], me.core).wait_recv()

        def gate_up(f):
            for which, grads in enumerate((dga, dup)):
                for zz in range(4):
                    piece = dot_tn(n2[...], grads[:, 256 * zz : 256 * (zz + 1)]).astype(BF)
                    unit[SLOT[2 * f + which], zz % 2, :, :, :, :, 256 * (zz // 2) : 256 * (zz // 2 + 1)] = piece.reshape(
                        2, 2, 2, 96, 256
                    )
                red.poll()

        for f in range(2):
            for load in loads[4 + 12 * f : 16 + 12 * f]:
                load.wait()
            for i in range(2):
                rows = slice(256 * i, 256 * (i + 1))
                gate = dot(n2[rows, :], wg[f])
                up = dot(n2[rows, :], wu[f])
                dhid = dot_nt(gv[2 * i : 2 * (i + 1)].reshape(256, D), wd[f])
                square = gate * gate
                th = jnp.tanh(GELU_SCALE * gate * (1.0 + GELU_CUBE * square))
                half = 0.5 + 0.5 * th
                gelu = gate * half
                slope = half + 0.5 * GELU_SCALE * gate * (1.0 - th * th) * (1.0 + 3.0 * GELU_CUBE * square)
                hid[f, rows, :] = (gelu * up).astype(BF)
                dup[rows, :] = (dhid * gelu).astype(BF)
                dga[rows, :] = (dhid * up * slope).astype(BF)
                if f == 1:
                    red.poll()
            if f == 1:
                for i in range(4):
                    rows = slice(128 * i, 128 * (i + 1))
                    rows_out[i] = (h1[rows, :] + acc[rows, :] + dot(hid[f, rows, :], wd[f])).astype(BF)
                start_home(*out_way)
                red.poll()
            if f == 0:
                gate_up(0)
            if f == 0:
                acc[...] = dot(hid[f], wd[f])
                red.poll()
                dh1[...] = dot_nt(dga[...], wg[f])
            else:
                dh1[...] += dot_nt(dga[...], wg[f])
            red.poll()
            dh1[...] += dot_nt(dup[...], wu[f])
            red.poll()
        total = jnp.zeros((1, D), F32)
        for i in range(4):
            rows = slice(128 * i, 128 * (i + 1))
            h = h1[rows, :]
            r2 = lax.rsqrt(jnp.mean(h * h, axis=-1, keepdims=True) + EPSILON)
            u2 = h * r2
            dn2 = dh1[rows, :]
            total = total + jnp.sum(dn2 * u2, axis=0, keepdims=True)
            wn = dn2 * gain
            dh = gv[i].astype(F32) + r2 * (wn - u2 * jnp.mean(wn * u2, axis=-1, keepdims=True))
            dh1[rows, :] = dh
            dab_v[rows, :] = dh.astype(BF)
        stat[...] = jnp.zeros((6, 8, 256), F32)
        for i in range(3):
            stat[0, i : i + 1, :] = total[:, 256 * i : 256 * (i + 1)]
        red.poll()
        dab = dab_v[...]
        for cp in range(2):
            dobv[cp] = dot_nt(dab, wout[cp]).astype(BF).reshape(4, STRIPE, HALF)
        to_partner.start()
        dobrow[:, c] = dobv[c]
        red.poll()
        gate_up(1)
        for a in range(2):
            dz = jnp.concatenate([dab[:, ZB * a : ZB * (a + 1)], dab[:, ZB * (a + 2) : ZB * (a + 3)]], axis=1)
            for cp in range(2):
                piece = dot_tn(obf[cp].reshape(OWN, HALF), dz).astype(BF)
                for yy in range(2):
                    for cc in range(2):
                        row = 96 * (2 * yy + cc)
                        unit[SLOT[6], a, yy, cp, cc, :, 0:HALF] = piece[row : row + 96]
        red.poll()

    def down(hid):
        for f in range(2):
            for zz in range(4):
                piece = dot_tn(gv[...].reshape(OWN, D), hid[f, :, 256 * zz : 256 * (zz + 1)]).astype(BF)
                for to in range(4):
                    for part in range(2):
                        row = ZB * to + 96 * part
                        unit[SLOT[4 + part], to % 2, zz // 2, zz % 2, f, :, 256 * (to // 2) : 256 * (to // 2 + 1)] = piece[
                            row : row + 96
                        ]
            red.poll()

    def attention(hid, dqkv, e, ds, dp_scr, dob_scr, dv_scr, dk_scr, dqt_scr, band):
        fetch = [pltpu.make_async_copy(e_o.at[h], e.at[h % 2], e_sem.at[2 + h]) for h in range(6)]
        fetch[0].start()
        fetch[1].start()
        to_partner.wait()
        first_half = lax.broadcasted_iota(jnp.int32, (1, 128), 1) < HD
        for p in range(3):
            lanes = slice(128 * p, 128 * (p + 1))
            kp, vp, qp = k[:, lanes], v[:, lanes], q[:, lanes]
            inverse = jnp.concatenate(
                [jnp.broadcast_to(linv[2 * p + hd : 2 * p + hd + 1, :], (HD, SLOTS)) for hd in range(2)], axis=0
            )
            scaled = dobrow[:, :, :, lanes].reshape(SLOTS, 128).astype(F32) * jnp.transpose(inverse)
            dob_scr[...] = scaled.astype(BF)
            product = jnp.transpose(scaled * o[:, lanes])
            for hd in range(2):
                h = 2 * p + hd
                delta = jnp.sum(product[HD * hd : HD * (hd + 1)], axis=0, keepdims=True)
                vm = vp * lane_mask(hd)
                fetch[h].wait()
                ev = e.at[hd]
                band[...] = jnp.zeros((128, 384), F32)
                after = jnp.zeros((8, 128), F32)
                before = jnp.zeros((8, 128), F32)
                for ib in range(4):
                    scr = dp_scr.at[ib % 2]
                    scr[...] = dot_nt(vm, dob_scr[256 * ib : 256 * (ib + 1), :])
                    for t in range(2):
                        here = 2 * ib + t
                        cols = slice(128 * here, 128 * (here + 1))
                        for jb in range(8):
                            rows = slice(128 * jb, 128 * (jb + 1))
                            dsv = ev[rows, cols].astype(F32) * (scr[rows, 128 * t : 128 * (t + 1)] - delta[:, cols])
                            ds[rows, cols] = dsv.astype(BF)
                            if abs(jb - here) <= 1:
                                off = 128 * (here - jb + 1)
                                band[:, off : off + 128] += dsv
                            elif jb > here:
                                after = after + jnp.sum(dsv.reshape(16, 8, 128), axis=0)
                            else:
                                before = before + jnp.sum(dsv.reshape(16, 8, 128), axis=0)
                    red.poll()
                dv = dot(ev[...], dob_scr[...])
                dk = dot(ds[...], qp)
                dqt_scr[HD * hd : HD * (hd + 1), :] = dot_tn(kp, ds[...])[HD * hd : HD * (hd + 1)]
                if hd == 0:
                    dv_scr[...] = dv
                    dk_scr[...] = dk
                else:
                    for i, val in enumerate(
                        (
                            jnp.transpose(dqt_scr[...]),
                            jnp.where(first_half, dk_scr[...], dk),
                            jnp.where(first_half, dv_scr[...], dv),
                        )
                    ):
                        dqkv[:, :, :, HALF * i + 128 * p : HALF * i + 128 * (p + 1)] = val.astype(BF).reshape(
                            4, 2, STRIPE, 128
                        )
                if h + 2 < 6:
                    fetch[h + 2].start()
                for b in range(32):
                    part = jnp.zeros((1, 128), F32)
                    for t in range(3):
                        own = slice(128 * t, 128 * (t + 1))
                        part = part + jnp.sum(jnp.where(bkt[:, own] == b, band[:, own], 0.0), axis=0, keepdims=True)
                    if b == FAR_AFTER:
                        part = part + jnp.sum(after, axis=0, keepdims=True)
                    if b == FAR_BEFORE:
                        part = part + jnp.sum(before, axis=0, keepdims=True)
                    bcount[32 * h + b : 32 * h + b + 1, :] = part
                if h == DOWN_AFTER:
                    down(hid)

    def tail(dqkv, wown, dn1, pn_send):
        load = pltpu.make_async_copy(wown_o, wown, l_sem.at[0])
        load.start()
        sent_home(*out_way)
        load.wait()
        pn_send[...] = dot_nt(dqkv[:, 1 - c].reshape(OWN, 3 * HALF), wown[...]).astype(BF).reshape(4, STRIPE, D)
        partial = remote(pn_send, pn_recv, p_send, p_recv, me.core)
        partial.start()
        red.poll()
        dn1[...] = dot_nt(dqkv[:, c].reshape(OWN, 3 * HALF), wown[...])
        red.poll()
        partial.wait()
        gain = gain_a[...].astype(F32).reshape(1, D)
        total = jnp.zeros((1, D), F32)
        for i in range(4):
            rows = slice(128 * i, 128 * (i + 1))
            xf = xrow[i, c].astype(F32)
            r1 = lax.rsqrt(jnp.mean(xf * xf, axis=-1, keepdims=True) + EPSILON)
            u1 = xf * r1
            dn = dn1[rows, :] + pn_recv[i].astype(F32)
            total = total + jnp.sum(dn * u1, axis=0, keepdims=True)
            wn = dn * gain
            ig = dh1[rows, :] + r1 * (wn - u1 * jnp.mean(wn * u1, axis=-1, keepdims=True))
            rows_out[i] = ig.astype(BF)
        start_home(*ig_way)
        red.poll()
        for i in range(3):
            grads = dqkv[:, :, :, HALF * i : HALF * (i + 1)].reshape(SLOTS, HALF)
            unit[SLOT[7 + i], c, :, :, :, :, 0:HALF] = dot_tn(n1[...], grads).astype(BF).reshape(2, 2, 2, 96, HALF)
            red.poll()
        for i in range(3):
            stat[0, 3 + i : 4 + i, :] = total[:, 256 * i : 256 * (i + 1)]
        counts = jnp.sum(jnp.transpose(bcount[...]), axis=0, keepdims=True)
        stat[0, pl.ds(6 + c, 1), :] = jnp.concatenate([counts, jnp.zeros((1, 64), F32)], axis=1)
        copies = []
        for i, other in enumerate((me.core, me.xp, me.yp, me.z0p, me.z1p)):
            copy = remote(stat.at[i], stat_in.at[i], s_send.at[i], s_recv.at[i], other)
            copy.start()
            red.poll()
            copy.wait()
            stat[i + 1] = stat[i] + stat_in[i]
        stat_o[...] = stat[5]
        red.poll()
        sent_home(*ig_way)
        got_home(*out_way)
        got_home(*ig_way)
        for r, kk, device, here in targets():

            @pl.when(jnp.logical_not(here))
            def _():
                src = tok.at[r, pl.ds(STRIPE * kk, STRIPE)]
                remote(src, xrow.at[z, kk], x_send.at[r, kk], x_recv.at[z], device).wait_send()
                remote(seg, segb.at[z], g_send.at[r, kk], g_recv.at[z], device).wait_send()
                srcc = cot.at[r, pl.ds(STRIPE * kk, STRIPE)]
                remote(srcc, gv.at[z], c_send.at[r, kk], c_recv.at[z], device).wait_send()

    def first_half(hid, wg, wu, wd):
        pl.run_scoped(
            functools.partial(attend, wg, wu, wd),
            pltpu.VMEM((D, 3 * HALF), BF),
            pltpu.VMEM((6, 128, 384), F32),
            pltpu.VMEM((SLOTS, 128), F32),
            pltpu.VMEM((1, SLOTS), F32),
            pltpu.VMEM((2, SLOTS, 256), F32),
            pltpu.VMEM((2, SLOTS, SLOTS), BF),
            pltpu.VMEM((128, SLOTS), F32),
            pltpu.VMEM((4, 2, STRIPE, HALF), BF),
        )
        pl.run_scoped(
            functools.partial(feed_forward, hid, wg, wu, wd),
            pltpu.VMEM((OWN, D), BF),
            pltpu.VMEM((OWN, D), F32),
            pltpu.VMEM((OWN, D), F32),
            pltpu.VMEM((OWN, 1024), BF),
            pltpu.VMEM((OWN, 1024), BF),
            pltpu.VMEM((OWN, D), BF),
        )

    def second_half(hid, dqkv):
        pl.run_scoped(
            functools.partial(attention, hid, dqkv),
            pltpu.VMEM((2, SLOTS, SLOTS), BF),
            pltpu.VMEM((SLOTS, SLOTS), BF),
            pltpu.VMEM((2, SLOTS, 256), F32),
            pltpu.VMEM((SLOTS, 128), BF),
            pltpu.VMEM((SLOTS, 128), F32),
            pltpu.VMEM((SLOTS, 128), F32),
            pltpu.VMEM((128, SLOTS), F32),
            pltpu.VMEM((128, 384), F32),
        )
        pl.run_scoped(
            functools.partial(tail, dqkv),
            pltpu.VMEM((D, 3 * HALF), BF),
            pltpu.VMEM((OWN, D), F32),
            pltpu.VMEM((4, STRIPE, D), BF),
        )

    def whole(hid):
        pl.run_scoped(
            functools.partial(first_half, hid),
            pltpu.VMEM((2, D, 1024), BF),
            pltpu.VMEM((2, D, 1024), BF),
            pltpu.VMEM((2, 1024, D), BF),
        )
        pl.run_scoped(functools.partial(second_half, hid), pltpu.VMEM((4, 2, STRIPE, 3 * HALF), BF))

    pl.run_scoped(whole, pltpu.VMEM((2, OWN, 1024), BF))


def run_layer(low, *arrays):
    shapes = (
        ((2, 256, D), BF),
        ((2, 256, D), BF),
        ((96, ZB), F32),
        ((96, ZB), F32),
        ((96, ZB), F32),
        ((96, ZB), F32),
        ((96, 512), F32),
        ((96, 512), F32),
        ((ZB, 256), F32),
        ((8, 256), F32),
        ((6, SLOTS, SLOTS), BF),
        ((D, 3 * HALF), BF),
    )
    dma = pltpu.SemaphoreType.DMA
    wide = [(2, 2, 2, 96, 512), (2, 2, 96, 512), (2, 96, 512), (96, 512), (96, 256)]
    narrow = [(2, 2, 2, 96, HALF), (2, 2, 96, HALF), (2, 96, HALF), (96, HALF), (96, ZB)]
    specs = [ANY] * 13
    specs[2] = specs[7] = VM
    return pl.pallas_call(
        functools.partial(layer_kernel, low),
        out_shape=[jax.ShapeDtypeStruct(s, t) for s, t in shapes],
        in_specs=specs,
        out_specs=[ANY, ANY] + [VM] * 8 + [ANY, ANY],
        scratch_shapes=[
            pltpu.SMEM((H, 32), F32),
            pltpu.VMEM((5, 2, 2, 2, 2, 96, 512), BF),
            *[pltpu.VMEM((6, *s), BF) for s in wide],
            *[pltpu.VMEM((4, *s), BF) for s in narrow],
            pltpu.VMEM((4, 96, ZB), BF),
            pltpu.VMEM((4, 2, STRIPE, D), BF),
            pltpu.VMEM((4, 2, 256), jnp.int32),
            pltpu.VMEM((SLOTS, D), BF),
            pltpu.VMEM((SLOTS, HALF), BF),
            pltpu.VMEM((SLOTS, HALF), BF),
            pltpu.VMEM((SLOTS, HALF), BF),
            pltpu.VMEM((SLOTS, HALF), F32),
            pltpu.VMEM((8, SLOTS), F32),
            pltpu.VMEM((128, 384), jnp.int32),
            pltpu.VMEM((4, STRIPE, D), BF),
            pltpu.VMEM((2, 4, STRIPE, HALF), BF),
            pltpu.VMEM((2, HALF, D), BF),
            pltpu.VMEM((2, 4, STRIPE, HALF), BF),
            pltpu.VMEM((4, 2, STRIPE, HALF), BF),
            pltpu.VMEM((4, STRIPE, D), BF),
            pltpu.VMEM((OWN, D), F32),
            pltpu.VMEM((4, STRIPE, D), BF),
            pltpu.VMEM((192, 128), F32),
            pltpu.VMEM((6, 8, 256), F32),
            pltpu.VMEM((5, 8, 256), F32),
            dma((2, 2)), dma((4,)), dma((4,)), dma((4,)), dma((2, 2)), dma((4,)),
            dma((2, 2)), dma((4,)), dma((3,)), dma((3,)),
            dma((10, 5)), dma((10, 5)),
            dma((4,)), dma((2, 2)), dma((4,)), dma((2, 2)),
            dma, dma, dma, dma, dma((5,)), dma((5,)),
            dma((8,)), dma((2, 3, 4)), dma((8,)),
        ],
        compiler_params=pltpu.CompilerParams(
            collective_id=0, has_side_effects=True, vmem_limit_bytes=63 * 2**20
        ),
        cost_estimate=pl.CostEstimate(flops=36 * 10**9, bytes_accessed=60 * 10**6, transcendentals=8 * 10**6),
        name="layer",
    )(*arrays)


def finish_kernel(*refs):
    ins, outs, held, (igf, na, nf, table), sems = refs[:10], refs[10:22], refs[22:32], refs[32:36], refs[36]
    out_o, ig_o, na_o, gq_o, gk_o, gv_o, go_o, nf_o, gg_o, gu_o, gd_o, table_o = outs
    loads = [pltpu.make_async_copy(src, dst, sems.at[i]) for i, (src, dst) in enumerate(zip(ins, held))]
    saves = []

    def save(src, dst):
        saves.append(pltpu.make_async_copy(src, dst, sems.at[10 + len(saves)]))
        saves[-1].start()

    for load in loads:
        load.start()
    ig, stat = held[1], held[9]
    loads[9].wait()
    nf[...] = jnp.concatenate([stat[i : i + 1, :] for i in range(3)], axis=1).reshape(D)
    na[...] = jnp.concatenate([stat[i : i + 1, :] for i in range(3, 6)], axis=1).reshape(D)
    rows = []
    for head in range(H):
        core, local = (head // 3) % 2, head % 3 + 3 * (head // 6)
        rows.append(stat[6 + core : 7 + core, 32 * local : 32 * (local + 1)])
    table[...] = jnp.concatenate(rows, axis=0)
    save(nf, nf_o)
    save(na, na_o)
    save(table, table_o)
    for i, dst in ((2, gq_o), (3, gk_o), (4, gv_o), (5, go_o), (6, gg_o), (7, gu_o), (8, gd_o), (0, out_o)):
        loads[i].wait()
        save(held[i], dst)
    loads[1].wait()
    for r in range(2):
        igf[r] = ig[r].astype(F32)
        save(igf.at[r], ig_o.at[r])
    for copy in saves:
        copy.wait()


def run_finish(results):
    output, input_grad, gq, gk, gv, go, gg, gu, gd, stat = results
    outs = [
        (output.shape, BF), (input_grad.shape, F32), ((D,), F32), (gq.shape, F32), (gk.shape, F32), (gv.shape, F32),
        (go.shape, F32), ((D,), F32), (gg.shape, F32), (gu.shape, F32), (gd.shape, F32), ((H, 32), F32),
    ]
    return pl.pallas_call(
        finish_kernel,
        out_shape=[jax.ShapeDtypeStruct(s, t) for s, t in outs],
        in_specs=[ANY] * 10,
        out_specs=[ANY] * 12,
        scratch_shapes=[
            *[pltpu.VMEM(r.shape, r.dtype) for r in results],
            pltpu.VMEM(input_grad.shape, F32),
            pltpu.VMEM((D,), F32),
            pltpu.VMEM((D,), F32),
            pltpu.VMEM((H, 32), F32),
            pltpu.SemaphoreType.DMA((24,)),
        ],
        compiler_params=pltpu.CompilerParams(vmem_limit_bytes=60 * 2**20),
        name="finish",
    )(*results)


def on_device(low, *arrays):
    arrays = list(arrays)
    arrays[11] = arrays[11].T
    output, input_grad, *grads, stat, _, _ = run_layer(low, *arrays)
    if low > 1:
        groups = [[low * high + i for i in range(low)] for high in range(8)]
        *grads, down = grads
        grads = [
            lax.psum_scatter(g, "dp", scatter_dimension=0, axis_index_groups=groups, tiled=True) for g in grads
        ]
        grads.append(lax.psum_scatter(down, "dp", scatter_dimension=1, axis_index_groups=groups, tiled=True))
        stat = lax.psum(stat, "dp", axis_index_groups=groups)
    results = list(run_finish([output, input_grad, *grads, stat]))
    results[10] = results[10].T
    results[11] = results[11].T
    return tuple(results)


def solution(mesh):
    rows = P("dp", "blk", None)
    split = P("dp", "blk")
    return jax.shard_map(
        functools.partial(on_device, mesh.shape["dp"] // 8),
        mesh=mesh,
        in_specs=(rows, split, P(), P(), P(), P(), P(), P(), P(), P(), P(), P(), rows),
        out_specs=(rows, rows, P(), split, split, split, split, P(), split, split, split, P()),
        check_vma=False,
    )
```

```python
import functools

import jax
import jax.numpy as jnp
from jax import lax
from jax.experimental import pallas as pl
from jax.experimental.pallas import tpu as pltpu
from jax.sharding import PartitionSpec as P

H = 12
HD = 64
EPSILON = 1e-06
MASKED = -1e30
LIMITS = (12, 16, 23, 32, 46, 64, 91)
FAR_BEFORE = 15
FAR_AFTER = 31

MESH = pl.DeviceIdType.MESH
BF = jnp.bfloat16
F32 = jnp.float32
ANY = pl.BlockSpec(memory_space=pl.ANY)
VM = pl.BlockSpec(memory_space=pltpu.VMEM)

D = 768
HALF = 384
ZB = 192
SLOTS = 1024
STRIPE = 128
OWN = 512


def dot(a, b):
    return lax.dot_general(a, b, (((1,), (0,)), ((), ())), preferred_element_type=F32)


def dot_nt(a, b):
    return lax.dot_general(a, b, (((1,), (1,)), ((), ())), preferred_element_type=F32)


def dot_tn(a, b):
    return lax.dot_general(a, b, (((0,), (0,)), ((), ())), preferred_element_type=F32)


class Place:
    def __init__(self, low):
        self.low = low
        self.dp = lax.axis_index("dp")
        self.z = lax.axis_index("blk")
        high = self.dp // low
        self.c = high % 2
        self.x = (high // 2) % 2
        self.y = high // 4
        self.base = self.dp - self.c * low
        self.z0 = self.z % 2
        self.z1 = self.z // 2
        self.core = (self.dp + low * (1 - 2 * self.c), self.z)
        self.xp = (self.dp + 2 * low * (1 - 2 * self.x), self.z)
        self.yp = (self.dp + 4 * low * (1 - 2 * self.y), self.z)
        self.z0p = (self.dp, self.z + 1 - 2 * self.z0)
        self.z1p = (self.dp, self.z + 2 - 4 * self.z1)

    def group(self):
        found = []
        for dc in range(2):
            for dz in range(4):
                if dc or dz:
                    found.append((self.base + ((self.c + dc) % 2) * self.low, (self.z + dz) % 4))
        return found

    def near(self, k):
        fold = jnp.where(self.z < 2, self.z, 3 - self.z)
        step = (k + fold * (1 - 2 * k)) if k < 2 else k
        return jnp.where(self.z < 2, step, 3 - step)


def greet(others):
    barrier = pltpu.get_barrier_semaphore()
    for other in others:
        pl.semaphore_signal(barrier, inc=1, device_id=other, device_id_type=MESH)
    pl.semaphore_wait(barrier, len(others))


def remote(src, dst, send, recv, device):
    return pltpu.make_async_remote_copy(
        src_ref=src, dst_ref=dst, send_sem=send, recv_sem=recv, device_id=device, device_id_type=MESH
    )


def bucket_tile():
    key = lax.broadcasted_iota(jnp.int32, (128, 384), 0)
    query = lax.broadcasted_iota(jnp.int32, (128, 384), 1)
    rel = key - query + 128
    dist = jnp.abs(rel)
    beyond = jnp.full((128, 384), 8, jnp.int32)
    for threshold in LIMITS:
        beyond = beyond + (dist >= threshold).astype(jnp.int32)
    return jnp.where(dist < 8, dist, beyond) + jnp.where(rel > 0, 16, 0)


def head_of(place, local):
    return 3 * place.c + local % 3 + 6 * (local // 3)


def lane_mask(head_in_pair):
    lane = lax.broadcasted_iota(jnp.int32, (1, 128), 1)
    inside = (lane < HD) if head_in_pair == 0 else (lane >= HD)
    return inside.astype(F32).astype(BF)


GELU_SCALE = 0.7978845608028654
GELU_CUBE = 0.044715
GROUPS = ("gate0", "up0", "gate1", "up1", "down0", "down1", "out", "query", "key", "value")
WIDE = 6
ORDER = (
    ("x", "y", "z0"),
    ("y", "x", "z0"),
    ("x", "y", "z0"),
    ("y", "x", "z0"),
    ("z0", "y", "x"),
    ("y", "x", "z0"),
    ("x", "z0", "y"),
    ("y", "x", "z0"),
    ("x", "y", "z0"),
    ("y", "x", "z0"),
)
DOWN_AFTER = 2
SLOT = (0, 1, 2, 3, 0, 1, 4, 2, 3, 4)
PLAN = (
    (0,), (1,), (), (), (0,), (1,), (), (), (), (), (), (), (2,), (3,), (0, 6), (), (), (1, 2), (), (3,), (6,), (),
    (), (), (), (), (0,), (), (1, 4, 5), (), (), (), (), (), (4,), (), (5,), (), (), (0,), (3,), (2,), (1,), (),
    (7,), (0, 8), (9,), (6, 7, 8, 5, 1), (9, 3), (2,), (8,), (7,),
    (5, 4, 6, 3, 2, 7, 9, 8, 9, 5, 4, 3, 2, 6, 7, 4, 8, 9, 5, 6, 7, 8, 4, 9),
)


class Reduction:
    def __init__(self, me, unit, wide, narrow, stage, send, recv, finish):
        self.me, self.unit, self.wide, self.narrow, self.stage = me, unit, wide, narrow, stage
        self.send, self.recv, self.finish = send, recv, finish
        self.step = [0] * len(GROUPS)
        self.polls = 0

    def buffers(self, u):
        if u < WIDE:
            return [ref.at[u] for ref in self.wide]
        return [ref.at[u - WIDE] for ref in self.narrow]

    def half(self, u, k, mine):
        axis = ORDER[u][k - 1]
        left = [a for a in ("z0", "y", "x") if a not in ORDER[u][: k - 1]]
        at = {"x": self.me.x, "y": self.me.y, "z0": self.me.z0}[axis]
        return tuple((at if mine else 1 - at) if a == axis else slice(None) for a in left)

    def copy(self, u, k):
        me = self.me
        r0, r1, r2, r3, r4 = self.buffers(u)
        cols = 512 if u < WIDE else HALF
        unit = self.unit.at[SLOT[u]]
        if k == 0 and u <= WIDE:
            src, dst, device = unit.at[:, :, :, 1 - me.c, :, pl.ds(0, cols)], r0, me.core
        elif k == 0:
            src, dst, device = unit.at[me.c, :, :, 1 - me.c, :, pl.ds(0, cols)], r0.at[me.c], me.core
        elif k < 4:
            src, dst = (r0, r1, r2)[k - 1].at[self.half(u, k, False)], (r1, r2, r3)[k - 1]
            device = {"x": me.xp, "y": me.yp, "z0": me.z0p}[ORDER[u][k - 1]]
        elif u < WIDE:
            there = pl.ds(pl.multiple_of(256 * (1 - me.z1), 256), 256)
            src, dst, device = r3.at[:, there], r4, me.z1p
        else:
            src, dst, device = self.stage.at[u - WIDE], r4, me.z1p
        return remote(src, dst, self.send.at[u, k], self.recv.at[u, k], device)

    def poll(self):
        for u in PLAN[self.polls]:
            self.advance_one(u)
        self.polls += 1

    def advance_one(self, u):
        me = self.me
        k = self.step[u]
        r0, r1, r2, r3, r4 = self.buffers(u)
        cols = 512 if u < WIDE else HALF
        unit = self.unit.at[SLOT[u]]
        if k > 0:
            self.copy(u, k - 1).wait()

        if k == 1 and u <= WIDE:
            r0[...] += unit[:, :, :, me.c, :, 0:cols]
        elif k == 1:
            r0[me.c] = unit[me.c, :, :, me.c, :, 0:cols]
        elif 1 < k < 5:
            held, came = (r0, r1, r2)[k - 2], (r1, r2, r3)[k - 2]
            came[...] += held[self.half(u, k - 1, True)]
            if k == 4 and u >= WIDE:
                self.stage[u - WIDE] = jnp.where(me.z1 == 0, r3[:, ZB:], r3[:, :ZB])
        elif k == 5:
            if u < WIDE:
                own = r3[:, pl.ds(pl.multiple_of(256 * me.z1, 256), 256)]
            else:
                own = jnp.where(me.z1 == 0, r3[:, :ZB], r3[:, ZB:])
            self.finish(GROUPS[u], own.astype(F32) + r4[...].astype(F32))
        if k < 5:
            self.copy(u, k).start()
        self.step[u] = k + 1


def layer_kernel(
    low,
    tok, seg, gain_a, wq, wk, wv, w_out, gain_f, w_gate, w_up, w_down, table_i, cot,
    out_o, ig_o, gq_o, gk_o, gv_o, go_o, gg_o, gu_o, gd_o, stat_o, e_o, wown_o,
    table, unit, a0, a1, a2, a3, a4, b0, b1, b2, b3, b4, bstage,
    xrow, segb, n1, q, k, v, o, ob, linv, bkt,
    gv, obf, wout, dobv, dobrow, pn_recv, dh1, rows_out, bcount, stat, stat_in,
    x_send, x_recv, f_send, f_recv, c_send, c_recv, g_send, g_recv, o_send, o_recv,
    red_send, red_recv, t_send, t_recv, i_send, i_recv, d_send, d_recv, p_send, p_recv, s_send, s_recv,
    l_sem, w_sem, e_sem,
):
    me = Place(low)
    c, z = me.c, me.z

    def finish(name, total):
        if name[-1] in "01":
            kind, part = name[:-1], int(name[-1])
            if kind == "down":
                gd_o[96 * part : 96 * (part + 1), :] = total
            else:
                {"gate": gg_o, "up": gu_o}[kind][:, 256 * part : 256 * (part + 1)] = total
        else:
            {"out": go_o, "query": gq_o, "key": gk_o, "value": gv_o}[name][...] = total

    red = Reduction(me, unit, (a0, a1, a2, a3, a4), (b0, b1, b2, b3, b4), bstage, red_send, red_recv, finish)

    def targets():
        for r in range(2):
            for kk in range(2):
                yield r, kk, (me.base + kk * low, 2 * c + r), jnp.logical_and(2 * c + r == z, kk == c)

    def home(zz, send_sem, recv_sem, dest):
        dst = dest.at[me.z0, pl.ds(pl.multiple_of(STRIPE * c, STRIPE), STRIPE)]
        recv = recv_sem.at[me.z0, c]
        here = jnp.logical_and(zz == z, me.z1 == c)
        return here, rows_out.at[zz], dst, send_sem.at[zz], recv, (me.base + me.z1 * low, zz)

    def start_home(*where):
        for zz in range(4):
            here, src, dst, send, recv, device = home(zz, *where)

            @pl.when(here)
            def _():
                pltpu.make_async_copy(src, dst, send).start()

            @pl.when(jnp.logical_not(here))
            def _():
                remote(src, dst, send, recv, device).start()

    def sent_home(*where):
        for zz in range(4):
            here, src, dst, send, recv, device = home(zz, *where)

            @pl.when(here)
            def _():
                pltpu.make_async_copy(src, dst, send).wait()

            @pl.when(jnp.logical_not(here))
            def _():
                remote(src, dst, send, recv, device).wait_send()

    def got_home(send_sem, recv_sem, dest):
        for r in range(2):
            for kk in range(2):
                part = dest.at[r, pl.ds(STRIPE * kk, STRIPE)]

                @pl.when(jnp.logical_not(jnp.logical_and(2 * c + r == z, kk == c)))
                def _():
                    remote(part, part, send_sem.at[0], recv_sem.at[r, kk], me.core).wait_recv()

    to_partner = remote(dobv.at[1 - c], dobrow.at[:, c], d_send, d_recv, me.core)
    out_way = (t_send, t_recv, out_o)
    ig_way = (i_send, i_recv, ig_o)

    def attend(wg, wu, wd, wown, band, segcol, segrow, s_scr, e_scr, ot_scr):
        raw = (wd.at[0, pl.ds(0, D)], wd.at[1, pl.ds(0, D)], wu.at[0, :, pl.ds(0, D)])
        loads = [pltpu.make_async_copy(w, dst, l_sem.at[i]) for i, (w, dst) in enumerate(zip((wq, wk, wv), raw))]
        table_load = pltpu.make_async_copy(table_i, table, l_sem.at[3])
        for load in loads + [table_load]:
            load.start()
        greet(me.group() + [me.xp, me.yp])

        for r, kk, device, here in targets():
            src = tok.at[r, pl.ds(STRIPE * kk, STRIPE)]
            dst = xrow.at[z, kk]
            far = remote(src, dst, x_send.at[r, kk], x_recv.at[z], device)
            near = pltpu.make_async_copy(src, dst, x_recv.at[z])
            sfar = remote(seg, segb.at[z], g_send.at[r, kk], g_recv.at[z], device)
            snear = pltpu.make_async_copy(seg, segb.at[z], g_recv.at[z])

            @pl.when(here)
            def _():
                near.start()
                snear.start()

            @pl.when(jnp.logical_not(here))
            def _():
                far.start()
                sfar.start()

        for i in range(3):
            loads[i].wait()
            w = raw[i]
            lo = jnp.concatenate([w[:, 0:ZB], w[:, 2 * ZB : 3 * ZB]], axis=1)
            hi = jnp.concatenate([w[:, ZB : 2 * ZB], w[:, 3 * ZB : 4 * ZB]], axis=1)
            wown[:, HALF * i : HALF * (i + 1)] = jnp.where(c == 0, lo, hi)
        bkt[...] = bucket_tile()
        table_load.wait()

        def make_band(hl, _):
            head = head_of(me, hl)
            for t in range(3):
                which = bkt[:, 128 * t : 128 * (t + 1)]
                total = jnp.zeros((128, 128), F32)
                for b in range(32):
                    total = jnp.where(which == b, table[head, b], total)
                band[hl, :, 128 * t : 128 * (t + 1)] = total
            return 0

        lax.fori_loop(0, 6, make_band, 0)

        for load in weight_loads(wg, wu, wd):
            load.start()
        keep = pltpu.make_async_copy(wown, wown_o, l_sem.at[0])
        keep.start()

        gain_f = gain_a[...].astype(F32).reshape(1, D)
        forwards = []
        def project(step):
            zz = me.near(step)
            other = xrow.at[zz, 1 - c]
            remote(other, other, f_send.at[step], f_recv.at[zz], me.core).wait_recv()
            xf = xrow[zz].reshape(256, D).astype(F32)
            r1 = lax.rsqrt(jnp.mean(xf * xf, axis=-1, keepdims=True) + EPSILON)
            nb = (xf * r1 * gain_f).astype(BF)
            rows = pl.ds(pl.multiple_of(zz * 256, 256), 256)
            n1[rows, :] = nb
            for i, dest in enumerate((q, k, v)):
                dest[rows, :] = dot(nb, wown[:, HALF * i : HALF * (i + 1)]).astype(BF)

        for step in range(4):
            zz = me.near(step)
            own = xrow.at[zz, c]
            remote(own, own, x_send.at[0, 0], x_recv.at[zz], me.core).wait_recv()
            fwd = remote(own, own, f_send.at[step], f_recv.at[zz], me.core)
            fwd.start()
            forwards.append(fwd)
            if step == 3:
                for r, kk, device, here in targets():
                    src = cot.at[r, pl.ds(STRIPE * kk, STRIPE)]
                    dst = gv.at[z]
                    far = remote(src, dst, c_send.at[r, kk], c_recv.at[z], device)
                    near = pltpu.make_async_copy(src, dst, c_recv.at[z])

                    @pl.when(here)
                    def _():
                        near.start()

                    @pl.when(jnp.logical_not(here))
                    def _():
                        far.start()

            if step > 0:
                project(step - 1)
        project(3)
        for zz in range(4):
            blk_seg = segb.at[zz]
            remote(blk_seg, blk_seg, g_send.at[0, 0], g_recv.at[zz], me.core).wait_recv()
            segrow[:, 256 * zz : 256 * (zz + 1)] = segb[zz, pl.ds(z % 2, 1), :].astype(F32)
        segcol[...] = jnp.transpose(jnp.broadcast_to(segrow[...], (128, SLOTS)))
        linv[...] = jnp.zeros((8, SLOTS), F32)

        def pair_step(p, _):
            lanes = pl.ds(pl.multiple_of(p * 128, 128), 128)
            kp, vp = k[:, lanes], v[:, lanes]
            for hd in range(2):
                mask = lane_mask(hd)
                vm = vp * mask + (1 - mask)
                hl = 2 * p + hd
                head = head_of(me, hl)
                after, before = table[head, FAR_AFTER], table[head, FAR_BEFORE]

                @pl.when(p > 0)
                def _():
                    pltpu.make_async_copy(e_scr.at[hd], e_o.at[hl], e_sem.at[hd]).wait()

                for ib in range(4):
                    qm = q[256 * ib : 256 * (ib + 1), lanes] * mask
                    scr = s_scr.at[ib % 2]
                    scr[...] = dot_nt(kp, qm)
                    for t in range(2):
                        here = 2 * ib + t
                        cols = slice(128 * t, 128 * (t + 1))
                        seg_q = segrow[:, 256 * ib + 128 * t : 256 * ib + 128 * (t + 1)]
                        top = jnp.full((8, 128), MASKED, F32)
                        for jb in range(8):
                            rows = slice(128 * jb, 128 * (jb + 1))
                            tile = scr[rows, cols]
                            if abs(jb - here) <= 1:
                                off = 128 * (here - jb + 1)
                                tile = tile + band[hl, :, off : off + 128]
                            else:
                                tile = tile + (after if jb > here else before)
                            tile = jnp.where(segcol[rows, :] == seg_q, tile, MASKED)
                            scr[rows, cols] = tile
                            top = jnp.maximum(top, jnp.max(tile.reshape(16, 8, 128), axis=0))
                        top = jnp.max(top, axis=0, keepdims=True)
                        for jb in range(8):
                            rows = slice(128 * jb, 128 * (jb + 1))
                            weight = jnp.exp(scr[rows, cols] - top)
                            e_scr[hd, rows, 256 * ib + 128 * t : 256 * ib + 128 * (t + 1)] = weight.astype(BF)
                both = dot_tn(vm, e_scr[hd])
                data, sums = (both[0:HD], both[HD:128]) if hd == 0 else (both[HD:128], both[0:HD])
                inverse = 1.0 / sums
                ot_scr[HD * hd : HD * (hd + 1), :] = data * inverse
                linv[pl.ds(hl, 1), :] = inverse[0:1]
                pltpu.make_async_copy(e_scr.at[hd], e_o.at[hl], e_sem.at[hd]).start()
            mixed = jnp.transpose(ot_scr[...])
            o[:, lanes] = mixed
            ob[:, :, :, lanes] = mixed.astype(BF).reshape(4, 2, STRIPE, 128)
            mine = ob.at[:, 1 - c, :, lanes]
            remote(mine, obf.at[c, :, :, lanes], o_send.at[p], o_recv.at[p], me.core).start()
            return 0

        lax.fori_loop(0, 3, pair_step, 0)

        for hd in range(2):
            pltpu.make_async_copy(e_scr.at[hd], e_o.at[4 + hd], e_sem.at[hd]).wait()
        obf[c] = ob[:, c]
        keep.wait()
        for fwd in forwards:
            fwd.wait_send()

    def weight_loads(wg, wu, wd):
        loads = []
        for i in range(4):
            loads.append(
                pltpu.make_async_copy(
                    w_out.at[pl.ds(ZB * i, ZB)], wout.at[i % 2, pl.ds(ZB * (i // 2), ZB)], l_sem.at[4 + i]
                )
            )
        for f in range(2):
            for which, (src, dst) in enumerate(((w_gate, wg), (w_up, wu), (w_down, wd))):
                for zz in range(4):
                    far = pl.ds(512 * zz + 256 * f, 256)
                    own = pl.ds(256 * zz, 256)
                    sem = w_sem.at[f, which, zz]
                    if which < 2:
                        loads.append(pltpu.make_async_copy(src.at[:, far], dst.at[f, :, own], sem))
                    else:
                        loads.append(pltpu.make_async_copy(src.at[far], dst.at[f, own], sem))
        return loads

    def feed_forward(hid, wg, wu, wd, n2, h1, acc, dga, dup, dab_v):
        loads = weight_loads(wg, wu, wd)
        for load in loads[:4]:
            load.wait()
        gain = gain_f[...].astype(F32).reshape(1, D)
        for i in range(2):
            rows = slice(256 * i, 256 * (i + 1))
            parts = slice(2 * i, 2 * (i + 1))
            h1[rows, :] = xrow[parts, c].reshape(256, D).astype(F32) + dot(
                obf[c, parts].reshape(256, HALF), wout[c]
            )
        for p in range(3):
            lanes = slice(128 * p, 128 * (p + 1))
            mine = ob.at[:, 1 - c, :, lanes]
            there = remote(mine, obf.at[1 - c, :, :, lanes], o_send.at[p], o_recv.at[p], me.core)
            there.wait_send()
            there.wait_recv()
        for i in range(2):
            rows = slice(256 * i, 256 * (i + 1))
            parts = slice(2 * i, 2 * (i + 1))
            h = h1[rows, :] + dot(obf[1 - c, parts].reshape(256, HALF), wout[1 - c])
            h1[rows, :] = h
            r2 = lax.rsqrt(jnp.mean(h * h, axis=-1, keepdims=True) + EPSILON)
            n2[rows, :] = (h * r2 * gain).astype(BF)
        def gate_up(f):
            for which, grads in enumerate((dga, dup)):
                for zz in range(4):
                    piece = dot_tn(n2[...], grads[:, 256 * zz : 256 * (zz + 1)]).astype(BF)
                    unit[SLOT[2 * f + which], zz % 2, :, :, :, :, 256 * (zz // 2) : 256 * (zz // 2 + 1)] = piece.reshape(
                        2, 2, 2, 96, 256
                    )
                red.poll()

        for f in range(2):
            for load in loads[4 + 12 * f : 16 + 12 * f]:
                load.wait()
            for i in range(2):
                rows = slice(256 * i, 256 * (i + 1))
                gate = dot(n2[rows, :], wg[f])
                up = dot(n2[rows, :], wu[f])
                if f == 0 and i == 0:
                    for zz in range(4):
                        got = gv.at[zz]
                        remote(got, got, c_send.at[0, 0], c_recv.at[zz], me.core).wait_recv()
                dhid = dot_nt(gv[2 * i : 2 * (i + 1)].reshape(256, D), wd[f])
                square = gate * gate
                th = jnp.tanh(GELU_SCALE * gate * (1.0 + GELU_CUBE * square))
                half = 0.5 + 0.5 * th
                gelu = gate * half
                slope = half + 0.5 * GELU_SCALE * gate * (1.0 - th * th) * (1.0 + 3.0 * GELU_CUBE * square)
                hid[f, rows, :] = (gelu * up).astype(BF)
                dup[rows, :] = (dhid * gelu).astype(BF)
                dga[rows, :] = (dhid * up * slope).astype(BF)
                if f == 1:
                    red.poll()
            if f == 1:
                for i in range(4):
                    rows = slice(128 * i, 128 * (i + 1))
                    rows_out[i] = (h1[rows, :] + acc[rows, :] + dot(hid[f, rows, :], wd[f])).astype(BF)
                start_home(*out_way)
                red.poll()
            if f == 0:
                gate_up(0)
            if f == 0:
                acc[...] = dot(hid[f], wd[f])
                red.poll()
                dh1[...] = dot_nt(dga[...], wg[f])
            else:
                dh1[...] += dot_nt(dga[...], wg[f])
            red.poll()
            dh1[...] += dot_nt(dup[...], wu[f])
            red.poll()
        total = jnp.zeros((1, D), F32)
        for i in range(4):
            rows = slice(128 * i, 128 * (i + 1))
            h = h1[rows, :]
            r2 = lax.rsqrt(jnp.mean(h * h, axis=-1, keepdims=True) + EPSILON)
            u2 = h * r2
            dn2 = dh1[rows, :]
            total = total + jnp.sum(dn2 * u2, axis=0, keepdims=True)
            wn = dn2 * gain
            dh = gv[i].astype(F32) + r2 * (wn - u2 * jnp.mean(wn * u2, axis=-1, keepdims=True))
            dh1[rows, :] = dh
            dab_v[rows, :] = dh.astype(BF)
        stat[...] = jnp.zeros((6, 8, 256), F32)
        for i in range(3):
            stat[0, i : i + 1, :] = total[:, 256 * i : 256 * (i + 1)]
        red.poll()
        dab = dab_v[...]
        for cp in range(2):
            dobv[cp] = dot_nt(dab, wout[cp]).astype(BF).reshape(4, STRIPE, HALF)
        to_partner.start()
        dobrow[:, c] = dobv[c]
        red.poll()
        gate_up(1)
        for a in range(2):
            dz = jnp.concatenate([dab[:, ZB * a : ZB * (a + 1)], dab[:, ZB * (a + 2) : ZB * (a + 3)]], axis=1)
            for cp in range(2):
                piece = dot_tn(obf[cp].reshape(OWN, HALF), dz).astype(BF)
                for yy in range(2):
                    for cc in range(2):
                        row = 96 * (2 * yy + cc)
                        unit[SLOT[6], a, yy, cp, cc, :, 0:HALF] = piece[row : row + 96]
        red.poll()

    def down(hid):
        for f in range(2):
            for zz in range(4):
                piece = dot_tn(gv[...].reshape(OWN, D), hid[f, :, 256 * zz : 256 * (zz + 1)]).astype(BF)
                for to in range(4):
                    for part in range(2):
                        row = ZB * to + 96 * part
                        unit[SLOT[4 + part], to % 2, zz // 2, zz % 2, f, :, 256 * (to // 2) : 256 * (to // 2 + 1)] = piece[
                            row : row + 96
                        ]
            red.poll()

    def attention(hid, dqkv, e, ds, dp_scr, dob_scr, dv_scr, dk_scr, dqt_scr, band):
        fetch = [pltpu.make_async_copy(e_o.at[h], e.at[h % 2], e_sem.at[2 + h]) for h in range(6)]
        fetch[0].start()
        fetch[1].start()
        to_partner.wait()
        first_half = lax.broadcasted_iota(jnp.int32, (1, 128), 1) < HD
        for p in range(3):
            lanes = slice(128 * p, 128 * (p + 1))
            kp, vp, qp = k[:, lanes], v[:, lanes], q[:, lanes]
            inverse = jnp.concatenate(
                [jnp.broadcast_to(linv[2 * p + hd : 2 * p + hd + 1, :], (HD, SLOTS)) for hd in range(2)], axis=0
            )
            scaled = dobrow[:, :, :, lanes].reshape(SLOTS, 128).astype(F32) * jnp.transpose(inverse)
            dob_scr[...] = scaled.astype(BF)
            product = jnp.transpose(scaled * o[:, lanes])
            for hd in range(2):
                h = 2 * p + hd
                delta = jnp.sum(product[HD * hd : HD * (hd + 1)], axis=0, keepdims=True)
                vm = vp * lane_mask(hd)
                fetch[h].wait()
                ev = e.at[hd]
                band[...] = jnp.zeros((128, 384), F32)
                after = jnp.zeros((8, 128), F32)
                before = jnp.zeros((8, 128), F32)
                for ib in range(4):
                    scr = dp_scr.at[ib % 2]
                    scr[...] = dot_nt(vm, dob_scr[256 * ib : 256 * (ib + 1), :])
                    for t in range(2):
                        here = 2 * ib + t
                        cols = slice(128 * here, 128 * (here + 1))
                        for jb in range(8):
                            rows = slice(128 * jb, 128 * (jb + 1))
                            dsv = ev[rows, cols].astype(F32) * (scr[rows, 128 * t : 128 * (t + 1)] - delta[:, cols])
                            ds[rows, cols] = dsv.astype(BF)
                            if abs(jb - here) <= 1:
                                off = 128 * (here - jb + 1)
                                band[:, off : off + 128] += dsv
                            elif jb > here:
                                after = after + jnp.sum(dsv.reshape(16, 8, 128), axis=0)
                            else:
                                before = before + jnp.sum(dsv.reshape(16, 8, 128), axis=0)
                    red.poll()
                dv = dot(ev[...], dob_scr[...])
                dk = dot(ds[...], qp)
                dqt_scr[HD * hd : HD * (hd + 1), :] = dot_tn(kp, ds[...])[HD * hd : HD * (hd + 1)]
                if hd == 0:
                    dv_scr[...] = dv
                    dk_scr[...] = dk
                else:
                    for i, val in enumerate(
                        (
                            jnp.transpose(dqt_scr[...]),
                            jnp.where(first_half, dk_scr[...], dk),
                            jnp.where(first_half, dv_scr[...], dv),
                        )
                    ):
                        dqkv[:, :, :, HALF * i + 128 * p : HALF * i + 128 * (p + 1)] = val.astype(BF).reshape(
                            4, 2, STRIPE, 128
                        )
                if h + 2 < 6:
                    fetch[h + 2].start()
                for b in range(32):
                    part = jnp.zeros((1, 128), F32)
                    for t in range(3):
                        own = slice(128 * t, 128 * (t + 1))
                        part = part + jnp.sum(jnp.where(bkt[:, own] == b, band[:, own], 0.0), axis=0, keepdims=True)
                    if b == FAR_AFTER:
                        part = part + jnp.sum(after, axis=0, keepdims=True)
                    if b == FAR_BEFORE:
                        part = part + jnp.sum(before, axis=0, keepdims=True)
                    bcount[32 * h + b : 32 * h + b + 1, :] = part
                if h == DOWN_AFTER:
                    down(hid)

    def tail(dqkv, wown, dn1, pn_send):
        load = pltpu.make_async_copy(wown_o, wown, l_sem.at[0])
        load.start()
        sent_home(*out_way)
        load.wait()
        pn_send[...] = dot_nt(dqkv[:, 1 - c].reshape(OWN, 3 * HALF), wown[...]).astype(BF).reshape(4, STRIPE, D)
        partial = remote(pn_send, pn_recv, p_send, p_recv, me.core)
        partial.start()
        red.poll()
        dn1[...] = dot_nt(dqkv[:, c].reshape(OWN, 3 * HALF), wown[...])
        red.poll()
        partial.wait()
        gain = gain_a[...].astype(F32).reshape(1, D)
        total = jnp.zeros((1, D), F32)
        for i in range(4):
            rows = slice(128 * i, 128 * (i + 1))
            xf = xrow[i, c].astype(F32)
            r1 = lax.rsqrt(jnp.mean(xf * xf, axis=-1, keepdims=True) + EPSILON)
            u1 = xf * r1
            dn = dn1[rows, :] + pn_recv[i].astype(F32)
            total = total + jnp.sum(dn * u1, axis=0, keepdims=True)
            wn = dn * gain
            ig = dh1[rows, :] + r1 * (wn - u1 * jnp.mean(wn * u1, axis=-1, keepdims=True))
            rows_out[i] = ig.astype(BF)
        start_home(*ig_way)
        red.poll()
        for i in range(3):
            grads = dqkv[:, :, :, HALF * i : HALF * (i + 1)].reshape(SLOTS, HALF)
            unit[SLOT[7 + i], c, :, :, :, :, 0:HALF] = dot_tn(n1[...], grads).astype(BF).reshape(2, 2, 2, 96, HALF)
            red.poll()
        for i in range(3):
            stat[0, 3 + i : 4 + i, :] = total[:, 256 * i : 256 * (i + 1)]
        counts = jnp.sum(jnp.transpose(bcount[...]), axis=0, keepdims=True)
        stat[0, pl.ds(6 + c, 1), :] = jnp.concatenate([counts, jnp.zeros((1, 64), F32)], axis=1)
        copies = []
        for i, other in enumerate((me.core, me.xp, me.yp, me.z0p, me.z1p)):
            copy = remote(stat.at[i], stat_in.at[i], s_send.at[i], s_recv.at[i], other)
            copy.start()
            red.poll()
            copy.wait()
            stat[i + 1] = stat[i] + stat_in[i]
        stat_o[...] = stat[5]
        red.poll()
        sent_home(*ig_way)
        got_home(*out_way)
        got_home(*ig_way)
        for r, kk, device, here in targets():

            @pl.when(jnp.logical_not(here))
            def _():
                src = tok.at[r, pl.ds(STRIPE * kk, STRIPE)]
                remote(src, xrow.at[z, kk], x_send.at[r, kk], x_recv.at[z], device).wait_send()
                remote(seg, segb.at[z], g_send.at[r, kk], g_recv.at[z], device).wait_send()
                srcc = cot.at[r, pl.ds(STRIPE * kk, STRIPE)]
                remote(srcc, gv.at[z], c_send.at[r, kk], c_recv.at[z], device).wait_send()

    def first_half(hid, wg, wu, wd):
        pl.run_scoped(
            functools.partial(attend, wg, wu, wd),
            pltpu.VMEM((D, 3 * HALF), BF),
            pltpu.VMEM((6, 128, 384), F32),
            pltpu.VMEM((SLOTS, 128), F32),
            pltpu.VMEM((1, SLOTS), F32),
            pltpu.VMEM((2, SLOTS, 256), F32),
            pltpu.VMEM((2, SLOTS, SLOTS), BF),
            pltpu.VMEM((128, SLOTS), F32),
        )
        pl.run_scoped(
            functools.partial(feed_forward, hid, wg, wu, wd),
            pltpu.VMEM((OWN, D), BF),
            pltpu.VMEM((OWN, D), F32),
            pltpu.VMEM((OWN, D), F32),
            pltpu.VMEM((OWN, 1024), BF),
            pltpu.VMEM((OWN, 1024), BF),
            pltpu.VMEM((OWN, D), BF),
        )

    def second_half(hid, dqkv):
        pl.run_scoped(
            functools.partial(attention, hid, dqkv),
            pltpu.VMEM((2, SLOTS, SLOTS), BF),
            pltpu.VMEM((SLOTS, SLOTS), BF),
            pltpu.VMEM((2, SLOTS, 256), F32),
            pltpu.VMEM((SLOTS, 128), BF),
            pltpu.VMEM((SLOTS, 128), F32),
            pltpu.VMEM((SLOTS, 128), F32),
            pltpu.VMEM((128, SLOTS), F32),
            pltpu.VMEM((128, 384), F32),
        )
        pl.run_scoped(
            functools.partial(tail, dqkv),
            pltpu.VMEM((D, 3 * HALF), BF),
            pltpu.VMEM((OWN, D), F32),
            pltpu.VMEM((4, STRIPE, D), BF),
        )

    def whole(hid):
        pl.run_scoped(
            functools.partial(first_half, hid),
            pltpu.VMEM((2, D, 1024), BF),
            pltpu.VMEM((2, D, 1024), BF),
            pltpu.VMEM((2, 1024, D), BF),
        )
        pl.run_scoped(functools.partial(second_half, hid), pltpu.VMEM((4, 2, STRIPE, 3 * HALF), BF))

    pl.run_scoped(whole, pltpu.VMEM((2, OWN, 1024), BF))


def run_layer(low, *arrays):
    shapes = (
        ((2, 256, D), BF),
        ((2, 256, D), BF),
        ((96, ZB), F32),
        ((96, ZB), F32),
        ((96, ZB), F32),
        ((96, ZB), F32),
        ((96, 512), F32),
        ((96, 512), F32),
        ((ZB, 256), F32),
        ((8, 256), F32),
        ((6, SLOTS, SLOTS), BF),
        ((D, 3 * HALF), BF),
    )
    dma = pltpu.SemaphoreType.DMA
    wide = [(2, 2, 2, 96, 512), (2, 2, 96, 512), (2, 96, 512), (96, 512), (96, 256)]
    narrow = [(2, 2, 2, 96, HALF), (2, 2, 96, HALF), (2, 96, HALF), (96, HALF), (96, ZB)]
    specs = [ANY] * 13
    specs[2] = specs[7] = VM
    return pl.pallas_call(
        functools.partial(layer_kernel, low),
        out_shape=[jax.ShapeDtypeStruct(s, t) for s, t in shapes],
        in_specs=specs,
        out_specs=[ANY, ANY] + [VM] * 8 + [ANY, ANY],
        scratch_shapes=[
            pltpu.SMEM((H, 32), F32),
            pltpu.VMEM((5, 2, 2, 2, 2, 96, 512), BF),
            *[pltpu.VMEM((6, *s), BF) for s in wide],
            *[pltpu.VMEM((4, *s), BF) for s in narrow],
            pltpu.VMEM((4, 96, ZB), BF),
            pltpu.VMEM((4, 2, STRIPE, D), BF),
            pltpu.VMEM((4, 2, 256), jnp.int32),
            pltpu.VMEM((SLOTS, D), BF),
            pltpu.VMEM((SLOTS, HALF), BF),
            pltpu.VMEM((SLOTS, HALF), BF),
            pltpu.VMEM((SLOTS, HALF), BF),
            pltpu.VMEM((SLOTS, HALF), F32),
            pltpu.VMEM((4, 2, STRIPE, HALF), BF),
            pltpu.VMEM((8, SLOTS), F32),
            pltpu.VMEM((128, 384), jnp.int32),
            pltpu.VMEM((4, STRIPE, D), BF),
            pltpu.VMEM((2, 4, STRIPE, HALF), BF),
            pltpu.VMEM((2, HALF, D), BF),
            pltpu.VMEM((2, 4, STRIPE, HALF), BF),
            pltpu.VMEM((4, 2, STRIPE, HALF), BF),
            pltpu.VMEM((4, STRIPE, D), BF),
            pltpu.VMEM((OWN, D), F32),
            pltpu.VMEM((4, STRIPE, D), BF),
            pltpu.VMEM((192, 128), F32),
            pltpu.VMEM((6, 8, 256), F32),
            pltpu.VMEM((5, 8, 256), F32),
            dma((2, 2)), dma((4,)), dma((4,)), dma((4,)), dma((2, 2)), dma((4,)),
            dma((2, 2)), dma((4,)), dma((3,)), dma((3,)),
            dma((10, 5)), dma((10, 5)),
            dma((4,)), dma((2, 2)), dma((4,)), dma((2, 2)),
            dma, dma, dma, dma, dma((5,)), dma((5,)),
            dma((8,)), dma((2, 3, 4)), dma((8,)),
        ],
        compiler_params=pltpu.CompilerParams(
            collective_id=0, has_side_effects=True, vmem_limit_bytes=63 * 2**20
        ),
        cost_estimate=pl.CostEstimate(flops=36 * 10**9, bytes_accessed=60 * 10**6, transcendentals=8 * 10**6),
        name="layer",
    )(*arrays)


def finish_kernel(*refs):
    ins, outs, held, (igf, na, nf, table), sems = refs[:10], refs[10:22], refs[22:32], refs[32:36], refs[36]
    out_o, ig_o, na_o, gq_o, gk_o, gv_o, go_o, nf_o, gg_o, gu_o, gd_o, table_o = outs
    loads = [pltpu.make_async_copy(src, dst, sems.at[i]) for i, (src, dst) in enumerate(zip(ins, held))]
    saves = []

    def save(src, dst):
        saves.append(pltpu.make_async_copy(src, dst, sems.at[10 + len(saves)]))
        saves[-1].start()

    for load in loads:
        load.start()
    ig, stat = held[1], held[9]
    loads[9].wait()
    nf[...] = jnp.concatenate([stat[i : i + 1, :] for i in range(3)], axis=1).reshape(D)
    na[...] = jnp.concatenate([stat[i : i + 1, :] for i in range(3, 6)], axis=1).reshape(D)
    rows = []
    for head in range(H):
        core, local = (head // 3) % 2, head % 3 + 3 * (head // 6)
        rows.append(stat[6 + core : 7 + core, 32 * local : 32 * (local + 1)])
    table[...] = jnp.concatenate(rows, axis=0)
    save(nf, nf_o)
    save(na, na_o)
    save(table, table_o)
    for i, dst in ((2, gq_o), (3, gk_o), (4, gv_o), (5, go_o), (6, gg_o), (7, gu_o), (8, gd_o), (0, out_o)):
        loads[i].wait()
        save(held[i], dst)
    loads[1].wait()
    for r in range(2):
        igf[r] = ig[r].astype(F32)
        save(igf.at[r], ig_o.at[r])
    for copy in saves:
        copy.wait()


def run_finish(results):
    output, input_grad, gq, gk, gv, go, gg, gu, gd, stat = results
    outs = [
        (output.shape, BF), (input_grad.shape, F32), ((D,), F32), (gq.shape, F32), (gk.shape, F32), (gv.shape, F32),
        (go.shape, F32), ((D,), F32), (gg.shape, F32), (gu.shape, F32), (gd.shape, F32), ((H, 32), F32),
    ]
    return pl.pallas_call(
        finish_kernel,
        out_shape=[jax.ShapeDtypeStruct(s, t) for s, t in outs],
        in_specs=[ANY] * 10,
        out_specs=[ANY] * 12,
        scratch_shapes=[
            *[pltpu.VMEM(r.shape, r.dtype) for r in results],
            pltpu.VMEM(input_grad.shape, F32),
            pltpu.VMEM((D,), F32),
            pltpu.VMEM((D,), F32),
            pltpu.VMEM((H, 32), F32),
            pltpu.SemaphoreType.DMA((24,)),
        ],
        compiler_params=pltpu.CompilerParams(vmem_limit_bytes=60 * 2**20),
        name="finish",
    )(*results)


def on_device(low, *arrays):
    arrays = list(arrays)
    arrays[11] = arrays[11].T
    output, input_grad, *grads, stat, _, _ = run_layer(low, *arrays)
    if low > 1:
        groups = [[low * high + i for i in range(low)] for high in range(8)]
        *grads, down = grads
        grads = [
            lax.psum_scatter(g, "dp", scatter_dimension=0, axis_index_groups=groups, tiled=True) for g in grads
        ]
        grads.append(lax.psum_scatter(down, "dp", scatter_dimension=1, axis_index_groups=groups, tiled=True))
        stat = lax.psum(stat, "dp", axis_index_groups=groups)
    results = list(run_finish([output, input_grad, *grads, stat]))
    results[10] = results[10].T
    results[11] = results[11].T
    return tuple(results)


def solution(mesh):
    rows = P("dp", "blk", None)
    split = P("dp", "blk")
    return jax.shard_map(
        functools.partial(on_device, mesh.shape["dp"] // 8),
        mesh=mesh,
        in_specs=(rows, split, P(), P(), P(), P(), P(), P(), P(), P(), P(), P(), rows),
        out_specs=(rows, rows, P(), split, split, split, split, P(), split, split, split, P()),
        check_vma=False,
    )
```
